256 devices in a mesh: gx: 8 (over y_hi, x), gy: 32 (over z, y_lo, core).
Axes of the slice: x: 4, y: 4 (y_hi: 2, y_lo: 2; y = y_hi * 2 + y_lo), z: 8, core: 2. Of those that a mesh axis runs over, the one named last changes fastest.
Arguments:
- velocity: float32 [3, 16, 1024, 4096], P(None, None, 'gx', 'gy'), may hold values from -6 to 6
- leaf_class: int32 [16, 1024, 4096], P(None, 'gx', 'gy'), may hold values from 0 to 15
- drag_table: float32 [16], replicated, may hold values from 0.05 to 0.6
Outputs:
- tendency: float32 [3, 16, 1024, 4096], P(None, None, 'gx', 'gy')
The draws below stay inside these ranges and needn't reach their ends.
All inputs are finite; a program needn't handle non-finite values.
Results may differ from the reference program's by a relative error of at most 0.000057.
Values sent between devices are 32-bit elements; how exact they have to be, the bound alone decides.
A program may use at most 192 MiB of HBM per device.

```python
import math
import jax
import jax.numpy as jnp
from jax import lax

NZ = 16
CLASSES = 16
NX = 1024
NY = 4096


def set_ends(entries, rng, smallest, largest):
    shape = entries.shape
    place = [jax.random.randint(jax.random.fold_in(rng, axis), (), 0, shape[axis]) for axis in range(len(shape))]
    entries = entries.at[tuple(place)].set(smallest)
    longest = shape.index(max(shape))
    place[longest] = (place[longest] + 1) % shape[longest]
    return entries.at[tuple(place)].set(largest)


def steps_of(stream_key, extent, shards, smallest, top_value):
    loudness = 1.0
    for dim, shards_of in shards:
        heights = jax.random.uniform(jax.random.fold_in(jax.random.fold_in(stream_key, 6), dim), (shards_of,), jnp.float32, smallest / len(shards), top_value / len(shards))
        loudness = loudness * jnp.repeat(jnp.exp(heights), extent[dim] // shards_of).reshape((-1,) + (1,) * (len(extent) - 1 - dim))
    return loudness


def normal_values(rng, extent, deviation, reach, pieces=(), held_as=jnp.bfloat16):
    drawn = jax.random.normal(rng, extent, jnp.float32) * deviation
    if len(pieces) > 0:
        drawn = steps_of(rng, extent, pieces, -0.22, 0.18) * drawn
    return jnp.clip(drawn, min=-reach, max=reach).astype(held_as)


def setup_inputs(seed: int = 0) -> dict:
    arg_keys = jax.random.split(jax.random.key(seed), 4)
    velocity = normal_values(arg_keys[0], (3, NZ, NX, NY), 1.0, 6.0, ((2, 8), (3, 32)), jnp.float32)
    leaf_class = set_ends(jax.random.randint(arg_keys[1], (NZ, NX, NY), 0, CLASSES), jax.random.fold_in(arg_keys[1], 1), 0, CLASSES - 1).astype(jnp.int32)
    drag_table = jnp.clip(jnp.exp(jax.random.uniform(arg_keys[2], (CLASSES,), jnp.float32, math.log(0.05), math.log(0.6))), 0.05, 0.6)
    return dict(velocity=velocity, leaf_class=leaf_class, drag_table=drag_table)


SPACING = 2.0
VISCOSITY = 1.0

def compact_sides(values, axis_dim):
    plus_one = jnp.roll(values, -1, axis_dim)
    minus_one = jnp.roll(values, 1, axis_dim)
    plus_two = jnp.roll(values, -2, axis_dim)
    minus_two = jnp.roll(values, 2, axis_dim)
    first_side = 14.0 / 9.0 / (2.0 * SPACING) * (plus_one - minus_one) + 1.0 / 9.0 / (4.0 * SPACING) * (plus_two - minus_two)
    second_side = 12.0 / 11.0 / (SPACING * SPACING) * (plus_one - 2.0 * values + minus_one) + 3.0 / 11.0 / (4.0 * SPACING * SPACING) * (plus_two - 2.0 * values + minus_two)
    return (first_side, second_side)

def periodic_solve(sides, coupling, axis_dim):
    length = sides.shape[axis_dim]
    angles = 2.0 * math.pi / length * jnp.arange(length, dtype=sides.dtype)
    symbol = 1.0 + 2.0 * coupling * jnp.cos(angles)
    layout = [1] * sides.ndim
    layout[axis_dim] = length
    spectrum = jnp.fft.fft(sides, axis=axis_dim) / symbol.reshape(layout)
    return jnp.real(jnp.fft.ifft(spectrum, axis=axis_dim)).astype(sides.dtype)

def level_tendency(values, class_plane, drag_table):
    first_x, second_x = compact_sides(values, 1)
    gradient_x = periodic_solve(first_x, 1.0 / 3.0, 1)
    curvature_x = periodic_solve(second_x, 2.0 / 11.0, 1)
    first_y, second_y = compact_sides(values, 2)
    gradient_y = periodic_solve(first_y, 1.0 / 3.0, 2)
    curvature_y = periodic_solve(second_y, 2.0 / 11.0, 2)
    drag_coef = drag_table[class_plane]
    wind_speed = jnp.sqrt(lax.optimization_barrier(jnp.sum(values * values, axis=0)))
    advection = values[0][None] * gradient_x + values[1][None] * gradient_y
    return -advection + VISCOSITY * (curvature_x + curvature_y) - (drag_coef * wind_speed)[None] * values

def reference(velocity, leaf_class, drag_table):
    levels = jnp.moveaxis(velocity, 1, 0)

    def one_level(pair):
        return level_tendency(pair[0], pair[1], drag_table)
    result = lax.map(one_level, (levels, leaf_class))
    return jnp.moveaxis(result, 0, 1)
```

```python
import math

import jax
import jax.numpy as jnp
import ml_dtypes
import numpy as np
from jax import lax
from jax.experimental import pallas as pl
from jax.experimental.pallas import tpu as pltpu
from jax.sharding import PartitionSpec as P

SPACING = 2.0
CELLS = 128
GROUP = 4
EDGE = 24
BF16 = jnp.bfloat16


def kernel_of(coupling, stencil):
    root = (-1.0 + math.sqrt(1.0 - 4.0 * coupling * coupling)) / (2.0 * coupling)
    scale = 1.0 / math.sqrt(1.0 - 4.0 * coupling * coupling)

    def at(d):
        return sum(w * scale * root ** abs(d - m) for m, w in stencil.items())

    amplitude = at(2) / root**2
    return at, root, amplitude


def operators():
    h = SPACING
    a, b = 14.0 / 9.0 / (2.0 * h), 1.0 / 9.0 / (4.0 * h)
    first = {-1: a, 1: -a, -2: b, 2: -b}
    c, e = 12.0 / 11.0 / (h * h), 3.0 / 11.0 / (4.0 * h * h)
    second = {-1: c, 1: c, -2: e, 2: e, 0: -2.0 * c - 2.0 * e}
    return kernel_of(1.0 / 3.0, first), kernel_of(2.0 / 11.0, second)


def split(values):
    high = np.asarray(values, np.float64).astype(ml_dtypes.bfloat16)
    low = (np.asarray(values, np.float64) - high.astype(np.float64)).astype(ml_dtypes.bfloat16)
    return high, low


def constants():
    (k1, r1, a1), (k2, r2, a2) = operators()
    n = CELLS
    d1 = np.array([[k1(i - j) for j in range(n)] for i in range(n)])
    d2 = np.array([[k2(i - j) for j in range(n)] for i in range(n)])
    rows = np.concatenate([d1.reshape(n // 8, 8, n), d2.reshape(n // 8, 8, n)], axis=1).reshape(2 * n, n)
    high, low = split(rows)
    along_x = np.concatenate([high, high, low], axis=1)
    high, low = split(np.concatenate([d1.T, d2.T], axis=1))
    i = np.arange(n)
    e1, e2 = k1(1) - a1 * r1, k2(1) - a2 * r2
    zero = np.zeros(n)
    first, last = (i == 0) * 1.0, (i == n - 1) * 1.0
    before = np.stack([
        np.concatenate([r1**i, zero]),
        np.concatenate([zero, r2**i]),
        np.concatenate([e1 * first, e2 * first]),
        np.zeros(2 * n),
    ])
    after = np.stack([
        np.concatenate([-(r1 ** (n - 1 - i)), zero]),
        np.concatenate([zero, r2 ** (n - 1 - i)]),
        np.concatenate([-e1 * last, e2 * last]),
        np.zeros(2 * n),
    ])
    spread = np.repeat(np.concatenate([before, after]), GROUP, axis=0)
    spread_high, spread_low = split(spread)
    along_y = np.concatenate([high, high, low, spread_high, spread_high, spread_low], axis=0)
    forward = np.stack([a1 * r1 ** (n - i.astype(float)), a2 * r2 ** (n - i.astype(float)), last, zero])
    backward = np.stack([a1 * r1 ** (1.0 + i), a2 * r2 ** (1.0 + i), first, zero])
    high, low = split(np.concatenate([forward, backward]))
    sums_y = np.concatenate(
        [np.concatenate([high, high], axis=1), np.concatenate([low, np.zeros_like(low)], axis=1)], axis=0
    )
    lanes = np.ones((1, n))
    edge_x = np.stack([
        forward[0, n - EDGE :, None] * lanes,
        forward[1, n - EDGE :, None] * lanes,
        backward[0, :EDGE, None] * lanes,
        backward[1, :EDGE, None] * lanes,
        (r1 ** i[:EDGE])[:, None] * lanes,
        (r2 ** i[:EDGE])[:, None] * lanes,
        (e1 * first)[:EDGE, None] * lanes,
        (e2 * first)[:EDGE, None] * lanes,
        (-(r1 ** (n - 1 - i)))[n - EDGE :, None] * lanes,
        (r2 ** (n - 1 - i))[n - EDGE :, None] * lanes,
        (-e1 * last)[n - EDGE :, None] * lanes,
        (e2 * last)[n - EDGE :, None] * lanes,
    ]).astype(np.float32)
    return along_x, along_y, sums_y, edge_x


def dot(a, b):
    return lax.dot_general(a, b, (((1,), (0,)), ((), ())), preferred_element_type=jnp.float32)


def dot_transposed(a, b):
    return lax.dot_general(a, b, (((1,), (1,)), ((), ())), preferred_element_type=jnp.float32)


def kernel(
    groups, vel_hbm, leaf_hbm, table_ref, along_x_ref, along_y_ref, sums_y_ref, edge_x_ref, out_hbm,
    vel, parts, leaf, tend, send_x, send_y, recv_x, recv_y,
    vel_sem, leaf_sem, out_sem, send_sem, recv_sem,
):
    n = CELLS

    def levels(g):
        return pl.ds(g * GROUP, GROUP)

    def vel_copy(g):
        return pltpu.make_async_copy(vel_hbm.at[:, levels(g)], vel.at[:, levels(g)], vel_sem.at[g])

    def leaf_copy(g):
        return pltpu.make_async_copy(leaf_hbm.at[levels(g)], leaf.at[levels(g)], leaf_sem.at[g])

    def out_copy(g):
        return pltpu.make_async_copy(tend.at[:, levels(g)], out_hbm.at[:, levels(g)], out_sem.at[g])

    for g in range(groups):
        vel_copy(g).start()
    for g in range(groups):
        leaf_copy(g).start()

    mx, my = lax.axis_index("gx"), lax.axis_index("gy")
    nx, ny = lax.axis_size("gx"), lax.axis_size("gy")
    targets = [
        {"gx": lax.rem(mx + 1, nx)},
        {"gx": lax.rem(mx + nx - 1, nx)},
        {"gy": lax.rem(my + 1, ny)},
        {"gy": lax.rem(my + ny - 1, ny)},
    ]
    barrier = pltpu.get_barrier_semaphore()
    for target in targets:
        pl.semaphore_signal(barrier, inc=1, device_id=target, device_id_type=pl.DeviceIdType.MESH)

    blank = jnp.zeros((GROUP, n), jnp.float32)

    @pl.loop(0, groups)
    def _(g):
        vel_copy(g).wait()
        for c in range(3):
            for k in range(GROUP):
                values = vel[c, g * GROUP + k]
                high = values.astype(BF16)
                low = (values - high.astype(jnp.float32)).astype(BF16)
                parts[c, g * GROUP + k, :, :n] = high
                parts[c, g * GROUP + k, :, n:] = low
                top, bottom = values[:EDGE], values[n - EDGE :]
                for q in range(2):
                    row = q * GROUP + k
                    send_x[0, c, g, row : row + 1] = jnp.sum(edge_x_ref[q] * bottom, axis=0, keepdims=True)
                    send_x[1, c, g, row : row + 1] = jnp.sum(edge_x_ref[2 + q] * top, axis=0, keepdims=True)
                row = 2 * GROUP + k
                send_x[0, c, g, row : row + 1] = values[n - 1 :]
                send_x[1, c, g, row : row + 1] = values[:1]
            for k in range(0, GROUP, 2):
                pair = parts[c, pl.ds(g * GROUP + k, 2)].reshape(2 * n, 2 * n)
                sums = dot_transposed(sums_y_ref[...], pair)
                sums = sums[:8] + sums[8:]
                for j in range(2):
                    for q in range(3):
                        row = q * GROUP + k + j
                        send_y[0, c, g, row : row + 1] = sums[q : q + 1, j * n : (j + 1) * n]
                        send_y[1, c, g, row : row + 1] = sums[4 + q : 5 + q, j * n : (j + 1) * n]
            for side in range(2):
                send_x[side, c, g, 3 * GROUP :] = blank
                send_y[side, c, g, 3 * GROUP :] = blank

    pl.semaphore_wait(barrier, 4)
    copies = []
    for t, target in enumerate(targets):
        source, landing = ((send_x, recv_x), (send_y, recv_y))[t // 2]
        copies.append(
            pltpu.make_async_remote_copy(
                src_ref=source.at[t % 2],
                dst_ref=landing.at[t % 2],
                send_sem=send_sem.at[t],
                recv_sem=recv_sem.at[t],
                device_id=target,
                device_id_type=pl.DeviceIdType.MESH,
            )
        )
        copies[-1].start()

    lane = lax.broadcasted_iota(jnp.int32, (n, n), 1)
    table = jnp.zeros((n, n), jnp.float32)
    for k in range(table_ref.shape[0]):
        table = jnp.where(lane == k, table_ref[k], table)

    @pl.loop(0, groups)
    def _(g):
        leaf_copy(g).wait()
        for k in range(0, GROUP, 2):
            z = (g * GROUP + k, g * GROUP + k + 1)
            drag = []
            for j in range(2):
                speed = jnp.sqrt(vel[0, z[j]] ** 2 + vel[1, z[j]] ** 2 + vel[2, z[j]] ** 2)
                drag.append(jnp.take_along_axis(table, leaf[z[j]], axis=1) * speed)
            for c in range(3):
                high = jnp.concatenate([parts[c, z[0], :, :n], parts[c, z[1], :, :n]], axis=1)
                low = jnp.concatenate([parts[c, z[0], :, n:], parts[c, z[1], :, n:]], axis=1)
                both = dot(along_x_ref[...], jnp.concatenate([high, low, high], axis=0))
                both = both.reshape(n // 8, 2, 8, 2 * n)
                for j in range(2):
                    gradient = both[:, 0, :, j * n : (j + 1) * n].reshape(n, n)
                    curvature = both[:, 1, :, j * n : (j + 1) * n].reshape(n, n)
                    tend[c, z[j]] = curvature - vel[0, z[j]] * gradient - drag[j] * vel[c, z[j]]

    for copy in copies:
        copy.wait()

    lane = lax.broadcasted_iota(jnp.int32, (n, 6 * GROUP * 4), 1)

    @pl.loop(0, groups)
    def _(g):
        spread = []
        for c in range(3):
            got = jnp.concatenate([recv_y[0, c, g], recv_y[1, c, g]], axis=0)
            high = got.astype(BF16).astype(jnp.float32)
            low = (got - high).astype(BF16).astype(jnp.float32)
            spread.append(jnp.concatenate([high, low, high], axis=0).T.astype(BF16))
        for k in range(GROUP):
            z = g * GROUP + k
            mask = (lane[:, : 24 * GROUP] % GROUP) == k
            left = []
            for c in range(3):
                mine = jnp.where(mask, spread[c], jnp.zeros_like(spread[c]))
                left.append(jnp.concatenate([parts[c, z], parts[c, z, :, :n], mine], axis=1))
            both = dot(jnp.concatenate(left, axis=0), along_y_ref[...])
            for c in range(3):
                gradient = both[c * n : (c + 1) * n, :n]
                curvature = both[c * n : (c + 1) * n, n:]
                tend[c, z] += curvature - vel[1, z] * gradient
                for side in range(2):
                    rows = pl.ds(0, EDGE) if side == 0 else pl.ds(n - EDGE, EDGE)
                    s1 = recv_x[side, c, g, k : k + 1]
                    s2 = recv_x[side, c, g, GROUP + k : GROUP + k + 1]
                    s3 = recv_x[side, c, g, 2 * GROUP + k : 2 * GROUP + k + 1]
                    at = 4 + 4 * side
                    gradient = edge_x_ref[at] * s1 + edge_x_ref[at + 2] * s3
                    curvature = edge_x_ref[at + 1] * s2 + edge_x_ref[at + 3] * s3
                    tend[c, z, rows] += curvature - vel[0, z, rows] * gradient
        out_copy(g).start()

    for g in range(groups):
        out_copy(g).wait()


def body(velocity, leaf_class, drag_table):
    along_x, along_y, sums_y, edge_x = constants()
    levels, n = velocity.shape[1], CELLS
    groups = levels // GROUP
    import functools

    any_space = pl.BlockSpec(memory_space=pl.ANY)
    vmem = pl.BlockSpec(memory_space=pltpu.VMEM)
    exchanged = pltpu.VMEM((2, 3, groups, 4 * GROUP, n), jnp.float32)
    return pl.pallas_call(
        functools.partial(kernel, groups),
        out_shape=jax.ShapeDtypeStruct(velocity.shape, jnp.float32),
        in_specs=[any_space, any_space, pl.BlockSpec(memory_space=pltpu.SMEM), vmem, vmem, vmem, vmem],
        out_specs=any_space,
        scratch_shapes=[
            pltpu.VMEM(velocity.shape, jnp.float32),
            pltpu.VMEM((3, levels, n, 2 * n), BF16),
            pltpu.VMEM(leaf_class.shape, jnp.int32),
            pltpu.VMEM(velocity.shape, jnp.float32),
            exchanged, exchanged, exchanged, exchanged,
            pltpu.SemaphoreType.DMA((groups,)),
            pltpu.SemaphoreType.DMA((groups,)),
            pltpu.SemaphoreType.DMA((groups,)),
            pltpu.SemaphoreType.DMA((4,)),
            pltpu.SemaphoreType.DMA((4,)),
        ],
        compiler_params=pltpu.CompilerParams(
            collective_id=0, has_side_effects=True, vmem_limit_bytes=48 * 1024 * 1024
        ),
        cost_estimate=pl.CostEstimate(flops=5_000_000_000, bytes_accessed=8_000_000, transcendentals=300_000),
    )(velocity, leaf_class, drag_table, jnp.asarray(along_x), jnp.asarray(along_y), jnp.asarray(sums_y), jnp.asarray(edge_x))


def solution(mesh):
    return jax.shard_map(
        body,
        mesh=mesh,
        in_specs=(P(None, None, "gx", "gy"), P(None, "gx", "gy"), P()),
        out_specs=P(None, None, "gx", "gy"),
        check_vma=False,
    )
```

```python
import functools
import math

import jax
import jax.numpy as jnp
import ml_dtypes
import numpy as np
from jax import lax
from jax.experimental import pallas as pl
from jax.experimental.pallas import tpu as pltpu
from jax.sharding import PartitionSpec as P

SPACING = 2.0
CELLS = 128
GROUP = 4
EDGE = 24
BF16 = jnp.bfloat16


def kernel_of(coupling, stencil):
    root = (-1.0 + math.sqrt(1.0 - 4.0 * coupling * coupling)) / (2.0 * coupling)
    scale = 1.0 / math.sqrt(1.0 - 4.0 * coupling * coupling)

    def at(d):
        return sum(w * scale * root ** abs(d - m) for m, w in stencil.items())

    amplitude = at(2) / root**2
    return at, root, amplitude


def operators():
    h = SPACING
    a, b = 14.0 / 9.0 / (2.0 * h), 1.0 / 9.0 / (4.0 * h)
    first = {-1: a, 1: -a, -2: b, 2: -b}
    c, e = 12.0 / 11.0 / (h * h), 3.0 / 11.0 / (4.0 * h * h)
    second = {-1: c, 1: c, -2: e, 2: e, 0: -2.0 * c - 2.0 * e}
    return kernel_of(1.0 / 3.0, first), kernel_of(2.0 / 11.0, second)


def split(values):
    high = np.asarray(values, np.float64).astype(ml_dtypes.bfloat16)
    low = (np.asarray(values, np.float64) - high.astype(np.float64)).astype(ml_dtypes.bfloat16)
    return high, low


def constants():
    (k1, r1, a1), (k2, r2, a2) = operators()
    n = CELLS
    d1 = np.array([[k1(i - j) for j in range(n)] for i in range(n)])
    d2 = np.array([[k2(i - j) for j in range(n)] for i in range(n)])
    rows = np.concatenate([d1.reshape(n // 8, 8, n), d2.reshape(n // 8, 8, n)], axis=1).reshape(2 * n, n)
    high, low = split(rows)
    along_x = np.concatenate([high, high, low], axis=1)
    high, low = split(np.concatenate([d1.T, d2.T], axis=1))
    i = np.arange(n)
    e1, e2 = k1(1) - a1 * r1, k2(1) - a2 * r2
    zero = np.zeros(n)
    first, last = (i == 0) * 1.0, (i == n - 1) * 1.0
    before = np.stack([
        np.concatenate([r1**i, zero]),
        np.concatenate([zero, r2**i]),
        np.concatenate([e1 * first, e2 * first]),
    ])
    after = np.stack([
        np.concatenate([-(r1 ** (n - 1 - i)), zero]),
        np.concatenate([zero, r2 ** (n - 1 - i)]),
        np.concatenate([-e1 * last, e2 * last]),
    ])
    spread = np.repeat(np.concatenate([before, after]), GROUP, axis=0)
    spread_high, spread_low = split(spread)
    blank = np.zeros((8, 2 * n), spread_high.dtype)
    along_y = np.concatenate([high, high, low, spread_high, spread_high, spread_low, blank], axis=0)
    forward = np.stack([a1 * r1 ** (n - i.astype(float)), a2 * r2 ** (n - i.astype(float)), last, zero])
    backward = np.stack([a1 * r1 ** (1.0 + i), a2 * r2 ** (1.0 + i), first, zero])
    high, low = split(np.concatenate([forward, backward]))
    sums_y = np.concatenate(
        [np.concatenate([high, high], axis=1), np.concatenate([low, np.zeros_like(low)], axis=1)], axis=0
    )
    lanes = np.ones((1, n))
    edge_x = np.stack([
        forward[0, n - EDGE :, None] * lanes,
        forward[1, n - EDGE :, None] * lanes,
        backward[0, :EDGE, None] * lanes,
        backward[1, :EDGE, None] * lanes,
        (r1 ** i[:EDGE])[:, None] * lanes,
        (r2 ** i[:EDGE])[:, None] * lanes,
        (e1 * first)[:EDGE, None] * lanes,
        (e2 * first)[:EDGE, None] * lanes,
        (-(r1 ** (n - 1 - i)))[n - EDGE :, None] * lanes,
        (r2 ** (n - 1 - i))[n - EDGE :, None] * lanes,
        (-e1 * last)[n - EDGE :, None] * lanes,
        (e2 * last)[n - EDGE :, None] * lanes,
    ]).astype(np.float32)
    return along_x, along_y, sums_y, edge_x


def dot(a, b):
    return lax.dot_general(a, b, (((1,), (0,)), ((), ())), preferred_element_type=jnp.float32)


def dot_transposed(a, b):
    return lax.dot_general(a, b, (((1,), (1,)), ((), ())), preferred_element_type=jnp.float32)


def solve_y(g, vel, parts, tend, recv_y, along_y, store):
    n = CELLS
    values = 3 * GROUP
    lane = lax.broadcasted_iota(jnp.int32, (n, 80), 1)
    spread = []
    for c in range(3):
        got = jnp.concatenate([recv_y[side, g, c * values : (c + 1) * values] for side in range(2)], axis=0)
        high = got.astype(BF16).astype(jnp.float32)
        low = (got - high).astype(BF16).astype(jnp.float32)
        blank = jnp.zeros((8, n), jnp.float32)
        spread.append(jnp.concatenate([high, low, high, blank], axis=0).T.astype(BF16))
    for k in range(GROUP):
        z = g * GROUP + k
        mask = (lane % GROUP) == k
        left = []
        for c in range(3):
            mine = jnp.where(mask, spread[c], jnp.zeros_like(spread[c]))
            left.append(jnp.concatenate([parts[c, z], parts[c, z, :, :n], mine], axis=1))
        both = dot(jnp.concatenate(left, axis=0), along_y[...])
        for c in range(3):
            gradient = both[c * n : (c + 1) * n, :n]
            curvature = both[c * n : (c + 1) * n, n:]
            store(c, k, tend[c, z] + curvature - vel[1, z] * gradient)


def first_kernel(
    groups, solved, vel_hbm, leaf_hbm, table_hbm, along_x_hbm, along_y_hbm, sums_y_hbm, edge_x_hbm,
    vel, parts, tend, recv_x, recv_y,
    leaf, send_x, send_y, along_x, along_y, sums_y, edge_x, table_ref,
    vel_sem, leaf_sem, const_sem, send_sem, recv_sem, send_y_sem, recv_y_sem,
):
    n = CELLS
    half = 2 * GROUP
    halves = groups // 2

    consts = [
        pltpu.make_async_copy(a, b, const_sem.at[i])
        for i, (a, b) in enumerate(
            [(edge_x_hbm, edge_x), (sums_y_hbm, sums_y), (along_x_hbm, along_x), (along_y_hbm, along_y),
             (table_hbm, table_ref)]
        )
    ]

    def levels(g):
        return pl.ds(g * GROUP, GROUP)

    def edge_copy(h, side):
        at = (slice(None), pl.ds(h * half, half), pl.ds(side * (n - EDGE), EDGE))
        return pltpu.make_async_copy(vel_hbm.at[at], vel.at[at], vel_sem.at[side, h])

    def middle_copy(g):
        at = (slice(None), levels(g), pl.ds(EDGE, n - 2 * EDGE))
        return pltpu.make_async_copy(vel_hbm.at[at], vel.at[at], vel_sem.at[2, g])

    def leaf_copy(g):
        return pltpu.make_async_copy(leaf_hbm.at[levels(g)], leaf.at[levels(g)], leaf_sem.at[g])

    consts[0].start()
    for h in range(halves):
        for side in range(2):
            edge_copy(h, side).start()
    consts[1].start()
    for g in range(groups):
        middle_copy(g).start()
    consts[4].start()
    consts[2].start()
    for g in range(groups):
        leaf_copy(g).start()
    consts[3].start()

    mx, my = lax.axis_index("gx"), lax.axis_index("gy")
    nx, ny = lax.axis_size("gx"), lax.axis_size("gy")
    targets = [
        {"gx": lax.rem(mx + 1, nx)},
        {"gx": lax.rem(mx + nx - 1, nx)},
        {"gy": lax.rem(my + 1, ny)},
        {"gy": lax.rem(my + ny - 1, ny)},
    ]
    barrier = pltpu.get_barrier_semaphore()
    for target in targets:
        pl.semaphore_signal(barrier, inc=1, device_id=target, device_id_type=pl.DeviceIdType.MESH)

    def send_x_copy(side):
        return pltpu.make_async_remote_copy(
            src_ref=send_x.at[side], dst_ref=recv_x.at[side],
            send_sem=send_sem.at[side], recv_sem=recv_sem.at[side],
            device_id=targets[side], device_id_type=pl.DeviceIdType.MESH,
        )

    def send_y_copy(side, g):
        return pltpu.make_async_remote_copy(
            src_ref=send_y.at[side, g], dst_ref=recv_y.at[side, g],
            send_sem=send_y_sem.at[side, g], recv_sem=recv_y_sem.at[side, g],
            device_id=targets[2 + side], device_id_type=pl.DeviceIdType.MESH,
        )

    consts[0].wait()

    @pl.loop(0, halves)
    def _(h):
        edge_copy(h, 0).wait()
        edge_copy(h, 1).wait()
        for c in range(3):
            for k in range(half):
                top, bottom = vel[c, h * half + k, :EDGE], vel[c, h * half + k, n - EDGE :]
                for q in range(2):
                    row = (c * 3 + q) * half + k
                    send_x[0, h, row : row + 1] = jnp.sum(edge_x[q] * bottom, axis=0, keepdims=True)
                    send_x[1, h, row : row + 1] = jnp.sum(edge_x[2 + q] * top, axis=0, keepdims=True)
                row = (c * 3 + 2) * half + k
                send_x[0, h, row : row + 1] = bottom[EDGE - 1 :]
                send_x[1, h, row : row + 1] = top[:1]

    pl.semaphore_wait(barrier, 4)
    for side in range(2):
        send_x_copy(side).start()

    consts[1].wait()

    @pl.loop(0, groups)
    def _(g):
        middle_copy(g).wait()
        for c in range(3):
            for k in range(GROUP):
                values = vel[c, g * GROUP + k]
                high = values.astype(BF16)
                parts[c, g * GROUP + k, :, :n] = high
                parts[c, g * GROUP + k, :, n:] = (values - high.astype(jnp.float32)).astype(BF16)
            for k in range(0, GROUP, 2):
                pair = parts[c, pl.ds(g * GROUP + k, 2)].reshape(2 * n, 2 * n)
                sums = dot_transposed(sums_y[...], pair)
                sums = sums[:8] + sums[8:]
                for j in range(2):
                    for q in range(3):
                        row = (c * 3 + q) * GROUP + k + j
                        send_y[0, g, row : row + 1] = sums[q : q + 1, j * n : (j + 1) * n]
                        send_y[1, g, row : row + 1] = sums[4 + q : 5 + q, j * n : (j + 1) * n]
        for side in range(2):
            send_y[side, g, 9 * GROUP :] = jnp.zeros((4, n), jnp.float32)
            send_y_copy(side, g).start()

    lane = lax.broadcasted_iota(jnp.int32, (n, n), 1)
    consts[4].wait()
    table = jnp.zeros((n, n), jnp.float32)
    for k in range(table_ref.shape[0]):
        table = jnp.where(lane == k, table_ref[k], table)
    consts[2].wait()

    @pl.loop(0, groups)
    def _(g):
        leaf_copy(g).wait()
        for k in range(0, GROUP, 2):
            z = (g * GROUP + k, g * GROUP + k + 1)
            drag = []
            for j in range(2):
                speed = jnp.sqrt(vel[0, z[j]] ** 2 + vel[1, z[j]] ** 2 + vel[2, z[j]] ** 2)
                drag.append(jnp.take_along_axis(table, leaf[z[j]], axis=1) * speed)
            for c in range(3):
                high = jnp.concatenate([parts[c, z[0], :, :n], parts[c, z[1], :, :n]], axis=1)
                low = jnp.concatenate([parts[c, z[0], :, n:], parts[c, z[1], :, n:]], axis=1)
                both = dot(along_x[...], jnp.concatenate([high, low, high], axis=0))
                both = both.reshape(n // 8, 2, 8, 2 * n)
                for j in range(2):
                    gradient = both[:, 0, :, j * n : (j + 1) * n].reshape(n, n)
                    curvature = both[:, 1, :, j * n : (j + 1) * n].reshape(n, n)
                    tend[c, z[j]] = curvature - vel[0, z[j]] * gradient - drag[j] * vel[c, z[j]]

    consts[3].wait()

    @pl.loop(0, groups)
    def _(g):
        for side in range(2):
            send_y_copy(side, g).wait()

        @pl.when(g < solved)
        def _():
            def store(c, k, values):
                tend[c, g * GROUP + k] = values

            solve_y(g, vel, parts, tend, recv_y, along_y, store)

    for side in range(2):
        send_x_copy(side).wait()


def second_kernel(
    groups, solved, vel, parts, tend, recv_x, recv_y, along_y_hbm, edge_x_hbm, out_hbm,
    edges, rest, along_y, edge_x, const_sem, middle_sem, edge_sem, rest_sem,
):
    n = CELLS
    half = 2 * GROUP
    consts = [
        pltpu.make_async_copy(a, b, const_sem.at[i])
        for i, (a, b) in enumerate([(edge_x_hbm, edge_x), (along_y_hbm, along_y)])
    ]
    for copy in consts:
        copy.start()

    def middle_copy(g):
        at = (slice(None), pl.ds(g * GROUP, GROUP), pl.ds(EDGE, n - 2 * EDGE))
        return pltpu.make_async_copy(tend.at[at], out_hbm.at[at], middle_sem.at[g])

    def edge_copy(g, side):
        at = (slice(None), pl.ds(g * GROUP, GROUP), pl.ds(side * (n - EDGE), EDGE))
        source = edges.at[side, :, pl.ds(g * GROUP, GROUP)]
        return pltpu.make_async_copy(source, out_hbm.at[at], edge_sem.at[side, g])

    def rest_copy(z):
        return pltpu.make_async_copy(rest.at[:, z - solved * GROUP], out_hbm.at[:, z], rest_sem.at[z - solved * GROUP])

    def added(c, g, k, side):
        h, lev = g // 2, (g % 2) * GROUP + k
        s1, s2, s3 = (recv_x[side, h, (c * 3 + q) * half + lev : (c * 3 + q) * half + lev + 1] for q in range(3))
        gradient = edge_x[4 + 4 * side] * s1 + edge_x[6 + 4 * side] * s3
        curvature = edge_x[5 + 4 * side] * s2 + edge_x[7 + 4 * side] * s3
        return curvature - vel[0, g * GROUP + k, side * (n - EDGE) : side * (n - EDGE) + EDGE] * gradient

    for g in range(solved):
        middle_copy(g).start()
    consts[0].wait()
    for g in range(solved):
        for side in range(2):
            rows = slice(side * (n - EDGE), side * (n - EDGE) + EDGE)
            for c in range(3):
                for k in range(GROUP):
                    edges[side, c, g * GROUP + k] = tend[c, g * GROUP + k, rows] + added(c, g, k, side)
            edge_copy(g, side).start()
    consts[1].wait()
    for g in range(solved, groups):
        base = (g - solved) * GROUP

        def store(c, k, values):
            rest[c, base + k] = values
            for side in range(2):
                rows = slice(side * (n - EDGE), side * (n - EDGE) + EDGE)
                rest[c, base + k, rows] += added(c, g, k, side)
            if c == 2:
                rest_copy(g * GROUP + k).start()

        solve_y(g, vel, parts, tend, recv_y, along_y, store)
    for g in range(solved):
        middle_copy(g).wait()
        for side in range(2):
            edge_copy(g, side).wait()
    for z in range(solved * GROUP, groups * GROUP):
        rest_copy(z).wait()


def in_hbm(array):
    return pltpu.with_memory_space_constraint(array, pltpu.HBM)


def body(velocity, leaf_class, drag_table):
    along_x, along_y, sums_y, edge_x = (in_hbm(jnp.asarray(a)) for a in constants())
    velocity, leaf_class, drag_table = in_hbm(velocity), in_hbm(leaf_class), in_hbm(drag_table)
    levels, n = velocity.shape[1], CELLS
    groups = levels // GROUP
    solved = groups - 1
    hbm = pl.BlockSpec(memory_space=pltpu.HBM)
    vmem = pl.BlockSpec(memory_space=pltpu.VMEM)
    dma = pltpu.SemaphoreType.DMA
    sums_along_x = (2, groups // 2, 18 * GROUP, n)
    sums_along_y = (2, groups, 10 * GROUP, n)
    held = [
        jax.ShapeDtypeStruct(velocity.shape, jnp.float32),
        jax.ShapeDtypeStruct((3, levels, n, 2 * n), BF16),
        jax.ShapeDtypeStruct(velocity.shape, jnp.float32),
        jax.ShapeDtypeStruct(sums_along_x, jnp.float32),
        jax.ShapeDtypeStruct(sums_along_y, jnp.float32),
    ]
    held = pl.pallas_call(
        functools.partial(first_kernel, groups, solved),
        out_shape=held,
        in_specs=[hbm, hbm, hbm, hbm, hbm, hbm, hbm],
        out_specs=[vmem] * 5,
        scratch_shapes=[
            pltpu.VMEM(leaf_class.shape, jnp.int32),
            pltpu.VMEM(sums_along_x, jnp.float32),
            pltpu.VMEM(sums_along_y, jnp.float32),
            pltpu.VMEM(along_x.shape, BF16),
            pltpu.VMEM(along_y.shape, BF16),
            pltpu.VMEM(sums_y.shape, BF16),
            pltpu.VMEM(edge_x.shape, jnp.float32),
            pltpu.SMEM(drag_table.shape, jnp.float32),
            dma((3, groups)), dma((groups,)), dma((5,)), dma((2,)), dma((2,)), dma((2, groups)), dma((2, groups)),
        ],
        compiler_params=pltpu.CompilerParams(
            collective_id=0, has_side_effects=True, vmem_limit_bytes=40 * 1024 * 1024
        ),
        cost_estimate=pl.CostEstimate(flops=4_000_000_000, bytes_accessed=5_000_000, transcendentals=300_000),
        name="exchange_and_solve",
    )(velocity, leaf_class, drag_table, along_x, along_y, sums_y, edge_x)
    return pl.pallas_call(
        functools.partial(second_kernel, groups, solved),
        out_shape=jax.ShapeDtypeStruct(velocity.shape, jnp.float32),
        in_specs=[vmem] * 5 + [hbm, hbm],
        out_specs=hbm,
        scratch_shapes=[
            pltpu.VMEM((2, 3, levels, EDGE, n), jnp.float32),
            pltpu.VMEM((3, (groups - solved) * GROUP, n, n), jnp.float32),
            pltpu.VMEM(along_y.shape, BF16),
            pltpu.VMEM(edge_x.shape, jnp.float32),
            dma((2,)), dma((groups,)), dma((2, groups)), dma(((groups - solved) * GROUP,)),
        ],
        compiler_params=pltpu.CompilerParams(vmem_limit_bytes=40 * 1024 * 1024),
        cost_estimate=pl.CostEstimate(flops=1_000_000_000, bytes_accessed=3_000_000, transcendentals=0),
        name="finish",
    )(*held, along_y, edge_x)


def solution(mesh):
    return jax.shard_map(
        body,
        mesh=mesh,
        in_specs=(P(None, None, "gx", "gy"), P(None, "gx", "gy"), P()),
        out_specs=P(None, None, "gx", "gy"),
        check_vma=False,
    )
```

```python
import functools
import math

import jax
import jax.numpy as jnp
import ml_dtypes
import numpy as np
from jax import lax
from jax.experimental import pallas as pl
from jax.experimental.pallas import tpu as pltpu
from jax.sharding import PartitionSpec as P

SPACING = 2.0
CELLS = 128
GROUP = 4
EDGE = 24
BF16 = jnp.bfloat16


def kernel_of(coupling, stencil):
    root = (-1.0 + math.sqrt(1.0 - 4.0 * coupling * coupling)) / (2.0 * coupling)
    scale = 1.0 / math.sqrt(1.0 - 4.0 * coupling * coupling)

    def at(d):
        return sum(w * scale * root ** abs(d - m) for m, w in stencil.items())

    amplitude = at(2) / root**2
    return at, root, amplitude


def operators():
    h = SPACING
    a, b = 14.0 / 9.0 / (2.0 * h), 1.0 / 9.0 / (4.0 * h)
    first = {-1: a, 1: -a, -2: b, 2: -b}
    c, e = 12.0 / 11.0 / (h * h), 3.0 / 11.0 / (4.0 * h * h)
    second = {-1: c, 1: c, -2: e, 2: e, 0: -2.0 * c - 2.0 * e}
    return kernel_of(1.0 / 3.0, first), kernel_of(2.0 / 11.0, second)


def split(values):
    high = np.asarray(values, np.float64).astype(ml_dtypes.bfloat16)
    low = (np.asarray(values, np.float64) - high.astype(np.float64)).astype(ml_dtypes.bfloat16)
    return high, low


def constants():
    (k1, r1, a1), (k2, r2, a2) = operators()
    n = CELLS
    d1 = np.array([[k1(i - j) for j in range(n)] for i in range(n)])
    d2 = np.array([[k2(i - j) for j in range(n)] for i in range(n)])
    rows = np.concatenate([d1.reshape(n // 8, 8, n), d2.reshape(n // 8, 8, n)], axis=1).reshape(2 * n, n)
    high, low = split(rows)
    along_x = np.concatenate([high, high, low], axis=1)
    high, low = split(np.concatenate([d1.T, d2.T], axis=1))
    i = np.arange(n)
    e1, e2 = k1(1) - a1 * r1, k2(1) - a2 * r2
    zero = np.zeros(n)
    first, last = (i == 0) * 1.0, (i == n - 1) * 1.0
    before = np.stack([
        np.concatenate([r1**i, zero]),
        np.concatenate([zero, r2**i]),
        np.concatenate([e1 * first, e2 * first]),
    ])
    after = np.stack([
        np.concatenate([-(r1 ** (n - 1 - i)), zero]),
        np.concatenate([zero, r2 ** (n - 1 - i)]),
        np.concatenate([-e1 * last, e2 * last]),
    ])
    spread = np.repeat(np.concatenate([before, after]), GROUP, axis=0)
    spread_high, spread_low = split(spread)
    blank = np.zeros((8, 2 * n), spread_high.dtype)
    along_y = np.concatenate([high, high, low], axis=0)
    spread_y = np.concatenate([spread_high, spread_high, spread_low, blank], axis=0)
    forward = np.stack([a1 * r1 ** (n - i.astype(float)), a2 * r2 ** (n - i.astype(float)), last, zero])
    backward = np.stack([a1 * r1 ** (1.0 + i), a2 * r2 ** (1.0 + i), first, zero])
    high, low = split(np.concatenate([forward, backward]))
    sums_y = np.concatenate(
        [np.concatenate([high, high], axis=1), np.concatenate([low, np.zeros_like(low)], axis=1)], axis=0
    )
    lanes = np.ones((1, n))
    edge_x = np.stack([
        forward[0, n - EDGE :, None] * lanes,
        forward[1, n - EDGE :, None] * lanes,
        backward[0, :EDGE, None] * lanes,
        backward[1, :EDGE, None] * lanes,
        (r1 ** i[:EDGE])[:, None] * lanes,
        (r2 ** i[:EDGE])[:, None] * lanes,
        (e1 * first)[:EDGE, None] * lanes,
        (e2 * first)[:EDGE, None] * lanes,
        (-(r1 ** (n - 1 - i)))[n - EDGE :, None] * lanes,
        (r2 ** (n - 1 - i))[n - EDGE :, None] * lanes,
        (-e1 * last)[n - EDGE :, None] * lanes,
        (e2 * last)[n - EDGE :, None] * lanes,
    ]).astype(np.float32)
    return along_x, along_y, spread_y, sums_y, edge_x


def dot(a, b):
    return lax.dot_general(a, b, (((1,), (0,)), ((), ())), preferred_element_type=jnp.float32)


def dot_transposed(a, b):
    return lax.dot_general(a, b, (((1,), (1,)), ((), ())), preferred_element_type=jnp.float32)


def first_kernel(
    groups, vel_hbm, leaf_hbm, table_hbm, along_x_hbm, along_y_hbm, spread_y_hbm, sums_y_hbm, edge_x_hbm,
    vel, tend, recv_x, recv_y, spread_y, edge_x,
    parts, leaf, send_x, send_y, along_x, along_y, sums_y, table_ref,
    vel_sem, leaf_sem, const_sem, send_sem, recv_sem, send_y_sem, recv_y_sem,
):
    n = CELLS
    half = 2 * GROUP
    halves = groups // 2

    consts = [
        pltpu.make_async_copy(a, b, const_sem.at[i])
        for i, (a, b) in enumerate(
            [(edge_x_hbm, edge_x), (sums_y_hbm, sums_y), (along_x_hbm, along_x), (along_y_hbm, along_y),
             (table_hbm, table_ref), (spread_y_hbm, spread_y)]
        )
    ]

    def levels(g):
        return pl.ds(g * GROUP, GROUP)

    def edge_copy(h, side):
        at = (slice(None), pl.ds(h * half, half), pl.ds(side * (n - EDGE), EDGE))
        return pltpu.make_async_copy(vel_hbm.at[at], vel.at[at], vel_sem.at[side, h])

    def middle_copy(g):
        at = (slice(None), levels(g), pl.ds(EDGE, n - 2 * EDGE))
        return pltpu.make_async_copy(vel_hbm.at[at], vel.at[at], vel_sem.at[2, g])

    def leaf_copy(g):
        return pltpu.make_async_copy(leaf_hbm.at[levels(g)], leaf.at[levels(g)], leaf_sem.at[g])

    consts[0].start()
    for h in range(halves):
        for side in range(2):
            edge_copy(h, side).start()
    consts[1].start()
    for g in range(groups):
        middle_copy(g).start()
    consts[4].start()
    consts[2].start()
    for g in range(groups):
        leaf_copy(g).start()
    consts[3].start()
    consts[5].start()

    mx, my = lax.axis_index("gx"), lax.axis_index("gy")
    nx, ny = lax.axis_size("gx"), lax.axis_size("gy")
    targets = [
        {"gx": lax.rem(mx + 1, nx)},
        {"gx": lax.rem(mx + nx - 1, nx)},
        {"gy": lax.rem(my + 1, ny)},
        {"gy": lax.rem(my + ny - 1, ny)},
    ]
    barrier = pltpu.get_barrier_semaphore()
    for target in targets:
        pl.semaphore_signal(barrier, inc=1, device_id=target, device_id_type=pl.DeviceIdType.MESH)

    def send_x_copy(side):
        return pltpu.make_async_remote_copy(
            src_ref=send_x.at[side], dst_ref=recv_x.at[side],
            send_sem=send_sem.at[side], recv_sem=recv_sem.at[side],
            device_id=targets[side], device_id_type=pl.DeviceIdType.MESH,
        )

    def send_y_copy(side, g):
        return pltpu.make_async_remote_copy(
            src_ref=send_y.at[side, g], dst_ref=recv_y.at[side, g],
            send_sem=send_y_sem.at[side, g], recv_sem=recv_y_sem.at[side, g],
            device_id=targets[2 + side], device_id_type=pl.DeviceIdType.MESH,
        )

    consts[0].wait()

    @pl.loop(0, halves)
    def _(h):
        edge_copy(h, 0).wait()
        edge_copy(h, 1).wait()
        for c in range(3):
            for k in range(half):
                top, bottom = vel[c, h * half + k, :EDGE], vel[c, h * half + k, n - EDGE :]
                for q in range(2):
                    row = (c * 3 + q) * half + k
                    send_x[0, h, row : row + 1] = jnp.sum(edge_x[q] * bottom, axis=0, keepdims=True)
                    send_x[1, h, row : row + 1] = jnp.sum(edge_x[2 + q] * top, axis=0, keepdims=True)
                row = (c * 3 + 2) * half + k
                send_x[0, h, row : row + 1] = bottom[EDGE - 1 :]
                send_x[1, h, row : row + 1] = top[:1]

    pl.semaphore_wait(barrier, 4)
    for side in range(2):
        send_x_copy(side).start()

    consts[1].wait()

    @pl.loop(0, groups)
    def _(g):
        middle_copy(g).wait()
        for c in range(3):
            for k in range(GROUP):
                values = vel[c, g * GROUP + k]
                high = values.astype(BF16)
                parts[c, g * GROUP + k, :, :n] = high
                parts[c, g * GROUP + k, :, n:] = (values - high.astype(jnp.float32)).astype(BF16)
            for k in range(0, GROUP, 2):
                pair = parts[c, pl.ds(g * GROUP + k, 2)].reshape(2 * n, 2 * n)
                sums = dot_transposed(sums_y[...], pair)
                sums = sums[:8] + sums[8:]
                for j in range(2):
                    for q in range(3):
                        row = (c * 3 + q) * GROUP + k + j
                        send_y[0, g, row : row + 1] = sums[q : q + 1, j * n : (j + 1) * n]
                        send_y[1, g, row : row + 1] = sums[4 + q : 5 + q, j * n : (j + 1) * n]
        for side in range(2):
            send_y[side, g, 9 * GROUP :] = jnp.zeros((4, n), jnp.float32)
            send_y_copy(side, g).start()

    lane = lax.broadcasted_iota(jnp.int32, (n, n), 1)
    consts[4].wait()
    table = jnp.zeros((n, n), jnp.float32)
    for k in range(table_ref.shape[0]):
        table = jnp.where(lane == k, table_ref[k], table)
    consts[2].wait()

    @pl.loop(0, groups)
    def _(g):
        leaf_copy(g).wait()
        for k in range(0, GROUP, 2):
            z = (g * GROUP + k, g * GROUP + k + 1)
            drag = []
            for j in range(2):
                speed = jnp.sqrt(vel[0, z[j]] ** 2 + vel[1, z[j]] ** 2 + vel[2, z[j]] ** 2)
                drag.append(jnp.take_along_axis(table, leaf[z[j]], axis=1) * speed)
            for c in range(3):
                high = jnp.concatenate([parts[c, z[0], :, :n], parts[c, z[1], :, :n]], axis=1)
                low = jnp.concatenate([parts[c, z[0], :, n:], parts[c, z[1], :, n:]], axis=1)
                both = dot(along_x[...], jnp.concatenate([high, low, high], axis=0))
                both = both.reshape(n // 8, 2, 8, 2 * n)
                for j in range(2):
                    gradient = both[:, 0, :, j * n : (j + 1) * n].reshape(n, n)
                    curvature = both[:, 1, :, j * n : (j + 1) * n].reshape(n, n)
                    tend[c, z[j]] = curvature - vel[0, z[j]] * gradient - drag[j] * vel[c, z[j]]

    consts[3].wait()

    @pl.loop(0, groups)
    def _(g):
        for k in range(GROUP):
            z = g * GROUP + k
            left = [jnp.concatenate([parts[c, z], parts[c, z, :, :n]], axis=1) for c in range(3)]
            both = dot(jnp.concatenate(left, axis=0), along_y[...])
            for c in range(3):
                gradient = both[c * n : (c + 1) * n, :n]
                curvature = both[c * n : (c + 1) * n, n:]
                tend[c, z] += curvature - vel[1, z] * gradient

    @pl.loop(0, groups)
    def _(g):
        for side in range(2):
            send_y_copy(side, g).wait()

    for side in range(2):
        send_x_copy(side).wait()
    consts[5].wait()


def second_kernel(groups, vel, tend, recv_x, recv_y, spread_y, edge_x, out_hbm, result, out_sem):
    n = CELLS
    half = 2 * GROUP
    values = 3 * GROUP

    def out_copy(z):
        return pltpu.make_async_copy(result.at[:, z], out_hbm.at[:, z], out_sem.at[z])

    lane = lax.broadcasted_iota(jnp.int32, (n, 80), 1)
    for g in range(groups):
        spread = []
        for c in range(3):
            got = jnp.concatenate([recv_y[side, g, c * values : (c + 1) * values] for side in range(2)], axis=0)
            high = got.astype(BF16).astype(jnp.float32)
            low = (got - high).astype(BF16).astype(jnp.float32)
            blank = jnp.zeros((8, n), jnp.float32)
            spread.append(jnp.concatenate([high, low, high, blank], axis=0).T.astype(BF16))
        for k in range(GROUP):
            z = g * GROUP + k
            mask = (lane % GROUP) == k
            left = [jnp.where(mask, s, jnp.zeros_like(s)) for s in spread]
            both = dot(jnp.concatenate(left, axis=0), spread_y[...])
            for c in range(3):
                gradient = both[c * n : (c + 1) * n, :n]
                curvature = both[c * n : (c + 1) * n, n:]
                values_z = tend[c, z] + curvature - vel[1, z] * gradient
                ends = []
                for side in range(2):
                    h, at = g // 2, c * 3 * half + (g % 2) * GROUP + k
                    s1, s2, s3 = (recv_x[side, h, at + q * half : at + q * half + 1] for q in range(3))
                    gradient = edge_x[4 + 4 * side] * s1 + edge_x[6 + 4 * side] * s3
                    curvature = edge_x[5 + 4 * side] * s2 + edge_x[7 + 4 * side] * s3
                    rows = slice(side * (n - EDGE), side * (n - EDGE) + EDGE)
                    ends.append(values_z[rows] + curvature - vel[0, z, rows] * gradient)
                result[c, z] = jnp.concatenate([ends[0], values_z[EDGE : n - EDGE], ends[1]], axis=0)
            out_copy(z).start()
    for z in range(groups * GROUP):
        out_copy(z).wait()


def in_hbm(array):
    return pltpu.with_memory_space_constraint(array, pltpu.HBM)


def body(velocity, leaf_class, drag_table):
    along_x, along_y, spread_y, sums_y, edge_x = (in_hbm(jnp.asarray(a)) for a in constants())
    velocity, leaf_class, drag_table = in_hbm(velocity), in_hbm(leaf_class), in_hbm(drag_table)
    levels, n = velocity.shape[1], CELLS
    groups = levels // GROUP
    hbm = pl.BlockSpec(memory_space=pltpu.HBM)
    vmem = pl.BlockSpec(memory_space=pltpu.VMEM)
    dma = pltpu.SemaphoreType.DMA
    sums_along_x = (2, groups // 2, 18 * GROUP, n)
    sums_along_y = (2, groups, 10 * GROUP, n)
    held = [
        jax.ShapeDtypeStruct(velocity.shape, jnp.float32),
        jax.ShapeDtypeStruct(velocity.shape, jnp.float32),
        jax.ShapeDtypeStruct(sums_along_x, jnp.float32),
        jax.ShapeDtypeStruct(sums_along_y, jnp.float32),
        jax.ShapeDtypeStruct(spread_y.shape, BF16),
        jax.ShapeDtypeStruct(edge_x.shape, jnp.float32),
    ]
    held = pl.pallas_call(
        functools.partial(first_kernel, groups),
        out_shape=held,
        in_specs=[hbm] * 8,
        out_specs=[vmem] * 6,
        scratch_shapes=[
            pltpu.VMEM((3, levels, n, 2 * n), BF16),
            pltpu.VMEM(leaf_class.shape, jnp.int32),
            pltpu.VMEM(sums_along_x, jnp.float32),
            pltpu.VMEM(sums_along_y, jnp.float32),
            pltpu.VMEM(along_x.shape, BF16),
            pltpu.VMEM(along_y.shape, BF16),
            pltpu.VMEM(sums_y.shape, BF16),
            pltpu.SMEM(drag_table.shape, jnp.float32),
            dma((3, groups)), dma((groups,)), dma((6,)), dma((2,)), dma((2,)), dma((2, groups)), dma((2, groups)),
        ],
        compiler_params=pltpu.CompilerParams(
            collective_id=0, has_side_effects=True, vmem_limit_bytes=40 * 1024 * 1024
        ),
        cost_estimate=pl.CostEstimate(flops=4_000_000_000, bytes_accessed=5_000_000, transcendentals=300_000),
        name="exchange_and_solve",
    )(velocity, leaf_class, drag_table, along_x, along_y, spread_y, sums_y, edge_x)
    return pl.pallas_call(
        functools.partial(second_kernel, groups),
        out_shape=jax.ShapeDtypeStruct(velocity.shape, jnp.float32),
        in_specs=[vmem] * 6,
        out_specs=hbm,
        scratch_shapes=[pltpu.VMEM(velocity.shape, jnp.float32), dma((levels,))],
        compiler_params=pltpu.CompilerParams(vmem_limit_bytes=40 * 1024 * 1024),
        cost_estimate=pl.CostEstimate(flops=1_000_000_000, bytes_accessed=3_000_000, transcendentals=0),
        name="finish",
    )(*held)


def solution(mesh):
    return jax.shard_map(
        body,
        mesh=mesh,
        in_specs=(P(None, None, "gx", "gy"), P(None, "gx", "gy"), P()),
        out_specs=P(None, None, "gx", "gy"),
        check_vma=False,
    )
```

```python
import functools
import math

import jax
import jax.numpy as jnp
import ml_dtypes
import numpy as np
from jax import lax
from jax.experimental import pallas as pl
from jax.experimental.pallas import tpu as pltpu
from jax.sharding import PartitionSpec as P

SPACING = 2.0
CELLS = 128
GROUP = 4
EDGE = 24
BF16 = jnp.bfloat16


def kernel_of(coupling, stencil):
    root = (-1.0 + math.sqrt(1.0 - 4.0 * coupling * coupling)) / (2.0 * coupling)
    scale = 1.0 / math.sqrt(1.0 - 4.0 * coupling * coupling)

    def at(d):
        return sum(w * scale * root ** abs(d - m) for m, w in stencil.items())

    amplitude = at(2) / root**2
    return at, root, amplitude


def operators():
    h = SPACING
    a, b = 14.0 / 9.0 / (2.0 * h), 1.0 / 9.0 / (4.0 * h)
    first = {-1: a, 1: -a, -2: b, 2: -b}
    c, e = 12.0 / 11.0 / (h * h), 3.0 / 11.0 / (4.0 * h * h)
    second = {-1: c, 1: c, -2: e, 2: e, 0: -2.0 * c - 2.0 * e}
    return kernel_of(1.0 / 3.0, first), kernel_of(2.0 / 11.0, second)


def split(values):
    high = np.asarray(values, np.float64).astype(ml_dtypes.bfloat16)
    low = (np.asarray(values, np.float64) - high.astype(np.float64)).astype(ml_dtypes.bfloat16)
    return high, low


def constants():
    (k1, r1, a1), (k2, r2, a2) = operators()
    n = CELLS
    d1 = np.array([[k1(i - j) for j in range(n)] for i in range(n)])
    d2 = np.array([[k2(i - j) for j in range(n)] for i in range(n)])
    rows = np.concatenate([d1.reshape(n // 8, 8, n), d2.reshape(n // 8, 8, n)], axis=1).reshape(2 * n, n)
    high, low = split(rows)
    along_x = np.concatenate([high, high, low], axis=1)
    high, low = split(np.concatenate([d1.T, d2.T], axis=1))
    i = np.arange(n)
    e1, e2 = k1(1) - a1 * r1, k2(1) - a2 * r2
    zero = np.zeros(n)
    first, last = (i == 0) * 1.0, (i == n - 1) * 1.0
    before = np.stack([
        np.concatenate([r1**i, zero]),
        np.concatenate([zero, r2**i]),
        np.concatenate([e1 * first, e2 * first]),
    ])
    after = np.stack([
        np.concatenate([-(r1 ** (n - 1 - i)), zero]),
        np.concatenate([zero, r2 ** (n - 1 - i)]),
        np.concatenate([-e1 * last, e2 * last]),
    ])
    spread = np.repeat(np.concatenate([before, after]), GROUP, axis=0)
    spread_high, spread_low = split(spread)
    blank = np.zeros((8, 2 * n), spread_high.dtype)
    along_y = np.concatenate([high, high, low], axis=0)
    spread_y = np.concatenate([spread_high, spread_high, spread_low, blank], axis=0)
    forward = np.stack([a1 * r1 ** (n - i.astype(float)), a2 * r2 ** (n - i.astype(float)), last, zero])
    backward = np.stack([a1 * r1 ** (1.0 + i), a2 * r2 ** (1.0 + i), first, zero])
    high, low = split(np.concatenate([forward, backward]))
    sums_y = np.concatenate(
        [np.concatenate([high, high], axis=1), np.concatenate([low, np.zeros_like(low)], axis=1)], axis=0
    )
    lanes = np.ones((1, n))
    edge_x = np.stack([
        forward[0, n - EDGE :, None] * lanes,
        forward[1, n - EDGE :, None] * lanes,
        backward[0, :EDGE, None] * lanes,
        backward[1, :EDGE, None] * lanes,
        (r1 ** i[:EDGE])[:, None] * lanes,
        (r2 ** i[:EDGE])[:, None] * lanes,
        (e1 * first)[:EDGE, None] * lanes,
        (e2 * first)[:EDGE, None] * lanes,
        (-(r1 ** (n - 1 - i)))[n - EDGE :, None] * lanes,
        (r2 ** (n - 1 - i))[n - EDGE :, None] * lanes,
        (-e1 * last)[n - EDGE :, None] * lanes,
        (e2 * last)[n - EDGE :, None] * lanes,
    ]).astype(np.float32)
    return along_x, along_y, spread_y, sums_y, edge_x


def dot(a, b):
    return lax.dot_general(a, b, (((1,), (0,)), ((), ())), preferred_element_type=jnp.float32)


def dot_transposed(a, b):
    return lax.dot_general(a, b, (((1,), (1,)), ((), ())), preferred_element_type=jnp.float32)


def first_kernel(
    groups, vel_hbm, leaf_hbm, table_hbm, along_x_hbm, along_y_hbm, spread_y_hbm, sums_y_hbm, edge_x_hbm,
    vel, tend, recv_x, recv_y, spread_y, edge_x,
    parts, leaf, send_x, send_y, along_x, along_y, sums_y, table_ref,
    vel_sem, leaf_sem, const_sem, send_sem, recv_sem,
):
    n = CELLS
    half = 2 * GROUP
    halves = groups // 2

    consts = [
        pltpu.make_async_copy(a, b, const_sem.at[i])
        for i, (a, b) in enumerate(
            [(edge_x_hbm, edge_x), (sums_y_hbm, sums_y), (along_x_hbm, along_x), (along_y_hbm, along_y),
             (table_hbm, table_ref), (spread_y_hbm, spread_y)]
        )
    ]

    def levels(g):
        return pl.ds(g * GROUP, GROUP)

    def edge_copy(h, side):
        at = (slice(None), pl.ds(h * half, half), pl.ds(side * (n - EDGE), EDGE))
        return pltpu.make_async_copy(vel_hbm.at[at], vel.at[at], vel_sem.at[side, h])

    def middle_copy(g):
        at = (slice(None), levels(g), pl.ds(EDGE, n - 2 * EDGE))
        return pltpu.make_async_copy(vel_hbm.at[at], vel.at[at], vel_sem.at[2, g])

    def leaf_copy(g):
        return pltpu.make_async_copy(leaf_hbm.at[levels(g)], leaf.at[levels(g)], leaf_sem.at[g])

    consts[0].start()
    for h in range(halves):
        for side in range(2):
            edge_copy(h, side).start()
    consts[1].start()
    for g in range(groups):
        middle_copy(g).start()
    consts[4].start()
    consts[2].start()
    for g in range(groups):
        leaf_copy(g).start()
    consts[3].start()
    consts[5].start()

    mx, my = lax.axis_index("gx"), lax.axis_index("gy")
    nx, ny = lax.axis_size("gx"), lax.axis_size("gy")
    targets = [
        {"gx": lax.rem(mx + 1, nx)},
        {"gx": lax.rem(mx + nx - 1, nx)},
        {"gy": lax.rem(my + 1, ny)},
        {"gy": lax.rem(my + ny - 1, ny)},
    ]
    first, last = my == 0, my == ny - 1
    barrier = pltpu.get_barrier_semaphore()
    for target in (targets[0], targets[1], targets[3]):
        pl.semaphore_signal(barrier, inc=1, device_id=target, device_id_type=pl.DeviceIdType.MESH)

    @pl.when(jnp.logical_not(last))
    def _():
        pl.semaphore_signal(barrier, inc=1, device_id=targets[2], device_id_type=pl.DeviceIdType.MESH)

    late = jnp.logical_or(mx == nx - 1, last)
    sending_step = jnp.where(late, 0, jnp.where(mx == 0, groups, groups // 2))
    sending_step = jnp.where(jnp.logical_and(last, mx == 0), groups // 2, sending_step)

    def sum_copy(t):
        source, landing = ((send_x, recv_x), (send_y, recv_y))[t // 2]
        return pltpu.make_async_remote_copy(
            src_ref=source.at[t % 2], dst_ref=landing.at[t % 2],
            send_sem=send_sem.at[t], recv_sem=recv_sem.at[t],
            device_id=targets[t], device_id_type=pl.DeviceIdType.MESH,
        )

    def send_sums():
        @pl.when(first)
        def _():
            pl.semaphore_wait(barrier, 3)

        @pl.when(jnp.logical_not(first))
        def _():
            pl.semaphore_wait(barrier, 4)

        for t in range(3):
            sum_copy(t).start()

        @pl.when(jnp.logical_not(first))
        def _():
            sum_copy(3).start()

    consts[0].wait()

    @pl.loop(0, halves)
    def _(h):
        edge_copy(h, 0).wait()
        edge_copy(h, 1).wait()
        for c in range(3):
            for k in range(half):
                top, bottom = vel[c, h * half + k, :EDGE], vel[c, h * half + k, n - EDGE :]
                for q in range(2):
                    row = (c * 3 + q) * half + k
                    send_x[0, h, row : row + 1] = jnp.sum(edge_x[q] * bottom, axis=0, keepdims=True)
                    send_x[1, h, row : row + 1] = jnp.sum(edge_x[2 + q] * top, axis=0, keepdims=True)
                row = (c * 3 + 2) * half + k
                send_x[0, h, row : row + 1] = bottom[EDGE - 1 :]
                send_x[1, h, row : row + 1] = top[:1]

    consts[1].wait()

    @pl.loop(0, groups)
    def _(g):
        middle_copy(g).wait()
        for c in range(3):
            for k in range(GROUP):
                values = vel[c, g * GROUP + k]
                high = values.astype(BF16)
                parts[c, g * GROUP + k, :, :n] = high
                parts[c, g * GROUP + k, :, n:] = (values - high.astype(jnp.float32)).astype(BF16)
            for k in range(0, GROUP, 2):
                pair = parts[c, pl.ds(g * GROUP + k, 2)].reshape(2 * n, 2 * n)
                sums = dot_transposed(sums_y[...], pair)
                sums = sums[:8] + sums[8:]
                for j in range(2):
                    for q in range(3):
                        row = (c * 3 + q) * GROUP + k + j
                        send_y[0, g, row : row + 1] = sums[q : q + 1, j * n : (j + 1) * n]
                        send_y[1, g, row : row + 1] = sums[4 + q : 5 + q, j * n : (j + 1) * n]
        for side in range(2):
            send_y[side, g, 9 * GROUP :] = jnp.zeros((4, n), jnp.float32)

    lane = lax.broadcasted_iota(jnp.int32, (n, n), 1)
    consts[4].wait()
    table = jnp.zeros((n, n), jnp.float32)
    for k in range(table_ref.shape[0]):
        table = jnp.where(lane == k, table_ref[k], table)
    consts[2].wait()

    @pl.loop(0, groups)
    def _(g):
        @pl.when(g == sending_step)
        def _():
            send_sums()

        leaf_copy(g).wait()
        for k in range(0, GROUP, 2):
            z = (g * GROUP + k, g * GROUP + k + 1)
            drag = []
            for j in range(2):
                speed = jnp.sqrt(vel[0, z[j]] ** 2 + vel[1, z[j]] ** 2 + vel[2, z[j]] ** 2)
                drag.append(jnp.take_along_axis(table, leaf[z[j]], axis=1) * speed)
            for c in range(3):
                high = jnp.concatenate([parts[c, z[0], :, :n], parts[c, z[1], :, :n]], axis=1)
                low = jnp.concatenate([parts[c, z[0], :, n:], parts[c, z[1], :, n:]], axis=1)
                both = dot(along_x[...], jnp.concatenate([high, low, high], axis=0))
                both = both.reshape(n // 8, 2, 8, 2 * n)
                for j in range(2):
                    gradient = both[:, 0, :, j * n : (j + 1) * n].reshape(n, n)
                    curvature = both[:, 1, :, j * n : (j + 1) * n].reshape(n, n)
                    tend[c, z[j]] = curvature - vel[0, z[j]] * gradient - drag[j] * vel[c, z[j]]

    @pl.when(sending_step == groups)
    def _():
        send_sums()

    consts[3].wait()

    @pl.loop(0, groups)
    def _(g):
        for k in range(GROUP):
            z = g * GROUP + k
            left = [jnp.concatenate([parts[c, z], parts[c, z, :, :n]], axis=1) for c in range(3)]
            both = dot(jnp.concatenate(left, axis=0), along_y[...])
            for c in range(3):
                gradient = both[c * n : (c + 1) * n, :n]
                curvature = both[c * n : (c + 1) * n, n:]
                tend[c, z] += curvature - vel[1, z] * gradient

    consts[5].wait()
    sum_copy(2).wait_recv()

    @pl.when(first)
    def _():
        sum_copy(3).start()

    for t in (3, 0, 1):
        sum_copy(t).wait_recv()
    for t in range(4):
        sum_copy(t).wait_send()


def second_kernel(groups, vel, tend, recv_x, recv_y, spread_y, edge_x, out_hbm, result, out_sem):
    n = CELLS
    half = 2 * GROUP
    values = 3 * GROUP

    def out_copy(z):
        return pltpu.make_async_copy(result.at[:, z], out_hbm.at[:, z], out_sem.at[z])

    lane = lax.broadcasted_iota(jnp.int32, (n, 80), 1)
    for g in range(groups):
        spread = []
        for c in range(3):
            got = jnp.concatenate([recv_y[side, g, c * values : (c + 1) * values] for side in range(2)], axis=0)
            high = got.astype(BF16).astype(jnp.float32)
            low = (got - high).astype(BF16).astype(jnp.float32)
            blank = jnp.zeros((8, n), jnp.float32)
            spread.append(jnp.concatenate([high, low, high, blank], axis=0).T.astype(BF16))
        for k in range(GROUP):
            z = g * GROUP + k
            mask = (lane % GROUP) == k
            left = [jnp.where(mask, s, jnp.zeros_like(s)) for s in spread]
            both = dot(jnp.concatenate(left, axis=0), spread_y[...])
            for c in range(3):
                gradient = both[c * n : (c + 1) * n, :n]
                curvature = both[c * n : (c + 1) * n, n:]
                values_z = tend[c, z] + curvature - vel[1, z] * gradient
                ends = []
                for side in range(2):
                    h, at = g // 2, c * 3 * half + (g % 2) * GROUP + k
                    s1, s2, s3 = (recv_x[side, h, at + q * half : at + q * half + 1] for q in range(3))
                    gradient = edge_x[4 + 4 * side] * s1 + edge_x[6 + 4 * side] * s3
                    curvature = edge_x[5 + 4 * side] * s2 + edge_x[7 + 4 * side] * s3
                    rows = slice(side * (n - EDGE), side * (n - EDGE) + EDGE)
                    ends.append(values_z[rows] + curvature - vel[0, z, rows] * gradient)
                result[c, z] = jnp.concatenate([ends[0], values_z[EDGE : n - EDGE], ends[1]], axis=0)
            out_copy(z).start()
    for z in range(groups * GROUP):
        out_copy(z).wait()


def in_hbm(array):
    return pltpu.with_memory_space_constraint(array, pltpu.HBM)


def body(velocity, leaf_class, drag_table):
    along_x, along_y, spread_y, sums_y, edge_x = (in_hbm(jnp.asarray(a)) for a in constants())
    velocity, leaf_class, drag_table = in_hbm(velocity), in_hbm(leaf_class), in_hbm(drag_table)
    levels, n = velocity.shape[1], CELLS
    groups = levels // GROUP
    hbm = pl.BlockSpec(memory_space=pltpu.HBM)
    vmem = pl.BlockSpec(memory_space=pltpu.VMEM)
    dma = pltpu.SemaphoreType.DMA
    sums_along_x = (2, groups // 2, 18 * GROUP, n)
    sums_along_y = (2, groups, 10 * GROUP, n)
    held = [
        jax.ShapeDtypeStruct(velocity.shape, jnp.float32),
        jax.ShapeDtypeStruct(velocity.shape, jnp.float32),
        jax.ShapeDtypeStruct(sums_along_x, jnp.float32),
        jax.ShapeDtypeStruct(sums_along_y, jnp.float32),
        jax.ShapeDtypeStruct(spread_y.shape, BF16),
        jax.ShapeDtypeStruct(edge_x.shape, jnp.float32),
    ]
    held = pl.pallas_call(
        functools.partial(first_kernel, groups),
        out_shape=held,
        in_specs=[hbm] * 8,
        out_specs=[vmem] * 6,
        scratch_shapes=[
            pltpu.VMEM((3, levels, n, 2 * n), BF16),
            pltpu.VMEM(leaf_class.shape, jnp.int32),
            pltpu.VMEM(sums_along_x, jnp.float32),
            pltpu.VMEM(sums_along_y, jnp.float32),
            pltpu.VMEM(along_x.shape, BF16),
            pltpu.VMEM(along_y.shape, BF16),
            pltpu.VMEM(sums_y.shape, BF16),
            pltpu.SMEM(drag_table.shape, jnp.float32),
            dma((3, groups)), dma((groups,)), dma((6,)), dma((4,)), dma((4,)),
        ],
        compiler_params=pltpu.CompilerParams(
            collective_id=0, has_side_effects=True, vmem_limit_bytes=40 * 1024 * 1024
        ),
        cost_estimate=pl.CostEstimate(flops=4_000_000_000, bytes_accessed=5_000_000, transcendentals=300_000),
        name="exchange_and_solve",
    )(velocity, leaf_class, drag_table, along_x, along_y, spread_y, sums_y, edge_x)
    return pl.pallas_call(
        functools.partial(second_kernel, groups),
        out_shape=jax.ShapeDtypeStruct(velocity.shape, jnp.float32),
        in_specs=[vmem] * 6,
        out_specs=hbm,
        scratch_shapes=[pltpu.VMEM(velocity.shape, jnp.float32), dma((levels,))],
        compiler_params=pltpu.CompilerParams(vmem_limit_bytes=40 * 1024 * 1024),
        cost_estimate=pl.CostEstimate(flops=1_000_000_000, bytes_accessed=3_000_000, transcendentals=0),
        name="finish",
    )(*held)


def solution(mesh):
    return jax.shard_map(
        body,
        mesh=mesh,
        in_specs=(P(None, None, "gx", "gy"), P(None, "gx", "gy"), P()),
        out_specs=P(None, None, "gx", "gy"),
        check_vma=False,
    )
```

```python
import functools
import math

import jax
import jax.numpy as jnp
import ml_dtypes
import numpy as np
from jax import lax
from jax.experimental import pallas as pl
from jax.experimental.pallas import tpu as pltpu
from jax.sharding import PartitionSpec as P

SPACING = 2.0
CELLS = 128
GROUP = 4
EDGE = 24
BF16 = jnp.bfloat16


def kernel_of(coupling, stencil):
    root = (-1.0 + math.sqrt(1.0 - 4.0 * coupling * coupling)) / (2.0 * coupling)
    scale = 1.0 / math.sqrt(1.0 - 4.0 * coupling * coupling)

    def at(d):
        return sum(w * scale * root ** abs(d - m) for m, w in stencil.items())

    amplitude = at(2) / root**2
    return at, root, amplitude


def operators():
    h = SPACING
    a, b = 14.0 / 9.0 / (2.0 * h), 1.0 / 9.0 / (4.0 * h)
    first = {-1: a, 1: -a, -2: b, 2: -b}
    c, e = 12.0 / 11.0 / (h * h), 3.0 / 11.0 / (4.0 * h * h)
    second = {-1: c, 1: c, -2: e, 2: e, 0: -2.0 * c - 2.0 * e}
    return kernel_of(1.0 / 3.0, first), kernel_of(2.0 / 11.0, second)


def split(values):
    high = np.asarray(values, np.float64).astype(ml_dtypes.bfloat16)
    low = (np.asarray(values, np.float64) - high.astype(np.float64)).astype(ml_dtypes.bfloat16)
    return high, low


def constants():
    (k1, r1, a1), (k2, r2, a2) = operators()
    n = CELLS
    d1 = np.array([[k1(i - j) for j in range(n)] for i in range(n)])
    d2 = np.array([[k2(i - j) for j in range(n)] for i in range(n)])
    rows = np.concatenate([d1.reshape(n // 8, 8, n), d2.reshape(n // 8, 8, n)], axis=1).reshape(2 * n, n)
    high, low = split(rows)
    along_x = np.concatenate([high, high, low], axis=1)
    high, low = split(np.concatenate([d1.T, d2.T], axis=1))
    i = np.arange(n)
    e1, e2 = k1(1) - a1 * r1, k2(1) - a2 * r2
    zero = np.zeros(n)
    first, last = (i == 0) * 1.0, (i == n - 1) * 1.0
    before = np.stack([
        np.concatenate([r1**i, zero]),
        np.concatenate([zero, r2**i]),
        np.concatenate([e1 * first, e2 * first]),
    ])
    after = np.stack([
        np.concatenate([-(r1 ** (n - 1 - i)), zero]),
        np.concatenate([zero, r2 ** (n - 1 - i)]),
        np.concatenate([-e1 * last, e2 * last]),
    ])
    spread = np.repeat(np.concatenate([before, after]), GROUP, axis=0)
    spread_high, spread_low = split(spread)
    blank = np.zeros((8, 2 * n), spread_high.dtype)
    along_y = np.concatenate([high, high, low], axis=0)
    spread_y = np.concatenate([spread_high, spread_high, spread_low, blank], axis=0)
    forward = np.stack([a1 * r1 ** (n - i.astype(float)), a2 * r2 ** (n - i.astype(float)), last, zero])
    backward = np.stack([a1 * r1 ** (1.0 + i), a2 * r2 ** (1.0 + i), first, zero])
    high, low = split(np.concatenate([forward, backward]))
    sums_y = np.concatenate(
        [np.concatenate([high, high], axis=1), np.concatenate([low, np.zeros_like(low)], axis=1)], axis=0
    )
    lanes = np.ones((1, n))
    edge_x = np.stack([
        forward[0, n - EDGE :, None] * lanes,
        forward[1, n - EDGE :, None] * lanes,
        backward[0, :EDGE, None] * lanes,
        backward[1, :EDGE, None] * lanes,
        (r1 ** i[:EDGE])[:, None] * lanes,
        (r2 ** i[:EDGE])[:, None] * lanes,
        (e1 * first)[:EDGE, None] * lanes,
        (e2 * first)[:EDGE, None] * lanes,
        (-(r1 ** (n - 1 - i)))[n - EDGE :, None] * lanes,
        (r2 ** (n - 1 - i))[n - EDGE :, None] * lanes,
        (-e1 * last)[n - EDGE :, None] * lanes,
        (e2 * last)[n - EDGE :, None] * lanes,
    ]).astype(np.float32)
    return along_x, along_y, spread_y, sums_y, edge_x


def dot(a, b):
    return lax.dot_general(a, b, (((1,), (0,)), ((), ())), preferred_element_type=jnp.float32)


def dot_transposed(a, b):
    return lax.dot_general(a, b, (((1,), (1,)), ((), ())), preferred_element_type=jnp.float32)


def first_kernel(
    groups, vel_hbm, leaf_hbm, table_hbm, along_x_hbm, along_y_hbm, spread_y_hbm, sums_y_hbm, edge_x_hbm,
    vel, tend, recv_x, recv_y, spread_y, edge_x,
    parts, leaf, send_x, send_y, along_x, along_y, sums_y, table_ref,
    vel_sem, leaf_sem, const_sem, send_sem, recv_sem, send_y_sem, recv_y_sem, last_sem,
):
    n = CELLS
    half = 2 * GROUP
    halves = groups // 2

    consts = [
        pltpu.make_async_copy(a, b, const_sem.at[i])
        for i, (a, b) in enumerate(
            [(edge_x_hbm, edge_x), (sums_y_hbm, sums_y), (along_x_hbm, along_x), (along_y_hbm, along_y),
             (table_hbm, table_ref), (spread_y_hbm, spread_y)]
        )
    ]

    def levels(g):
        return pl.ds(g * GROUP, GROUP)

    def edge_copy(h, side):
        at = (slice(None), pl.ds(h * half, half), pl.ds(side * (n - EDGE), EDGE))
        return pltpu.make_async_copy(vel_hbm.at[at], vel.at[at], vel_sem.at[side, h])

    def middle_copy(g):
        at = (slice(None), levels(g), pl.ds(EDGE, n - 2 * EDGE))
        return pltpu.make_async_copy(vel_hbm.at[at], vel.at[at], vel_sem.at[2, g])

    def leaf_copy(g):
        return pltpu.make_async_copy(leaf_hbm.at[levels(g)], leaf.at[levels(g)], leaf_sem.at[g])

    consts[0].start()
    for h in range(halves):
        for side in range(2):
            edge_copy(h, side).start()
    consts[1].start()
    for g in range(groups):
        middle_copy(g).start()
    consts[4].start()
    consts[2].start()
    for g in range(groups):
        leaf_copy(g).start()
    consts[3].start()
    consts[5].start()

    mx, my = lax.axis_index("gx"), lax.axis_index("gy")
    nx, ny = lax.axis_size("gx"), lax.axis_size("gy")
    targets = [
        {"gx": lax.rem(mx + 1, nx)},
        {"gx": lax.rem(mx + nx - 1, nx)},
        {"gy": lax.rem(my + 1, ny)},
        {"gy": lax.rem(my + ny - 1, ny)},
    ]
    first, last = my == 0, my == ny - 1
    barrier = pltpu.get_barrier_semaphore()
    for target in (targets[0], targets[1], targets[3]):
        pl.semaphore_signal(barrier, inc=1, device_id=target, device_id_type=pl.DeviceIdType.MESH)

    @pl.when(jnp.logical_not(last))
    def _():
        pl.semaphore_signal(barrier, inc=1, device_id=targets[2], device_id_type=pl.DeviceIdType.MESH)

    late = jnp.logical_or(jnp.logical_and(last, mx != 0), mx == nx - 1)
    punctual = jnp.logical_not(late)
    sending_step = jnp.where(jnp.logical_and(mx == 0, jnp.logical_not(last)), groups, groups // 2)

    def x_copy(side):
        return pltpu.make_async_remote_copy(
            src_ref=send_x.at[side], dst_ref=recv_x.at[side],
            send_sem=send_sem.at[side], recv_sem=recv_sem.at[side],
            device_id=targets[side], device_id_type=pl.DeviceIdType.MESH,
        )

    def y_copy(side, g):
        return pltpu.make_async_remote_copy(
            src_ref=send_y.at[side, g], dst_ref=recv_y.at[side, g],
            send_sem=send_y_sem.at[side, g], recv_sem=recv_y_sem.at[side, g],
            device_id=targets[2 + side], device_id_type=pl.DeviceIdType.MESH,
        )

    def meet_and_send_x():
        @pl.when(first)
        def _():
            pl.semaphore_wait(barrier, 3)

        @pl.when(jnp.logical_not(first))
        def _():
            pl.semaphore_wait(barrier, 4)

        @pl.when(last)
        def _():
            pl.semaphore_signal(last_sem, inc=1, device_id=targets[2], device_id_type=pl.DeviceIdType.MESH)

        for side in range(2):
            x_copy(side).start()

    def send_y_group(g):
        y_copy(0, g).start()

        @pl.when(jnp.logical_not(first))
        def _():
            y_copy(1, g).start()

    def meet_and_send():
        meet_and_send_x()
        for g in range(groups):
            send_y_group(g)

    consts[0].wait()

    @pl.loop(0, halves)
    def _(h):
        edge_copy(h, 0).wait()
        edge_copy(h, 1).wait()
        for c in range(3):
            for k in range(half):
                top, bottom = vel[c, h * half + k, :EDGE], vel[c, h * half + k, n - EDGE :]
                for q in range(2):
                    row = (c * 3 + q) * half + k
                    send_x[0, h, row : row + 1] = jnp.sum(edge_x[q] * bottom, axis=0, keepdims=True)
                    send_x[1, h, row : row + 1] = jnp.sum(edge_x[2 + q] * top, axis=0, keepdims=True)
                row = (c * 3 + 2) * half + k
                send_x[0, h, row : row + 1] = bottom[EDGE - 1 :]
                send_x[1, h, row : row + 1] = top[:1]

    @pl.when(late)
    def _():
        meet_and_send_x()

    consts[1].wait()

    @pl.loop(0, groups)
    def _(g):
        middle_copy(g).wait()
        for c in range(3):
            for k in range(GROUP):
                values = vel[c, g * GROUP + k]
                high = values.astype(BF16)
                parts[c, g * GROUP + k, :, :n] = high
                parts[c, g * GROUP + k, :, n:] = (values - high.astype(jnp.float32)).astype(BF16)
            for k in range(0, GROUP, 2):
                pair = parts[c, pl.ds(g * GROUP + k, 2)].reshape(2 * n, 2 * n)
                sums = dot_transposed(sums_y[...], pair)
                sums = sums[:8] + sums[8:]
                for j in range(2):
                    for q in range(3):
                        row = (c * 3 + q) * GROUP + k + j
                        send_y[0, g, row : row + 1] = sums[q : q + 1, j * n : (j + 1) * n]
                        send_y[1, g, row : row + 1] = sums[4 + q : 5 + q, j * n : (j + 1) * n]
        for side in range(2):
            send_y[side, g, 9 * GROUP :] = jnp.zeros((4, n), jnp.float32)

        @pl.when(late)
        def _():
            send_y_group(g)

    lane = lax.broadcasted_iota(jnp.int32, (n, n), 1)
    consts[4].wait()
    table = jnp.zeros((n, n), jnp.float32)
    for k in range(table_ref.shape[0]):
        table = jnp.where(lane == k, table_ref[k], table)
    consts[2].wait()

    @pl.loop(0, groups)
    def _(g):
        @pl.when(jnp.logical_and(punctual, g == sending_step))
        def _():
            meet_and_send()

        leaf_copy(g).wait()
        for k in range(0, GROUP, 2):
            z = (g * GROUP + k, g * GROUP + k + 1)
            drag = []
            for j in range(2):
                speed = jnp.sqrt(vel[0, z[j]] ** 2 + vel[1, z[j]] ** 2 + vel[2, z[j]] ** 2)
                drag.append(jnp.take_along_axis(table, leaf[z[j]], axis=1) * speed)
            for c in range(3):
                high = jnp.concatenate([parts[c, z[0], :, :n], parts[c, z[1], :, :n]], axis=1)
                low = jnp.concatenate([parts[c, z[0], :, n:], parts[c, z[1], :, n:]], axis=1)
                both = dot(along_x[...], jnp.concatenate([high, low, high], axis=0))
                both = both.reshape(n // 8, 2, 8, 2 * n)
                for j in range(2):
                    gradient = both[:, 0, :, j * n : (j + 1) * n].reshape(n, n)
                    curvature = both[:, 1, :, j * n : (j + 1) * n].reshape(n, n)
                    tend[c, z[j]] = curvature - vel[0, z[j]] * gradient - drag[j] * vel[c, z[j]]

    @pl.when(jnp.logical_and(punctual, sending_step == groups))
    def _():
        meet_and_send()

    consts[3].wait()

    @pl.loop(0, groups)
    def _(g):
        for k in range(GROUP):
            z = g * GROUP + k
            left = [jnp.concatenate([parts[c, z], parts[c, z, :, :n]], axis=1) for c in range(3)]
            both = dot(jnp.concatenate(left, axis=0), along_y[...])
            for c in range(3):
                gradient = both[c * n : (c + 1) * n, :n]
                curvature = both[c * n : (c + 1) * n, n:]
                tend[c, z] += curvature - vel[1, z] * gradient

    consts[5].wait()

    @pl.when(first)
    def _():
        pl.semaphore_wait(last_sem, 1)
        for g in range(groups):
            y_copy(1, g).start()

    for side in range(2):
        for g in range(groups):
            y_copy(side, g).wait_recv()
    for side in range(2):
        x_copy(side).wait_recv()
    for side in range(2):
        x_copy(side).wait_send()
        for g in range(groups):
            y_copy(side, g).wait_send()


def second_kernel(groups, vel, tend, recv_x, recv_y, spread_y, edge_x, out_hbm, result, out_sem):
    n = CELLS
    half = 2 * GROUP
    values = 3 * GROUP

    def out_copy(z):
        return pltpu.make_async_copy(result.at[:, z], out_hbm.at[:, z], out_sem.at[z])

    lane = lax.broadcasted_iota(jnp.int32, (n, 80), 1)
    for g in range(groups):
        spread = []
        for c in range(3):
            got = jnp.concatenate([recv_y[side, g, c * values : (c + 1) * values] for side in range(2)], axis=0)
            high = got.astype(BF16).astype(jnp.float32)
            low = (got - high).astype(BF16).astype(jnp.float32)
            blank = jnp.zeros((8, n), jnp.float32)
            spread.append(jnp.concatenate([high, low, high, blank], axis=0).T.astype(BF16))
        for k in range(GROUP):
            z = g * GROUP + k
            mask = (lane % GROUP) == k
            left = [jnp.where(mask, s, jnp.zeros_like(s)) for s in spread]
            both = dot(jnp.concatenate(left, axis=0), spread_y[...])
            for c in range(3):
                gradient = both[c * n : (c + 1) * n, :n]
                curvature = both[c * n : (c + 1) * n, n:]
                values_z = tend[c, z] + curvature - vel[1, z] * gradient
                ends = []
                for side in range(2):
                    h, at = g // 2, c * 3 * half + (g % 2) * GROUP + k
                    s1, s2, s3 = (recv_x[side, h, at + q * half : at + q * half + 1] for q in range(3))
                    gradient = edge_x[4 + 4 * side] * s1 + edge_x[6 + 4 * side] * s3
                    curvature = edge_x[5 + 4 * side] * s2 + edge_x[7 + 4 * side] * s3
                    rows = slice(side * (n - EDGE), side * (n - EDGE) + EDGE)
                    ends.append(values_z[rows] + curvature - vel[0, z, rows] * gradient)
                result[c, z] = jnp.concatenate([ends[0], values_z[EDGE : n - EDGE], ends[1]], axis=0)
            out_copy(z).start()
    for z in range(groups * GROUP):
        out_copy(z).wait()


def in_hbm(array):
    return pltpu.with_memory_space_constraint(array, pltpu.HBM)


def body(velocity, leaf_class, drag_table):
    along_x, along_y, spread_y, sums_y, edge_x = (in_hbm(jnp.asarray(a)) for a in constants())
    velocity, leaf_class, drag_table = in_hbm(velocity), in_hbm(leaf_class), in_hbm(drag_table)
    levels, n = velocity.shape[1], CELLS
    groups = levels // GROUP
    hbm = pl.BlockSpec(memory_space=pltpu.HBM)
    vmem = pl.BlockSpec(memory_space=pltpu.VMEM)
    dma = pltpu.SemaphoreType.DMA
    sums_along_x = (2, groups // 2, 18 * GROUP, n)
    sums_along_y = (2, groups, 10 * GROUP, n)
    held = [
        jax.ShapeDtypeStruct(velocity.shape, jnp.float32),
        jax.ShapeDtypeStruct(velocity.shape, jnp.float32),
        jax.ShapeDtypeStruct(sums_along_x, jnp.float32),
        jax.ShapeDtypeStruct(sums_along_y, jnp.float32),
        jax.ShapeDtypeStruct(spread_y.shape, BF16),
        jax.ShapeDtypeStruct(edge_x.shape, jnp.float32),
    ]
    held = pl.pallas_call(
        functools.partial(first_kernel, groups),
        out_shape=held,
        in_specs=[hbm] * 8,
        out_specs=[vmem] * 6,
        scratch_shapes=[
            pltpu.VMEM((3, levels, n, 2 * n), BF16),
            pltpu.VMEM(leaf_class.shape, jnp.int32),
            pltpu.VMEM(sums_along_x, jnp.float32),
            pltpu.VMEM(sums_along_y, jnp.float32),
            pltpu.VMEM(along_x.shape, BF16),
            pltpu.VMEM(along_y.shape, BF16),
            pltpu.VMEM(sums_y.shape, BF16),
            pltpu.SMEM(drag_table.shape, jnp.float32),
            dma((3, groups)), dma((groups,)), dma((6,)), dma((2,)), dma((2,)), dma((2, groups)), dma((2, groups)),
            pltpu.SemaphoreType.REGULAR,
        ],
        compiler_params=pltpu.CompilerParams(
            collective_id=0, has_side_effects=True, vmem_limit_bytes=40 * 1024 * 1024
        ),
        cost_estimate=pl.CostEstimate(flops=4_000_000_000, bytes_accessed=5_000_000, transcendentals=300_000),
        name="exchange_and_solve",
    )(velocity, leaf_class, drag_table, along_x, along_y, spread_y, sums_y, edge_x)
    return pl.pallas_call(
        functools.partial(second_kernel, groups),
        out_shape=jax.ShapeDtypeStruct(velocity.shape, jnp.float32),
        in_specs=[vmem] * 6,
        out_specs=hbm,
        scratch_shapes=[pltpu.VMEM(velocity.shape, jnp.float32), dma((levels,))],
        compiler_params=pltpu.CompilerParams(vmem_limit_bytes=40 * 1024 * 1024),
        cost_estimate=pl.CostEstimate(flops=1_000_000_000, bytes_accessed=3_000_000, transcendentals=0),
        name="finish",
    )(*held)


def solution(mesh):
    return jax.shard_map(
        body,
        mesh=mesh,
        in_specs=(P(None, None, "gx", "gy"), P(None, "gx", "gy"), P()),
        out_specs=P(None, None, "gx", "gy"),
        check_vma=False,
    )
```

```python
import functools
import math

import jax
import jax.numpy as jnp
import ml_dtypes
import numpy as np
from jax import lax
from jax.experimental import pallas as pl
from jax.experimental.pallas import tpu as pltpu
from jax.sharding import PartitionSpec as P

SPACING = 2.0
CELLS = 128
GROUP = 4
EDGE = 24
BF16 = jnp.bfloat16


def kernel_of(coupling, stencil):
    root = (-1.0 + math.sqrt(1.0 - 4.0 * coupling * coupling)) / (2.0 * coupling)
    scale = 1.0 / math.sqrt(1.0 - 4.0 * coupling * coupling)

    def at(d):
        return sum(w * scale * root ** abs(d - m) for m, w in stencil.items())

    amplitude = at(2) / root**2
    return at, root, amplitude


def operators():
    h = SPACING
    a, b = 14.0 / 9.0 / (2.0 * h), 1.0 / 9.0 / (4.0 * h)
    first = {-1: a, 1: -a, -2: b, 2: -b}
    c, e = 12.0 / 11.0 / (h * h), 3.0 / 11.0 / (4.0 * h * h)
    second = {-1: c, 1: c, -2: e, 2: e, 0: -2.0 * c - 2.0 * e}
    return kernel_of(1.0 / 3.0, first), kernel_of(2.0 / 11.0, second)


def split(values):
    high = np.asarray(values, np.float64).astype(ml_dtypes.bfloat16)
    low = (np.asarray(values, np.float64) - high.astype(np.float64)).astype(ml_dtypes.bfloat16)
    return high, low


def constants():
    (k1, r1, a1), (k2, r2, a2) = operators()
    n = CELLS
    d1 = np.array([[k1(i - j) for j in range(n)] for i in range(n)])
    d2 = np.array([[k2(i - j) for j in range(n)] for i in range(n)])
    rows = np.concatenate([d1.reshape(n // 8, 8, n), d2.reshape(n // 8, 8, n)], axis=1).reshape(2 * n, n)
    high, low = split(rows)
    along_x = np.concatenate([high, high, low], axis=1)
    high, low = split(np.concatenate([d1.T, d2.T], axis=1))
    i = np.arange(n)
    e1, e2 = k1(1) - a1 * r1, k2(1) - a2 * r2
    zero = np.zeros(n)
    first, last = (i == 0) * 1.0, (i == n - 1) * 1.0
    before = np.stack([
        np.concatenate([r1**i, zero]),
        np.concatenate([zero, r2**i]),
        np.concatenate([e1 * first, e2 * first]),
    ])
    after = np.stack([
        np.concatenate([-(r1 ** (n - 1 - i)), zero]),
        np.concatenate([zero, r2 ** (n - 1 - i)]),
        np.concatenate([-e1 * last, e2 * last]),
    ])
    spread = np.repeat(np.concatenate([before, after]), GROUP, axis=0)
    spread_high, spread_low = split(spread)
    blank = np.zeros((8, 2 * n), spread_high.dtype)
    along_y = np.concatenate([high, high, low], axis=0)
    spread_y = np.concatenate([spread_high, spread_high, spread_low, blank], axis=0)
    forward = np.stack([a1 * r1 ** (n - i.astype(float)), a2 * r2 ** (n - i.astype(float)), last, zero])
    backward = np.stack([a1 * r1 ** (1.0 + i), a2 * r2 ** (1.0 + i), first, zero])
    high, low = split(np.concatenate([forward, backward]))
    sums_y = np.concatenate(
        [np.concatenate([high, high], axis=1), np.concatenate([low, np.zeros_like(low)], axis=1)], axis=0
    )
    lanes = np.ones((1, n))
    edge_x = np.stack([
        forward[0, n - EDGE :, None] * lanes,
        forward[1, n - EDGE :, None] * lanes,
        backward[0, :EDGE, None] * lanes,
        backward[1, :EDGE, None] * lanes,
        (r1 ** i[:EDGE])[:, None] * lanes,
        (r2 ** i[:EDGE])[:, None] * lanes,
        (e1 * first)[:EDGE, None] * lanes,
        (e2 * first)[:EDGE, None] * lanes,
        (-(r1 ** (n - 1 - i)))[n - EDGE :, None] * lanes,
        (r2 ** (n - 1 - i))[n - EDGE :, None] * lanes,
        (-e1 * last)[n - EDGE :, None] * lanes,
        (e2 * last)[n - EDGE :, None] * lanes,
    ]).astype(np.float32)
    return along_x, along_y, spread_y, sums_y, edge_x


def dot(a, b):
    return lax.dot_general(a, b, (((1,), (0,)), ((), ())), preferred_element_type=jnp.float32)


def dot_transposed(a, b):
    return lax.dot_general(a, b, (((1,), (1,)), ((), ())), preferred_element_type=jnp.float32)


def first_kernel(
    groups, vel_hbm, leaf_hbm, table_hbm, along_x_hbm, along_y_hbm, spread_y_hbm, sums_y_hbm, edge_x_hbm,
    vel, tend, recv_x, recv_y, spread_y, edge_x,
    parts, leaf, send_x, send_y, along_x, along_y, sums_y, table_ref,
    vel_sem, leaf_sem, const_sem, send_sem, recv_sem, send_y_sem, recv_y_sem, last_sem,
):
    n = CELLS
    half = 2 * GROUP
    halves = groups // 2

    consts = [
        pltpu.make_async_copy(a, b, const_sem.at[i])
        for i, (a, b) in enumerate(
            [(edge_x_hbm, edge_x), (sums_y_hbm, sums_y), (along_x_hbm, along_x), (along_y_hbm, along_y),
             (table_hbm, table_ref), (spread_y_hbm, spread_y)]
        )
    ]

    def levels(g):
        return pl.ds(g * GROUP, GROUP)

    def edge_copy(h, side):
        at = (slice(None), pl.ds(h * half, half), pl.ds(side * (n - EDGE), EDGE))
        return pltpu.make_async_copy(vel_hbm.at[at], vel.at[at], vel_sem.at[side, h])

    def middle_copy(g):
        at = (slice(None), levels(g), pl.ds(EDGE, n - 2 * EDGE))
        return pltpu.make_async_copy(vel_hbm.at[at], vel.at[at], vel_sem.at[2, g])

    def leaf_copy(g):
        return pltpu.make_async_copy(leaf_hbm.at[levels(g)], leaf.at[levels(g)], leaf_sem.at[g])

    consts[0].start()
    for h in range(halves):
        for side in range(2):
            edge_copy(h, side).start()
    consts[1].start()
    for g in range(groups):
        middle_copy(g).start()
    consts[4].start()
    consts[2].start()
    for g in range(groups):
        leaf_copy(g).start()
    consts[3].start()
    consts[5].start()

    mx, my = lax.axis_index("gx"), lax.axis_index("gy")
    nx, ny = lax.axis_size("gx"), lax.axis_size("gy")
    targets = [
        {"gx": lax.rem(mx + 1, nx)},
        {"gx": lax.rem(mx + nx - 1, nx)},
        {"gy": lax.rem(my + 1, ny)},
        {"gy": lax.rem(my + ny - 1, ny)},
    ]
    first, last = my == 0, my == ny - 1
    barrier = pltpu.get_barrier_semaphore()
    for target in (targets[0], targets[1], targets[3]):
        pl.semaphore_signal(barrier, inc=1, device_id=target, device_id_type=pl.DeviceIdType.MESH)

    @pl.when(jnp.logical_not(last))
    def _():
        pl.semaphore_signal(barrier, inc=1, device_id=targets[2], device_id_type=pl.DeviceIdType.MESH)

    late_x = mx == nx - 1
    late_y = jnp.logical_and(last, mx != 0)
    late = jnp.logical_or(late_x, late_y)
    punctual = jnp.logical_not(late)
    sending_step = jnp.where(jnp.logical_and(mx == 0, jnp.logical_not(last)), groups, groups // 2)

    def x_copy(side):
        return pltpu.make_async_remote_copy(
            src_ref=send_x.at[side], dst_ref=recv_x.at[side],
            send_sem=send_sem.at[side], recv_sem=recv_sem.at[side],
            device_id=targets[side], device_id_type=pl.DeviceIdType.MESH,
        )

    def y_copy(side, g):
        return pltpu.make_async_remote_copy(
            src_ref=send_y.at[side, g], dst_ref=recv_y.at[side, g],
            send_sem=send_y_sem.at[side, g], recv_sem=recv_y_sem.at[side, g],
            device_id=targets[2 + side], device_id_type=pl.DeviceIdType.MESH,
        )

    def meet():
        @pl.when(first)
        def _():
            pl.semaphore_wait(barrier, 3)

        @pl.when(jnp.logical_not(first))
        def _():
            pl.semaphore_wait(barrier, 4)

        @pl.when(last)
        def _():
            pl.semaphore_signal(last_sem, inc=1, device_id=targets[2], device_id_type=pl.DeviceIdType.MESH)

    def send_x_sums():
        for side in range(2):
            x_copy(side).start()

    def send_y_back(g):
        @pl.when(jnp.logical_not(first))
        def _():
            y_copy(1, g).start()

    def send_rest():
        @pl.when(punctual)
        def _():
            meet()

        @pl.when(jnp.logical_not(late_x))
        def _():
            send_x_sums()

        for g in range(groups):
            @pl.when(jnp.logical_not(late_y))
            def _():
                y_copy(0, g).start()

            send_y_back(g)

    consts[0].wait()

    @pl.loop(0, halves)
    def _(h):
        edge_copy(h, 0).wait()
        edge_copy(h, 1).wait()
        for c in range(3):
            for k in range(half):
                top, bottom = vel[c, h * half + k, :EDGE], vel[c, h * half + k, n - EDGE :]
                for q in range(2):
                    row = (c * 3 + q) * half + k
                    send_x[0, h, row : row + 1] = jnp.sum(edge_x[q] * bottom, axis=0, keepdims=True)
                    send_x[1, h, row : row + 1] = jnp.sum(edge_x[2 + q] * top, axis=0, keepdims=True)
                row = (c * 3 + 2) * half + k
                send_x[0, h, row : row + 1] = bottom[EDGE - 1 :]
                send_x[1, h, row : row + 1] = top[:1]

    @pl.when(late)
    def _():
        meet()

    @pl.when(late_x)
    def _():
        send_x_sums()

    consts[1].wait()

    @pl.loop(0, groups)
    def _(g):
        middle_copy(g).wait()
        for c in range(3):
            for k in range(GROUP):
                values = vel[c, g * GROUP + k]
                high = values.astype(BF16)
                parts[c, g * GROUP + k, :, :n] = high
                parts[c, g * GROUP + k, :, n:] = (values - high.astype(jnp.float32)).astype(BF16)
            for k in range(0, GROUP, 2):
                pair = parts[c, pl.ds(g * GROUP + k, 2)].reshape(2 * n, 2 * n)
                sums = dot_transposed(sums_y[...], pair)
                sums = sums[:8] + sums[8:]
                for j in range(2):
                    for q in range(3):
                        row = (c * 3 + q) * GROUP + k + j
                        send_y[0, g, row : row + 1] = sums[q : q + 1, j * n : (j + 1) * n]
                        send_y[1, g, row : row + 1] = sums[4 + q : 5 + q, j * n : (j + 1) * n]
        for side in range(2):
            send_y[side, g, 9 * GROUP :] = jnp.zeros((4, n), jnp.float32)

        @pl.when(late_y)
        def _():
            y_copy(0, g).start()

    lane = lax.broadcasted_iota(jnp.int32, (n, n), 1)
    consts[4].wait()
    table = jnp.zeros((n, n), jnp.float32)
    for k in range(table_ref.shape[0]):
        table = jnp.where(lane == k, table_ref[k], table)
    consts[2].wait()

    @pl.loop(0, groups)
    def _(g):
        @pl.when(g == sending_step)
        def _():
            send_rest()

        leaf_copy(g).wait()
        for k in range(0, GROUP, 2):
            z = (g * GROUP + k, g * GROUP + k + 1)
            drag = []
            for j in range(2):
                speed = jnp.sqrt(vel[0, z[j]] ** 2 + vel[1, z[j]] ** 2 + vel[2, z[j]] ** 2)
                drag.append(jnp.take_along_axis(table, leaf[z[j]], axis=1) * speed)
            for c in range(3):
                high = jnp.concatenate([parts[c, z[0], :, :n], parts[c, z[1], :, :n]], axis=1)
                low = jnp.concatenate([parts[c, z[0], :, n:], parts[c, z[1], :, n:]], axis=1)
                both = dot(along_x[...], jnp.concatenate([high, low, high], axis=0))
                both = both.reshape(n // 8, 2, 8, 2 * n)
                for j in range(2):
                    gradient = both[:, 0, :, j * n : (j + 1) * n].reshape(n, n)
                    curvature = both[:, 1, :, j * n : (j + 1) * n].reshape(n, n)
                    tend[c, z[j]] = curvature - vel[0, z[j]] * gradient - drag[j] * vel[c, z[j]]

    @pl.when(sending_step == groups)
    def _():
        send_rest()

    consts[3].wait()

    @pl.loop(0, groups)
    def _(g):
        for k in range(GROUP):
            z = g * GROUP + k
            left = [jnp.concatenate([parts[c, z], parts[c, z, :, :n]], axis=1) for c in range(3)]
            both = dot(jnp.concatenate(left, axis=0), along_y[...])
            for c in range(3):
                gradient = both[c * n : (c + 1) * n, :n]
                curvature = both[c * n : (c + 1) * n, n:]
                tend[c, z] += curvature - vel[1, z] * gradient

    consts[5].wait()

    @pl.when(first)
    def _():
        pl.semaphore_wait(last_sem, 1)
        for g in range(groups):
            y_copy(1, g).start()

    for side in range(2):
        for g in range(groups):
            y_copy(side, g).wait_recv()
    for side in range(2):
        x_copy(side).wait_recv()
    for side in range(2):
        x_copy(side).wait_send()
        for g in range(groups):
            y_copy(side, g).wait_send()


def second_kernel(groups, vel, tend, recv_x, recv_y, spread_y, edge_x, out_hbm, result, out_sem):
    n = CELLS
    half = 2 * GROUP
    values = 3 * GROUP

    def out_copy(z):
        return pltpu.make_async_copy(result.at[:, z], out_hbm.at[:, z], out_sem.at[z])

    lane = lax.broadcasted_iota(jnp.int32, (n, 80), 1)

    @pl.loop(0, groups // 2)
    def _(h):
        for part in range(2):
            g = h * 2 + part
            spread = []
            for c in range(3):
                got = jnp.concatenate([recv_y[side, g, c * values : (c + 1) * values] for side in range(2)], axis=0)
                high = got.astype(BF16).astype(jnp.float32)
                low = (got - high).astype(BF16).astype(jnp.float32)
                blank = jnp.zeros((8, n), jnp.float32)
                spread.append(jnp.concatenate([high, low, high, blank], axis=0).T.astype(BF16))
            for k in range(GROUP):
                z = g * GROUP + k
                mask = (lane % GROUP) == k
                left = [jnp.where(mask, s, jnp.zeros_like(s)) for s in spread]
                both = dot(jnp.concatenate(left, axis=0), spread_y[...])
                for c in range(3):
                    gradient = both[c * n : (c + 1) * n, :n]
                    curvature = both[c * n : (c + 1) * n, n:]
                    values_z = tend[c, z] + curvature - vel[1, z] * gradient
                    ends = []
                    for side in range(2):
                        at = c * 3 * half + part * GROUP + k
                        s1, s2, s3 = (recv_x[side, h, at + q * half : at + q * half + 1] for q in range(3))
                        gradient = edge_x[4 + 4 * side] * s1 + edge_x[6 + 4 * side] * s3
                        curvature = edge_x[5 + 4 * side] * s2 + edge_x[7 + 4 * side] * s3
                        rows = slice(side * (n - EDGE), side * (n - EDGE) + EDGE)
                        ends.append(values_z[rows] + curvature - vel[0, z, rows] * gradient)
                    result[c, z] = jnp.concatenate([ends[0], values_z[EDGE : n - EDGE], ends[1]], axis=0)
                out_copy(z).start()

    for z in range(groups * GROUP):
        out_copy(z).wait()


def in_hbm(array):
    return pltpu.with_memory_space_constraint(array, pltpu.HBM)


def body(velocity, leaf_class, drag_table):
    along_x, along_y, spread_y, sums_y, edge_x = (in_hbm(jnp.asarray(a)) for a in constants())
    velocity, leaf_class, drag_table = in_hbm(velocity), in_hbm(leaf_class), in_hbm(drag_table)
    levels, n = velocity.shape[1], CELLS
    groups = levels // GROUP
    hbm = pl.BlockSpec(memory_space=pltpu.HBM)
    vmem = pl.BlockSpec(memory_space=pltpu.VMEM)
    dma = pltpu.SemaphoreType.DMA
    sums_along_x = (2, groups // 2, 18 * GROUP, n)
    sums_along_y = (2, groups, 10 * GROUP, n)
    held = [
        jax.ShapeDtypeStruct(velocity.shape, jnp.float32),
        jax.ShapeDtypeStruct(velocity.shape, jnp.float32),
        jax.ShapeDtypeStruct(sums_along_x, jnp.float32),
        jax.ShapeDtypeStruct(sums_along_y, jnp.float32),
        jax.ShapeDtypeStruct(spread_y.shape, BF16),
        jax.ShapeDtypeStruct(edge_x.shape, jnp.float32),
    ]
    held = pl.pallas_call(
        functools.partial(first_kernel, groups),
        out_shape=held,
        in_specs=[hbm] * 8,
        out_specs=[vmem] * 6,
        scratch_shapes=[
            pltpu.VMEM((3, levels, n, 2 * n), BF16),
            pltpu.VMEM(leaf_class.shape, jnp.int32),
            pltpu.VMEM(sums_along_x, jnp.float32),
            pltpu.VMEM(sums_along_y, jnp.float32),
            pltpu.VMEM(along_x.shape, BF16),
            pltpu.VMEM(along_y.shape, BF16),
            pltpu.VMEM(sums_y.shape, BF16),
            pltpu.SMEM(drag_table.shape, jnp.float32),
            dma((3, groups)), dma((groups,)), dma((6,)), dma((2,)), dma((2,)), dma((2, groups)), dma((2, groups)),
            pltpu.SemaphoreType.REGULAR,
        ],
        compiler_params=pltpu.CompilerParams(
            collective_id=0, has_side_effects=True, vmem_limit_bytes=40 * 1024 * 1024
        ),
        cost_estimate=pl.CostEstimate(flops=4_000_000_000, bytes_accessed=5_000_000, transcendentals=300_000),
        name="exchange_and_solve",
    )(velocity, leaf_class, drag_table, along_x, along_y, spread_y, sums_y, edge_x)
    return pl.pallas_call(
        functools.partial(second_kernel, groups),
        out_shape=jax.ShapeDtypeStruct(velocity.shape, jnp.float32),
        in_specs=[vmem] * 6,
        out_specs=hbm,
        scratch_shapes=[pltpu.VMEM(velocity.shape, jnp.float32), dma((levels,))],
        compiler_params=pltpu.CompilerParams(vmem_limit_bytes=40 * 1024 * 1024),
        cost_estimate=pl.CostEstimate(flops=1_000_000_000, bytes_accessed=3_000_000, transcendentals=0),
        name="finish",
    )(*held)


def solution(mesh):
    return jax.shard_map(
        body,
        mesh=mesh,
        in_specs=(P(None, None, "gx", "gy"), P(None, "gx", "gy"), P()),
        out_specs=P(None, None, "gx", "gy"),
        check_vma=False,
    )
```

```python
import functools
import math

import jax
import jax.numpy as jnp
import ml_dtypes
import numpy as np
from jax import lax
from jax.experimental import pallas as pl
from jax.experimental.pallas import tpu as pltpu
from jax.sharding import PartitionSpec as P

SPACING = 2.0
CELLS = 128
GROUP = 4
EDGE = 24
BF16 = jnp.bfloat16


def kernel_of(coupling, stencil):
    root = (-1.0 + math.sqrt(1.0 - 4.0 * coupling * coupling)) / (2.0 * coupling)
    scale = 1.0 / math.sqrt(1.0 - 4.0 * coupling * coupling)

    def at(d):
        return sum(w * scale * root ** abs(d - m) for m, w in stencil.items())

    amplitude = at(2) / root**2
    return at, root, amplitude


def operators():
    h = SPACING
    a, b = 14.0 / 9.0 / (2.0 * h), 1.0 / 9.0 / (4.0 * h)
    first = {-1: a, 1: -a, -2: b, 2: -b}
    c, e = 12.0 / 11.0 / (h * h), 3.0 / 11.0 / (4.0 * h * h)
    second = {-1: c, 1: c, -2: e, 2: e, 0: -2.0 * c - 2.0 * e}
    return kernel_of(1.0 / 3.0, first), kernel_of(2.0 / 11.0, second)


def split(values):
    high = np.asarray(values, np.float64).astype(ml_dtypes.bfloat16)
    low = (np.asarray(values, np.float64) - high.astype(np.float64)).astype(ml_dtypes.bfloat16)
    return high, low


def constants():
    (k1, r1, a1), (k2, r2, a2) = operators()
    n = CELLS
    d1 = np.array([[k1(i - j) for j in range(n)] for i in range(n)])
    d2 = np.array([[k2(i - j) for j in range(n)] for i in range(n)])
    rows = np.concatenate([d1.reshape(n // 8, 8, n), d2.reshape(n // 8, 8, n)], axis=1).reshape(2 * n, n)
    high, low = split(rows)
    along_x = np.concatenate([high, high, low], axis=1)
    high, low = split(np.concatenate([d1.T, d2.T], axis=1))
    i = np.arange(n)
    e1, e2 = k1(1) - a1 * r1, k2(1) - a2 * r2
    zero = np.zeros(n)
    first, last = (i == 0) * 1.0, (i == n - 1) * 1.0
    before = np.stack([
        np.concatenate([r1**i, zero]),
        np.concatenate([zero, r2**i]),
        np.concatenate([e1 * first, e2 * first]),
    ])
    after = np.stack([
        np.concatenate([-(r1 ** (n - 1 - i)), zero]),
        np.concatenate([zero, r2 ** (n - 1 - i)]),
        np.concatenate([-e1 * last, e2 * last]),
    ])
    spread = np.repeat(np.concatenate([before, after]), GROUP, axis=0)
    spread_high, spread_low = split(spread)
    blank = np.zeros((8, 2 * n), spread_high.dtype)
    along_y = np.concatenate([high, high, low], axis=0)
    spread_y = np.concatenate([spread_high, spread_high, spread_low, blank], axis=0)
    forward = np.stack([a1 * r1 ** (n - i.astype(float)), a2 * r2 ** (n - i.astype(float)), last, zero])
    backward = np.stack([a1 * r1 ** (1.0 + i), a2 * r2 ** (1.0 + i), first, zero])
    high, low = split(np.concatenate([forward, backward]))
    sums_y = np.concatenate(
        [np.concatenate([high, high], axis=1), np.concatenate([low, np.zeros_like(low)], axis=1)], axis=0
    )
    lanes = np.ones((1, n))
    edge_x = np.stack([
        forward[0, n - EDGE :, None] * lanes,
        forward[1, n - EDGE :, None] * lanes,
        backward[0, :EDGE, None] * lanes,
        backward[1, :EDGE, None] * lanes,
        (r1 ** i[:EDGE])[:, None] * lanes,
        (r2 ** i[:EDGE])[:, None] * lanes,
        (e1 * first)[:EDGE, None] * lanes,
        (e2 * first)[:EDGE, None] * lanes,
        (-(r1 ** (n - 1 - i)))[n - EDGE :, None] * lanes,
        (r2 ** (n - 1 - i))[n - EDGE :, None] * lanes,
        (-e1 * last)[n - EDGE :, None] * lanes,
        (e2 * last)[n - EDGE :, None] * lanes,
    ]).astype(np.float32)
    return along_x, along_y, spread_y, sums_y, edge_x


def dot(a, b):
    return lax.dot_general(a, b, (((1,), (0,)), ((), ())), preferred_element_type=jnp.float32)


def dot_transposed(a, b):
    return lax.dot_general(a, b, (((1,), (1,)), ((), ())), preferred_element_type=jnp.float32)


def first_kernel(
    groups, vel_hbm, leaf_hbm, table_hbm, along_x_hbm, along_y_hbm, spread_y_hbm, sums_y_hbm, edge_x_hbm,
    vel, tend, recv_x, recv_y, spread_y, edge_x,
    parts, leaf, send_x, send_y, along_x, along_y, sums_y, table_ref,
    vel_sem, leaf_sem, const_sem, send_sem, recv_sem, send_y_sem, recv_y_sem, last_sem,
):
    n = CELLS
    half = 2 * GROUP
    halves = groups // 2

    consts = [
        pltpu.make_async_copy(a, b, const_sem.at[i])
        for i, (a, b) in enumerate(
            [(edge_x_hbm, edge_x), (sums_y_hbm, sums_y), (along_x_hbm, along_x), (along_y_hbm, along_y),
             (table_hbm, table_ref), (spread_y_hbm, spread_y)]
        )
    ]

    def levels(g):
        return pl.ds(g * GROUP, GROUP)

    def edge_copy(h, side):
        at = (slice(None), pl.ds(h * half, half), pl.ds(side * (n - EDGE), EDGE))
        return pltpu.make_async_copy(vel_hbm.at[at], vel.at[at], vel_sem.at[side, h])

    def middle_copy(g):
        at = (slice(None), levels(g), pl.ds(EDGE, n - 2 * EDGE))
        return pltpu.make_async_copy(vel_hbm.at[at], vel.at[at], vel_sem.at[2, g])

    def leaf_copy(g):
        return pltpu.make_async_copy(leaf_hbm.at[levels(g)], leaf.at[levels(g)], leaf_sem.at[g])

    mx, my = lax.axis_index("gx"), lax.axis_index("gy")
    nx, ny = lax.axis_size("gx"), lax.axis_size("gy")
    targets = [
        {"gx": lax.rem(mx + 1, nx)},
        {"gx": lax.rem(mx + nx - 1, nx)},
        {"gy": lax.rem(my + 1, ny)},
        {"gy": lax.rem(my + ny - 1, ny)},
    ]
    first, last = my == 0, my == ny - 1
    barrier = pltpu.get_barrier_semaphore()
    for target in (targets[0], targets[1], targets[3]):
        pl.semaphore_signal(barrier, inc=1, device_id=target, device_id_type=pl.DeviceIdType.MESH)

    @pl.when(jnp.logical_not(last))
    def _():
        pl.semaphore_signal(barrier, inc=1, device_id=targets[2], device_id_type=pl.DeviceIdType.MESH)

    consts[0].start()
    for h in range(halves):
        for side in range(2):
            edge_copy(h, side).start()
    consts[1].start()
    for g in range(groups):
        middle_copy(g).start()
    consts[4].start()
    consts[2].start()
    for g in range(groups):
        leaf_copy(g).start()
    consts[3].start()
    consts[5].start()

    late_x = mx == nx - 1
    late_y = jnp.logical_and(last, mx != 0)
    late = jnp.logical_or(late_x, late_y)
    punctual = jnp.logical_not(late)
    sending_step = jnp.where(jnp.logical_and(mx == 0, jnp.logical_not(last)), groups, groups // 2)

    def x_copy(side):
        return pltpu.make_async_remote_copy(
            src_ref=send_x.at[side], dst_ref=recv_x.at[side],
            send_sem=send_sem.at[side], recv_sem=recv_sem.at[side],
            device_id=targets[side], device_id_type=pl.DeviceIdType.MESH,
        )

    def y_copy(side, g):
        return pltpu.make_async_remote_copy(
            src_ref=send_y.at[side, g], dst_ref=recv_y.at[side, g],
            send_sem=send_y_sem.at[side, g], recv_sem=recv_y_sem.at[side, g],
            device_id=targets[2 + side], device_id_type=pl.DeviceIdType.MESH,
        )

    def meet():
        @pl.when(first)
        def _():
            pl.semaphore_wait(barrier, 3)

        @pl.when(jnp.logical_not(first))
        def _():
            pl.semaphore_wait(barrier, 4)

        @pl.when(last)
        def _():
            pl.semaphore_signal(last_sem, inc=1, device_id=targets[2], device_id_type=pl.DeviceIdType.MESH)

    def send_x_sums():
        for side in range(2):
            x_copy(side).start()

    def send_y_back(g):
        @pl.when(jnp.logical_not(first))
        def _():
            y_copy(1, g).start()

    def send_rest():
        @pl.when(punctual)
        def _():
            meet()

        @pl.when(jnp.logical_not(late_x))
        def _():
            send_x_sums()

        for g in range(groups):
            @pl.when(jnp.logical_not(late_y))
            def _():
                y_copy(0, g).start()

            send_y_back(g)

    consts[0].wait()

    @pl.loop(0, halves)
    def _(h):
        edge_copy(h, 0).wait()
        edge_copy(h, 1).wait()
        for c in range(3):
            for k in range(half):
                top, bottom = vel[c, h * half + k, :EDGE], vel[c, h * half + k, n - EDGE :]
                for q in range(2):
                    row = (c * 3 + q) * half + k
                    send_x[0, h, row : row + 1] = jnp.sum(edge_x[q] * bottom, axis=0, keepdims=True)
                    send_x[1, h, row : row + 1] = jnp.sum(edge_x[2 + q] * top, axis=0, keepdims=True)
                row = (c * 3 + 2) * half + k
                send_x[0, h, row : row + 1] = bottom[EDGE - 1 :]
                send_x[1, h, row : row + 1] = top[:1]

    @pl.when(late)
    def _():
        meet()

    @pl.when(late_x)
    def _():
        send_x_sums()

    consts[1].wait()

    @pl.loop(0, groups)
    def _(g):
        middle_copy(g).wait()
        for c in range(3):
            for k in range(GROUP):
                values = vel[c, g * GROUP + k]
                high = values.astype(BF16)
                parts[c, g * GROUP + k, :, :n] = high
                parts[c, g * GROUP + k, :, n:] = (values - high.astype(jnp.float32)).astype(BF16)
            for k in range(0, GROUP, 2):
                pair = parts[c, pl.ds(g * GROUP + k, 2)].reshape(2 * n, 2 * n)
                sums = dot_transposed(sums_y[...], pair)
                sums = sums[:8] + sums[8:]
                for j in range(2):
                    for q in range(3):
                        row = (c * 3 + q) * GROUP + k + j
                        send_y[0, g, row : row + 1] = sums[q : q + 1, j * n : (j + 1) * n]
                        send_y[1, g, row : row + 1] = sums[4 + q : 5 + q, j * n : (j + 1) * n]
        for side in range(2):
            send_y[side, g, 9 * GROUP :] = jnp.zeros((4, n), jnp.float32)

        @pl.when(late_y)
        def _():
            y_copy(0, g).start()

    lane = lax.broadcasted_iota(jnp.int32, (n, n), 1)
    consts[4].wait()
    table = jnp.zeros((n, n), jnp.float32)
    for k in range(table_ref.shape[0]):
        table = jnp.where(lane == k, table_ref[k], table)
    consts[2].wait()

    @pl.loop(0, groups)
    def _(g):
        @pl.when(g == sending_step)
        def _():
            send_rest()

        leaf_copy(g).wait()
        for k in range(0, GROUP, 2):
            z = (g * GROUP + k, g * GROUP + k + 1)
            drag = []
            for j in range(2):
                speed = jnp.sqrt(vel[0, z[j]] ** 2 + vel[1, z[j]] ** 2 + vel[2, z[j]] ** 2)
                drag.append(jnp.take_along_axis(table, leaf[z[j]], axis=1) * speed)
            for c in range(3):
                high = jnp.concatenate([parts[c, z[0], :, :n], parts[c, z[1], :, :n]], axis=1)
                low = jnp.concatenate([parts[c, z[0], :, n:], parts[c, z[1], :, n:]], axis=1)
                both = dot(along_x[...], jnp.concatenate([high, low, high], axis=0))
                both = both.reshape(n // 8, 2, 8, 2 * n)
                for j in range(2):
                    gradient = both[:, 0, :, j * n : (j + 1) * n].reshape(n, n)
                    curvature = both[:, 1, :, j * n : (j + 1) * n].reshape(n, n)
                    tend[c, z[j]] = curvature - vel[0, z[j]] * gradient - drag[j] * vel[c, z[j]]

    @pl.when(sending_step == groups)
    def _():
        send_rest()

    consts[3].wait()

    @pl.loop(0, groups)
    def _(g):
        for k in range(GROUP):
            z = g * GROUP + k
            left = [jnp.concatenate([parts[c, z], parts[c, z, :, :n]], axis=1) for c in range(3)]
            both = dot(jnp.concatenate(left, axis=0), along_y[...])
            for c in range(3):
                gradient = both[c * n : (c + 1) * n, :n]
                curvature = both[c * n : (c + 1) * n, n:]
                tend[c, z] += curvature - vel[1, z] * gradient

    consts[5].wait()

    @pl.when(first)
    def _():
        pl.semaphore_wait(last_sem, 1)
        for g in range(groups):
            y_copy(1, g).start()

    for side in range(2):
        for g in range(groups):
            y_copy(side, g).wait_recv()
    for side in range(2):
        x_copy(side).wait_recv()
    for side in range(2):
        x_copy(side).wait_send()
        for g in range(groups):
            y_copy(side, g).wait_send()


def second_kernel(groups, vel, tend, recv_x, recv_y, spread_y, edge_x, out_hbm, result, out_sem):
    n = CELLS
    half = 2 * GROUP
    values = 3 * GROUP

    def out_copy(z):
        return pltpu.make_async_copy(result.at[:, z], out_hbm.at[:, z], out_sem.at[z])

    lane = lax.broadcasted_iota(jnp.int32, (n, 80), 1)
    for g in range(groups):
        spread = []
        for c in range(3):
            got = jnp.concatenate([recv_y[side, g, c * values : (c + 1) * values] for side in range(2)], axis=0)
            high = got.astype(BF16).astype(jnp.float32)
            low = (got - high).astype(BF16).astype(jnp.float32)
            blank = jnp.zeros((8, n), jnp.float32)
            spread.append(jnp.concatenate([high, low, high, blank], axis=0).T.astype(BF16))
        for k in range(GROUP):
            z = g * GROUP + k
            mask = (lane % GROUP) == k
            left = [jnp.where(mask, s, jnp.zeros_like(s)) for s in spread]
            for c in range(3):
                both = dot(left[c], spread_y[...])
                gradient = both[:, :n]
                curvature = both[:, n:]
                values_z = tend[c, z] + curvature - vel[1, z] * gradient
                ends = []
                for side in range(2):
                    h, at = g // 2, c * 3 * half + (g % 2) * GROUP + k
                    s1, s2, s3 = (recv_x[side, h, at + q * half : at + q * half + 1] for q in range(3))
                    gradient = edge_x[4 + 4 * side] * s1 + edge_x[6 + 4 * side] * s3
                    curvature = edge_x[5 + 4 * side] * s2 + edge_x[7 + 4 * side] * s3
                    rows = slice(side * (n - EDGE), side * (n - EDGE) + EDGE)
                    ends.append(values_z[rows] + curvature - vel[0, z, rows] * gradient)
                result[c, z] = jnp.concatenate([ends[0], values_z[EDGE : n - EDGE], ends[1]], axis=0)
            out_copy(z).start()
    for z in range(groups * GROUP):
        out_copy(z).wait()


def in_hbm(array):
    return pltpu.with_memory_space_constraint(array, pltpu.HBM)


def body(velocity, leaf_class, drag_table):
    along_x, along_y, spread_y, sums_y, edge_x = (in_hbm(jnp.asarray(a)) for a in constants())
    velocity, leaf_class, drag_table = in_hbm(velocity), in_hbm(leaf_class), in_hbm(drag_table)
    levels, n = velocity.shape[1], CELLS
    groups = levels // GROUP
    hbm = pl.BlockSpec(memory_space=pltpu.HBM)
    vmem = pl.BlockSpec(memory_space=pltpu.VMEM)
    dma = pltpu.SemaphoreType.DMA
    sums_along_x = (2, groups // 2, 18 * GROUP, n)
    sums_along_y = (2, groups, 10 * GROUP, n)
    held = [
        jax.ShapeDtypeStruct(velocity.shape, jnp.float32),
        jax.ShapeDtypeStruct(velocity.shape, jnp.float32),
        jax.ShapeDtypeStruct(sums_along_x, jnp.float32),
        jax.ShapeDtypeStruct(sums_along_y, jnp.float32),
        jax.ShapeDtypeStruct(spread_y.shape, BF16),
        jax.ShapeDtypeStruct(edge_x.shape, jnp.float32),
    ]
    held = pl.pallas_call(
        functools.partial(first_kernel, groups),
        out_shape=held,
        in_specs=[hbm] * 8,
        out_specs=[vmem] * 6,
        scratch_shapes=[
            pltpu.VMEM((3, levels, n, 2 * n), BF16),
            pltpu.VMEM(leaf_class.shape, jnp.int32),
            pltpu.VMEM(sums_along_x, jnp.float32),
            pltpu.VMEM(sums_along_y, jnp.float32),
            pltpu.VMEM(along_x.shape, BF16),
            pltpu.VMEM(along_y.shape, BF16),
            pltpu.VMEM(sums_y.shape, BF16),
            pltpu.SMEM(drag_table.shape, jnp.float32),
            dma((3, groups)), dma((groups,)), dma((6,)), dma((2,)), dma((2,)), dma((2, groups)), dma((2, groups)),
            pltpu.SemaphoreType.REGULAR,
        ],
        compiler_params=pltpu.CompilerParams(
            collective_id=0, has_side_effects=True, vmem_limit_bytes=40 * 1024 * 1024
        ),
        cost_estimate=pl.CostEstimate(flops=4_000_000_000, bytes_accessed=5_000_000, transcendentals=300_000),
        name="exchange_and_solve",
    )(velocity, leaf_class, drag_table, along_x, along_y, spread_y, sums_y, edge_x)
    return pl.pallas_call(
        functools.partial(second_kernel, groups),
        out_shape=jax.ShapeDtypeStruct(velocity.shape, jnp.float32),
        in_specs=[vmem] * 6,
        out_specs=hbm,
        scratch_shapes=[pltpu.VMEM(velocity.shape, jnp.float32), dma((levels,))],
        compiler_params=pltpu.CompilerParams(vmem_limit_bytes=40 * 1024 * 1024),
        cost_estimate=pl.CostEstimate(flops=1_000_000_000, bytes_accessed=3_000_000, transcendentals=0),
        name="finish",
    )(*held)


def solution(mesh):
    return jax.shard_map(
        body,
        mesh=mesh,
        in_specs=(P(None, None, "gx", "gy"), P(None, "gx", "gy"), P()),
        out_specs=P(None, None, "gx", "gy"),
        check_vma=False,
    )
```

```python
import functools
import math

import jax
import jax.numpy as jnp
import ml_dtypes
import numpy as np
from jax import lax
from jax.experimental import pallas as pl
from jax.experimental.pallas import tpu as pltpu
from jax.sharding import PartitionSpec as P

SPACING = 2.0
CELLS = 128
GROUP = 4
EDGE = 24
BF16 = jnp.bfloat16


def kernel_of(coupling, stencil):
    root = (-1.0 + math.sqrt(1.0 - 4.0 * coupling * coupling)) / (2.0 * coupling)
    scale = 1.0 / math.sqrt(1.0 - 4.0 * coupling * coupling)

    def at(d):
        return sum(w * scale * root ** abs(d - m) for m, w in stencil.items())

    amplitude = at(2) / root**2
    return at, root, amplitude


def operators():
    h = SPACING
    a, b = 14.0 / 9.0 / (2.0 * h), 1.0 / 9.0 / (4.0 * h)
    first = {-1: a, 1: -a, -2: b, 2: -b}
    c, e = 12.0 / 11.0 / (h * h), 3.0 / 11.0 / (4.0 * h * h)
    second = {-1: c, 1: c, -2: e, 2: e, 0: -2.0 * c - 2.0 * e}
    return kernel_of(1.0 / 3.0, first), kernel_of(2.0 / 11.0, second)


def split(values):
    high = np.asarray(values, np.float64).astype(ml_dtypes.bfloat16)
    low = (np.asarray(values, np.float64) - high.astype(np.float64)).astype(ml_dtypes.bfloat16)
    return high, low


def constants():
    (k1, r1, a1), (k2, r2, a2) = operators()
    n = CELLS
    d1 = np.array([[k1(i - j) for j in range(n)] for i in range(n)])
    d2 = np.array([[k2(i - j) for j in range(n)] for i in range(n)])
    rows = np.concatenate([d1.reshape(n // 8, 8, n), d2.reshape(n // 8, 8, n)], axis=1).reshape(2 * n, n)
    high, low = split(rows)
    along_x = np.concatenate([high, high, low], axis=1)
    high, low = split(np.concatenate([d1.T, d2.T], axis=1))
    i = np.arange(n)
    e1, e2 = k1(1) - a1 * r1, k2(1) - a2 * r2
    zero = np.zeros(n)
    first, last = (i == 0) * 1.0, (i == n - 1) * 1.0
    before = np.stack([
        np.concatenate([r1**i, zero]),
        np.concatenate([zero, r2**i]),
        np.concatenate([e1 * first, e2 * first]),
    ])
    after = np.stack([
        np.concatenate([-(r1 ** (n - 1 - i)), zero]),
        np.concatenate([zero, r2 ** (n - 1 - i)]),
        np.concatenate([-e1 * last, e2 * last]),
    ])
    spread = np.repeat(np.concatenate([before, after]), GROUP, axis=0)
    spread_high, spread_low = split(spread)
    blank = np.zeros((8, 2 * n), spread_high.dtype)
    along_y = np.concatenate([high, high, low], axis=0)
    spread_y = np.concatenate([spread_high, spread_high, spread_low, blank], axis=0)
    forward = np.stack([a1 * r1 ** (n - i.astype(float)), a2 * r2 ** (n - i.astype(float)), last, zero])
    backward = np.stack([a1 * r1 ** (1.0 + i), a2 * r2 ** (1.0 + i), first, zero])
    high, low = split(np.concatenate([forward, backward]))
    sums_y = np.concatenate(
        [np.concatenate([high, high], axis=1), np.concatenate([low, np.zeros_like(low)], axis=1)], axis=0
    )
    lanes = np.ones((1, n))
    edge_x = np.stack([
        forward[0, n - EDGE :, None] * lanes,
        forward[1, n - EDGE :, None] * lanes,
        backward[0, :EDGE, None] * lanes,
        backward[1, :EDGE, None] * lanes,
        (r1 ** i[:EDGE])[:, None] * lanes,
        (r2 ** i[:EDGE])[:, None] * lanes,
        (e1 * first)[:EDGE, None] * lanes,
        (e2 * first)[:EDGE, None] * lanes,
        (-(r1 ** (n - 1 - i)))[n - EDGE :, None] * lanes,
        (r2 ** (n - 1 - i))[n - EDGE :, None] * lanes,
        (-e1 * last)[n - EDGE :, None] * lanes,
        (e2 * last)[n - EDGE :, None] * lanes,
    ]).astype(np.float32)
    return along_x, along_y, spread_y, sums_y, edge_x


def dot(a, b):
    return lax.dot_general(a, b, (((1,), (0,)), ((), ())), preferred_element_type=jnp.float32)


def dot_transposed(a, b):
    return lax.dot_general(a, b, (((1,), (1,)), ((), ())), preferred_element_type=jnp.float32)


def first_kernel(
    groups, vel_hbm, leaf_hbm, table_hbm, along_x_hbm, along_y_hbm, spread_y_hbm, sums_y_hbm, edge_x_hbm,
    vel, tend, recv_x, recv_y, spread_y, edge_x,
    parts, leaf, send_x, send_y, along_x, along_y, sums_y, table_ref,
    vel_sem, leaf_sem, const_sem, send_sem, recv_sem, send_y_sem, recv_y_sem, last_sem,
):
    n = CELLS
    half = 2 * GROUP
    halves = groups // 2

    consts = [
        pltpu.make_async_copy(a, b, const_sem.at[i])
        for i, (a, b) in enumerate(
            [(edge_x_hbm, edge_x), (sums_y_hbm, sums_y), (along_x_hbm, along_x), (along_y_hbm, along_y),
             (table_hbm, table_ref), (spread_y_hbm, spread_y)]
        )
    ]

    def levels(g):
        return pl.ds(g * GROUP, GROUP)

    def edge_copy(h, side):
        at = (slice(None), pl.ds(h * half, half), pl.ds(side * (n - EDGE), EDGE))
        return pltpu.make_async_copy(vel_hbm.at[at], vel.at[at], vel_sem.at[side, h])

    def middle_copy(g):
        at = (slice(None), levels(g), pl.ds(EDGE, n - 2 * EDGE))
        return pltpu.make_async_copy(vel_hbm.at[at], vel.at[at], vel_sem.at[2, g])

    def leaf_copy(g):
        return pltpu.make_async_copy(leaf_hbm.at[levels(g)], leaf.at[levels(g)], leaf_sem.at[g])

    mx, my = lax.axis_index("gx"), lax.axis_index("gy")
    nx, ny = lax.axis_size("gx"), lax.axis_size("gy")
    targets = [
        {"gx": lax.rem(mx + 1, nx)},
        {"gx": lax.rem(mx + nx - 1, nx)},
        {"gy": lax.rem(my + 1, ny)},
        {"gy": lax.rem(my + ny - 1, ny)},
    ]
    first, last = my == 0, my == ny - 1
    told = mx == nx // 2
    deferred = jnp.logical_and(first, jnp.logical_not(told))
    barrier = pltpu.get_barrier_semaphore()
    for target in (targets[0], targets[1], targets[3]):
        pl.semaphore_signal(barrier, inc=1, device_id=target, device_id_type=pl.DeviceIdType.MESH)

    @pl.when(jnp.logical_or(jnp.logical_not(last), told))
    def _():
        pl.semaphore_signal(barrier, inc=1, device_id=targets[2], device_id_type=pl.DeviceIdType.MESH)

    consts[0].start()
    for h in range(halves):
        for side in range(2):
            edge_copy(h, side).start()
    consts[1].start()
    for g in range(groups):
        middle_copy(g).start()
    consts[4].start()
    consts[2].start()
    for g in range(groups):
        leaf_copy(g).start()
    consts[3].start()
    consts[5].start()

    late_x = mx == nx - 1
    late_y = jnp.logical_and(last, mx != 0)
    late = jnp.logical_or(late_x, late_y)
    punctual = jnp.logical_not(late)
    slow = jnp.logical_or(jnp.logical_and(mx == 0, jnp.logical_not(last)), jnp.logical_and(first, told))
    sending_step = jnp.where(slow, groups, groups // 2)

    def x_copy(side):
        return pltpu.make_async_remote_copy(
            src_ref=send_x.at[side], dst_ref=recv_x.at[side],
            send_sem=send_sem.at[side], recv_sem=recv_sem.at[side],
            device_id=targets[side], device_id_type=pl.DeviceIdType.MESH,
        )

    def y_copy(side, g):
        return pltpu.make_async_remote_copy(
            src_ref=send_y.at[side, g], dst_ref=recv_y.at[side, g],
            send_sem=send_y_sem.at[side, g], recv_sem=recv_y_sem.at[side, g],
            device_id=targets[2 + side], device_id_type=pl.DeviceIdType.MESH,
        )

    def meet():
        @pl.when(deferred)
        def _():
            pl.semaphore_wait(barrier, 3)

        @pl.when(jnp.logical_not(deferred))
        def _():
            pl.semaphore_wait(barrier, 4)

        @pl.when(jnp.logical_and(last, jnp.logical_not(told)))
        def _():
            pl.semaphore_signal(last_sem, inc=1, device_id=targets[2], device_id_type=pl.DeviceIdType.MESH)

    def send_x_sums():
        for side in range(2):
            x_copy(side).start()

    def send_y_back(g):
        @pl.when(jnp.logical_not(deferred))
        def _():
            y_copy(1, g).start()

    def send_rest():
        @pl.when(punctual)
        def _():
            meet()

        @pl.when(jnp.logical_not(jnp.logical_or(late_x, mx == 0)))
        def _():
            send_x_sums()

        for g in range(groups):
            @pl.when(jnp.logical_not(late_y))
            def _():
                y_copy(0, g).start()

            send_y_back(g)

        @pl.when(mx == 0)
        def _():
            send_x_sums()

    consts[0].wait()

    @pl.loop(0, halves)
    def _(h):
        edge_copy(h, 0).wait()
        edge_copy(h, 1).wait()
        for c in range(3):
            for k in range(half):
                top, bottom = vel[c, h * half + k, :EDGE], vel[c, h * half + k, n - EDGE :]
                for q in range(2):
                    row = (c * 3 + q) * half + k
                    send_x[0, h, row : row + 1] = jnp.sum(edge_x[q] * bottom, axis=0, keepdims=True)
                    send_x[1, h, row : row + 1] = jnp.sum(edge_x[2 + q] * top, axis=0, keepdims=True)
                row = (c * 3 + 2) * half + k
                send_x[0, h, row : row + 1] = bottom[EDGE - 1 :]
                send_x[1, h, row : row + 1] = top[:1]

    @pl.when(late_x)
    def _():
        meet()
        send_x_sums()

    consts[1].wait()

    @pl.loop(0, groups)
    def _(g):
        middle_copy(g).wait()
        for c in range(3):
            for k in range(GROUP):
                values = vel[c, g * GROUP + k]
                high = values.astype(BF16)
                parts[c, g * GROUP + k, :, :n] = high
                parts[c, g * GROUP + k, :, n:] = (values - high.astype(jnp.float32)).astype(BF16)
            for k in range(0, GROUP, 2):
                pair = parts[c, pl.ds(g * GROUP + k, 2)].reshape(2 * n, 2 * n)
                sums = dot_transposed(sums_y[...], pair)
                sums = sums[:8] + sums[8:]
                for j in range(2):
                    for q in range(3):
                        row = (c * 3 + q) * GROUP + k + j
                        send_y[0, g, row : row + 1] = sums[q : q + 1, j * n : (j + 1) * n]
                        send_y[1, g, row : row + 1] = sums[4 + q : 5 + q, j * n : (j + 1) * n]
        for side in range(2):
            send_y[side, g, 9 * GROUP :] = jnp.zeros((4, n), jnp.float32)

    @pl.when(jnp.logical_and(late_y, jnp.logical_not(late_x)))
    def _():
        meet()

    @pl.when(late_y)
    def _():
        for g in range(groups):
            y_copy(0, g).start()

    lane = lax.broadcasted_iota(jnp.int32, (n, n), 1)
    consts[4].wait()
    table = jnp.zeros((n, n), jnp.float32)
    for k in range(table_ref.shape[0]):
        table = jnp.where(lane == k, table_ref[k], table)
    consts[2].wait()

    @pl.loop(0, groups)
    def _(g):
        @pl.when(g == sending_step)
        def _():
            send_rest()

        leaf_copy(g).wait()
        for k in range(0, GROUP, 2):
            z = (g * GROUP + k, g * GROUP + k + 1)
            drag = []
            for j in range(2):
                speed = jnp.sqrt(vel[0, z[j]] ** 2 + vel[1, z[j]] ** 2 + vel[2, z[j]] ** 2)
                drag.append(jnp.take_along_axis(table, leaf[z[j]], axis=1) * speed)
            for c in range(3):
                high = jnp.concatenate([parts[c, z[0], :, :n], parts[c, z[1], :, :n]], axis=1)
                low = jnp.concatenate([parts[c, z[0], :, n:], parts[c, z[1], :, n:]], axis=1)
                both = dot(along_x[...], jnp.concatenate([high, low, high], axis=0))
                both = both.reshape(n // 8, 2, 8, 2 * n)
                for j in range(2):
                    gradient = both[:, 0, :, j * n : (j + 1) * n].reshape(n, n)
                    curvature = both[:, 1, :, j * n : (j + 1) * n].reshape(n, n)
                    tend[c, z[j]] = curvature - vel[0, z[j]] * gradient - drag[j] * vel[c, z[j]]

    @pl.when(sending_step == groups)
    def _():
        send_rest()

    consts[3].wait()

    @pl.loop(0, groups)
    def _(g):
        for k in range(GROUP):
            z = g * GROUP + k
            left = [jnp.concatenate([parts[c, z], parts[c, z, :, :n]], axis=1) for c in range(3)]
            both = dot(jnp.concatenate(left, axis=0), along_y[...])
            for c in range(3):
                gradient = both[c * n : (c + 1) * n, :n]
                curvature = both[c * n : (c + 1) * n, n:]
                tend[c, z] += curvature - vel[1, z] * gradient

    consts[5].wait()

    @pl.when(deferred)
    def _():
        pl.semaphore_wait(last_sem, 1)
        for g in range(groups):
            y_copy(1, g).start()

    for side in range(2):
        for g in range(groups):
            y_copy(side, g).wait_recv()
    for side in range(2):
        x_copy(side).wait_recv()
    for side in range(2):
        x_copy(side).wait_send()
        for g in range(groups):
            y_copy(side, g).wait_send()


def second_kernel(groups, vel, tend, recv_x, recv_y, spread_y, edge_x, out_hbm, result, out_sem):
    n = CELLS
    half = 2 * GROUP
    values = 3 * GROUP

    def out_copy(z):
        return pltpu.make_async_copy(result.at[:, z], out_hbm.at[:, z], out_sem.at[z])

    lane = lax.broadcasted_iota(jnp.int32, (n, 80), 1)
    for g in range(groups):
        spread = []
        for c in range(3):
            got = jnp.concatenate([recv_y[side, g, c * values : (c + 1) * values] for side in range(2)], axis=0)
            high = got.astype(BF16).astype(jnp.float32)
            low = (got - high).astype(BF16).astype(jnp.float32)
            blank = jnp.zeros((8, n), jnp.float32)
            spread.append(jnp.concatenate([high, low, high, blank], axis=0).T.astype(BF16))
        for k in range(GROUP):
            z = g * GROUP + k
            mask = (lane % GROUP) == k
            left = [jnp.where(mask, s, jnp.zeros_like(s)) for s in spread]
            for c in range(3):
                both = dot(left[c], spread_y[...])
                gradient = both[:, :n]
                curvature = both[:, n:]
                values_z = tend[c, z] + curvature - vel[1, z] * gradient
                ends = []
                for side in range(2):
                    h, at = g // 2, c * 3 * half + (g % 2) * GROUP + k
                    s1, s2, s3 = (recv_x[side, h, at + q * half : at + q * half + 1] for q in range(3))
                    gradient = edge_x[4 + 4 * side] * s1 + edge_x[6 + 4 * side] * s3
                    curvature = edge_x[5 + 4 * side] * s2 + edge_x[7 + 4 * side] * s3
                    rows = slice(side * (n - EDGE), side * (n - EDGE) + EDGE)
                    ends.append(values_z[rows] + curvature - vel[0, z, rows] * gradient)
                result[c, z] = jnp.concatenate([ends[0], values_z[EDGE : n - EDGE], ends[1]], axis=0)
            out_copy(z).start()
    for z in range(groups * GROUP):
        out_copy(z).wait()


def in_hbm(array):
    return pltpu.with_memory_space_constraint(array, pltpu.HBM)


def body(velocity, leaf_class, drag_table):
    along_x, along_y, spread_y, sums_y, edge_x = (in_hbm(jnp.asarray(a)) for a in constants())
    velocity, leaf_class, drag_table = in_hbm(velocity), in_hbm(leaf_class), in_hbm(drag_table)
    levels, n = velocity.shape[1], CELLS
    groups = levels // GROUP
    hbm = pl.BlockSpec(memory_space=pltpu.HBM)
    vmem = pl.BlockSpec(memory_space=pltpu.VMEM)
    dma = pltpu.SemaphoreType.DMA
    sums_along_x = (2, groups // 2, 18 * GROUP, n)
    sums_along_y = (2, groups, 10 * GROUP, n)
    held = [
        jax.ShapeDtypeStruct(velocity.shape, jnp.float32),
        jax.ShapeDtypeStruct(velocity.shape, jnp.float32),
        jax.ShapeDtypeStruct(sums_along_x, jnp.float32),
        jax.ShapeDtypeStruct(sums_along_y, jnp.float32),
        jax.ShapeDtypeStruct(spread_y.shape, BF16),
        jax.ShapeDtypeStruct(edge_x.shape, jnp.float32),
    ]
    held = pl.pallas_call(
        functools.partial(first_kernel, groups),
        out_shape=held,
        in_specs=[hbm] * 8,
        out_specs=[vmem] * 6,
        scratch_shapes=[
            pltpu.VMEM((3, levels, n, 2 * n), BF16),
            pltpu.VMEM(leaf_class.shape, jnp.int32),
            pltpu.VMEM(sums_along_x, jnp.float32),
            pltpu.VMEM(sums_along_y, jnp.float32),
            pltpu.VMEM(along_x.shape, BF16),
            pltpu.VMEM(along_y.shape, BF16),
            pltpu.VMEM(sums_y.shape, BF16),
            pltpu.SMEM(drag_table.shape, jnp.float32),
            dma((3, groups)), dma((groups,)), dma((6,)), dma((2,)), dma((2,)), dma((2, groups)), dma((2, groups)),
            pltpu.SemaphoreType.REGULAR,
        ],
        compiler_params=pltpu.CompilerParams(
            collective_id=0, has_side_effects=True, vmem_limit_bytes=40 * 1024 * 1024
        ),
        cost_estimate=pl.CostEstimate(flops=4_000_000_000, bytes_accessed=5_000_000, transcendentals=300_000),
        name="exchange_and_solve",
    )(velocity, leaf_class, drag_table, along_x, along_y, spread_y, sums_y, edge_x)
    return pl.pallas_call(
        functools.partial(second_kernel, groups),
        out_shape=jax.ShapeDtypeStruct(velocity.shape, jnp.float32),
        in_specs=[vmem] * 6,
        out_specs=hbm,
        scratch_shapes=[pltpu.VMEM(velocity.shape, jnp.float32), dma((levels,))],
        compiler_params=pltpu.CompilerParams(vmem_limit_bytes=40 * 1024 * 1024),
        cost_estimate=pl.CostEstimate(flops=1_000_000_000, bytes_accessed=3_000_000, transcendentals=0),
        name="finish",
    )(*held)


def solution(mesh):
    return jax.shard_map(
        body,
        mesh=mesh,
        in_specs=(P(None, None, "gx", "gy"), P(None, "gx", "gy"), P()),
        out_specs=P(None, None, "gx", "gy"),
        check_vma=False,
    )
```

```python
import functools
import math

import jax
import jax.numpy as jnp
import ml_dtypes
import numpy as np
from jax import lax
from jax.experimental import pallas as pl
from jax.experimental.pallas import tpu as pltpu
from jax.sharding import PartitionSpec as P

SPACING = 2.0
CELLS = 128
GROUP = 4
EDGE = 24
BF16 = jnp.bfloat16


def kernel_of(coupling, stencil):
    root = (-1.0 + math.sqrt(1.0 - 4.0 * coupling * coupling)) / (2.0 * coupling)
    scale = 1.0 / math.sqrt(1.0 - 4.0 * coupling * coupling)

    def at(d):
        return sum(w * scale * root ** abs(d - m) for m, w in stencil.items())

    amplitude = at(2) / root**2
    return at, root, amplitude


def operators():
    h = SPACING
    a, b = 14.0 / 9.0 / (2.0 * h), 1.0 / 9.0 / (4.0 * h)
    first = {-1: a, 1: -a, -2: b, 2: -b}
    c, e = 12.0 / 11.0 / (h * h), 3.0 / 11.0 / (4.0 * h * h)
    second = {-1: c, 1: c, -2: e, 2: e, 0: -2.0 * c - 2.0 * e}
    return kernel_of(1.0 / 3.0, first), kernel_of(2.0 / 11.0, second)


def split(values):
    high = np.asarray(values, np.float64).astype(ml_dtypes.bfloat16)
    low = (np.asarray(values, np.float64) - high.astype(np.float64)).astype(ml_dtypes.bfloat16)
    return high, low


def constants():
    (k1, r1, a1), (k2, r2, a2) = operators()
    n = CELLS
    d1 = np.array([[k1(i - j) for j in range(n)] for i in range(n)])
    d2 = np.array([[k2(i - j) for j in range(n)] for i in range(n)])
    rows = np.concatenate([d1.reshape(n // 8, 8, n), d2.reshape(n // 8, 8, n)], axis=1).reshape(2 * n, n)
    high, low = split(rows)
    along_x = np.concatenate([high, high, low], axis=1)
    high, low = split(np.concatenate([d1.T, d2.T], axis=1))
    i = np.arange(n)
    e1, e2 = k1(1) - a1 * r1, k2(1) - a2 * r2
    zero = np.zeros(n)
    first, last = (i == 0) * 1.0, (i == n - 1) * 1.0
    before = np.stack([
        np.concatenate([r1**i, zero]),
        np.concatenate([zero, r2**i]),
        np.concatenate([e1 * first, e2 * first]),
    ])
    after = np.stack([
        np.concatenate([-(r1 ** (n - 1 - i)), zero]),
        np.concatenate([zero, r2 ** (n - 1 - i)]),
        np.concatenate([-e1 * last, e2 * last]),
    ])
    spread = np.repeat(np.concatenate([before, after]), GROUP, axis=0)
    spread_high, spread_low = split(spread)
    blank = np.zeros((8, 2 * n), spread_high.dtype)
    along_y = np.concatenate([high, high, low], axis=0)
    spread_y = np.concatenate([spread_high, spread_high, spread_low, blank], axis=0)
    forward = np.stack([a1 * r1 ** (n - i.astype(float)), a2 * r2 ** (n - i.astype(float)), last, zero])
    backward = np.stack([a1 * r1 ** (1.0 + i), a2 * r2 ** (1.0 + i), first, zero])
    high, low = split(np.concatenate([forward, backward]))
    sums_y = np.concatenate(
        [np.concatenate([high, high], axis=1), np.concatenate([low, np.zeros_like(low)], axis=1)], axis=0
    )
    lanes = np.ones((1, n))
    edge_x = np.stack([
        forward[0, n - EDGE :, None] * lanes,
        forward[1, n - EDGE :, None] * lanes,
        backward[0, :EDGE, None] * lanes,
        backward[1, :EDGE, None] * lanes,
        (r1 ** i[:EDGE])[:, None] * lanes,
        (r2 ** i[:EDGE])[:, None] * lanes,
        (e1 * first)[:EDGE, None] * lanes,
        (e2 * first)[:EDGE, None] * lanes,
        (-(r1 ** (n - 1 - i)))[n - EDGE :, None] * lanes,
        (r2 ** (n - 1 - i))[n - EDGE :, None] * lanes,
        (-e1 * last)[n - EDGE :, None] * lanes,
        (e2 * last)[n - EDGE :, None] * lanes,
    ]).astype(np.float32)
    return along_x, along_y, spread_y, sums_y, edge_x


def dot(a, b):
    return lax.dot_general(a, b, (((1,), (0,)), ((), ())), preferred_element_type=jnp.float32)


def dot_transposed(a, b):
    return lax.dot_general(a, b, (((1,), (1,)), ((), ())), preferred_element_type=jnp.float32)


def first_kernel(
    groups, vel_hbm, leaf_hbm, table_hbm, along_x_hbm, along_y_hbm, spread_y_hbm, sums_y_hbm, edge_x_hbm,
    vel, tend, recv_x, recv_y, spread_y, edge_x,
    parts, leaf, send_x, send_y, along_x, along_y, sums_y, table_ref,
    vel_sem, leaf_sem, const_sem, send_sem, recv_sem, send_y_sem, recv_y_sem, last_sem,
):
    n = CELLS
    half = 2 * GROUP
    halves = groups // 2

    consts = [
        pltpu.make_async_copy(a, b, const_sem.at[i])
        for i, (a, b) in enumerate(
            [(edge_x_hbm, edge_x), (sums_y_hbm, sums_y), (along_x_hbm, along_x), (along_y_hbm, along_y),
             (table_hbm, table_ref), (spread_y_hbm, spread_y)]
        )
    ]

    def levels(g):
        return pl.ds(g * GROUP, GROUP)

    def edge_copy(h, side):
        at = (slice(None), pl.ds(h * half, half), pl.ds(side * (n - EDGE), EDGE))
        return pltpu.make_async_copy(vel_hbm.at[at], vel.at[at], vel_sem.at[side, h])

    def middle_copy(g):
        at = (slice(None), levels(g), pl.ds(EDGE, n - 2 * EDGE))
        return pltpu.make_async_copy(vel_hbm.at[at], vel.at[at], vel_sem.at[2, g])

    def leaf_copy(g):
        return pltpu.make_async_copy(leaf_hbm.at[levels(g)], leaf.at[levels(g)], leaf_sem.at[g])

    mx, my = lax.axis_index("gx"), lax.axis_index("gy")
    nx, ny = lax.axis_size("gx"), lax.axis_size("gy")
    targets = [
        {"gx": lax.rem(mx + 1, nx)},
        {"gx": lax.rem(mx + nx - 1, nx)},
        {"gy": lax.rem(my + 1, ny)},
        {"gy": lax.rem(my + ny - 1, ny)},
    ]
    first, last = my == 0, my == ny - 1
    told = jnp.logical_or(mx == nx // 2, mx == nx // 2 - 1)
    untold = jnp.logical_not(told)
    deferred = jnp.logical_and(first, jnp.logical_not(told))
    barrier = pltpu.get_barrier_semaphore()
    for target in (targets[0], targets[1], targets[3]):
        pl.semaphore_signal(barrier, inc=1, device_id=target, device_id_type=pl.DeviceIdType.MESH)

    @pl.when(jnp.logical_or(jnp.logical_not(last), told))
    def _():
        pl.semaphore_signal(barrier, inc=1, device_id=targets[2], device_id_type=pl.DeviceIdType.MESH)

    consts[0].start()
    for h in range(halves):
        for side in range(2):
            edge_copy(h, side).start()
    consts[1].start()
    for g in range(groups):
        middle_copy(g).start()
    consts[4].start()
    consts[2].start()
    for g in range(groups):
        leaf_copy(g).start()
    consts[3].start()
    consts[5].start()

    late_x = mx == nx - 1
    late_y = jnp.logical_and(last, mx != 0)
    late = jnp.logical_or(late_x, late_y)
    punctual = jnp.logical_not(late)
    slow = jnp.logical_or(jnp.logical_and(mx == 0, jnp.logical_not(last)), jnp.logical_and(first, told))
    sending_step = jnp.where(slow, groups, groups // 2)

    def x_copy(side):
        return pltpu.make_async_remote_copy(
            src_ref=send_x.at[side], dst_ref=recv_x.at[side],
            send_sem=send_sem.at[side], recv_sem=recv_sem.at[side],
            device_id=targets[side], device_id_type=pl.DeviceIdType.MESH,
        )

    def y_copy(side, g):
        return pltpu.make_async_remote_copy(
            src_ref=send_y.at[side, g], dst_ref=recv_y.at[side, g],
            send_sem=send_y_sem.at[side, g], recv_sem=recv_y_sem.at[side, g],
            device_id=targets[2 + side], device_id_type=pl.DeviceIdType.MESH,
        )

    def meet():
        @pl.when(deferred)
        def _():
            pl.semaphore_wait(barrier, 3)

        @pl.when(jnp.logical_not(deferred))
        def _():
            pl.semaphore_wait(barrier, 4)

        @pl.when(jnp.logical_and(last, jnp.logical_not(told)))
        def _():
            pl.semaphore_signal(last_sem, inc=1, device_id=targets[2], device_id_type=pl.DeviceIdType.MESH)

    def send_x_sums():
        for side in range(2):
            x_copy(side).start()

    def send_y_back(g):
        @pl.when(jnp.logical_not(deferred))
        def _():
            y_copy(1, g).start()

    def send_rest():
        @pl.when(punctual)
        def _():
            meet()

        @pl.when(jnp.logical_not(jnp.logical_or(late_x, mx == 0)))
        def _():
            send_x_sums()

        @pl.when(late_x)
        def _():
            x_copy(1).start()

        for g in range(groups):
            @pl.when(jnp.logical_not(late_y))
            def _():
                y_copy(0, g).start()

            send_y_back(g)

        @pl.when(mx == 0)
        def _():
            send_x_sums()

    consts[0].wait()

    @pl.loop(0, halves)
    def _(h):
        edge_copy(h, 0).wait()
        edge_copy(h, 1).wait()
        for c in range(3):
            for k in range(half):
                top, bottom = vel[c, h * half + k, :EDGE], vel[c, h * half + k, n - EDGE :]
                for q in range(2):
                    row = (c * 3 + q) * half + k
                    send_x[0, h, row : row + 1] = jnp.sum(edge_x[q] * bottom, axis=0, keepdims=True)
                    send_x[1, h, row : row + 1] = jnp.sum(edge_x[2 + q] * top, axis=0, keepdims=True)
                row = (c * 3 + 2) * half + k
                send_x[0, h, row : row + 1] = bottom[EDGE - 1 :]
                send_x[1, h, row : row + 1] = top[:1]

    @pl.when(jnp.logical_or(late_x, jnp.logical_and(late_y, untold)))
    def _():
        meet()

    @pl.when(late_x)
    def _():
        x_copy(0).start()

    consts[1].wait()

    @pl.loop(0, groups)
    def _(g):
        middle_copy(g).wait()
        for c in range(3):
            for k in range(GROUP):
                values = vel[c, g * GROUP + k]
                high = values.astype(BF16)
                parts[c, g * GROUP + k, :, :n] = high
                parts[c, g * GROUP + k, :, n:] = (values - high.astype(jnp.float32)).astype(BF16)
            for k in range(0, GROUP, 2):
                pair = parts[c, pl.ds(g * GROUP + k, 2)].reshape(2 * n, 2 * n)
                sums = dot_transposed(sums_y[...], pair)
                sums = sums[:8] + sums[8:]
                for j in range(2):
                    for q in range(3):
                        row = (c * 3 + q) * GROUP + k + j
                        send_y[0, g, row : row + 1] = sums[q : q + 1, j * n : (j + 1) * n]
                        send_y[1, g, row : row + 1] = sums[4 + q : 5 + q, j * n : (j + 1) * n]
        for side in range(2):
            send_y[side, g, 9 * GROUP :] = jnp.zeros((4, n), jnp.float32)

        @pl.when(jnp.logical_and(late_y, jnp.logical_or(late_x, untold)))
        def _():
            y_copy(0, g).start()

    @pl.when(jnp.logical_and(jnp.logical_and(late_y, told), jnp.logical_not(late_x)))
    def _():
        meet()
        for g in range(groups):
            y_copy(0, g).start()

    lane = lax.broadcasted_iota(jnp.int32, (n, n), 1)
    consts[4].wait()
    table = jnp.zeros((n, n), jnp.float32)
    for k in range(table_ref.shape[0]):
        table = jnp.where(lane == k, table_ref[k], table)
    consts[2].wait()

    @pl.loop(0, groups)
    def _(g):
        @pl.when(g == sending_step)
        def _():
            send_rest()

        leaf_copy(g).wait()
        for k in range(0, GROUP, 2):
            z = (g * GROUP + k, g * GROUP + k + 1)
            drag = []
            for j in range(2):
                speed = jnp.sqrt(vel[0, z[j]] ** 2 + vel[1, z[j]] ** 2 + vel[2, z[j]] ** 2)
                drag.append(jnp.take_along_axis(table, leaf[z[j]], axis=1) * speed)
            for c in range(3):
                high = jnp.concatenate([parts[c, z[0], :, :n], parts[c, z[1], :, :n]], axis=1)
                low = jnp.concatenate([parts[c, z[0], :, n:], parts[c, z[1], :, n:]], axis=1)
                both = dot(along_x[...], jnp.concatenate([high, low, high], axis=0))
                both = both.reshape(n // 8, 2, 8, 2 * n)
                for j in range(2):
                    gradient = both[:, 0, :, j * n : (j + 1) * n].reshape(n, n)
                    curvature = both[:, 1, :, j * n : (j + 1) * n].reshape(n, n)
                    tend[c, z[j]] = curvature - vel[0, z[j]] * gradient - drag[j] * vel[c, z[j]]

    @pl.when(sending_step == groups)
    def _():
        send_rest()

    consts[3].wait()

    @pl.loop(0, groups)
    def _(g):
        for k in range(GROUP):
            z = g * GROUP + k
            left = [jnp.concatenate([parts[c, z], parts[c, z, :, :n]], axis=1) for c in range(3)]
            both = dot(jnp.concatenate(left, axis=0), along_y[...])
            for c in range(3):
                gradient = both[c * n : (c + 1) * n, :n]
                curvature = both[c * n : (c + 1) * n, n:]
                tend[c, z] += curvature - vel[1, z] * gradient

    consts[5].wait()

    @pl.when(deferred)
    def _():
        pl.semaphore_wait(last_sem, 1)
        for g in range(groups):
            y_copy(1, g).start()

    for side in range(2):
        for g in range(groups):
            y_copy(side, g).wait_recv()
    for side in range(2):
        x_copy(side).wait_recv()
    for side in range(2):
        x_copy(side).wait_send()
        for g in range(groups):
            y_copy(side, g).wait_send()


def second_kernel(groups, vel, tend, recv_x, recv_y, spread_y, edge_x, out_hbm, result, out_sem):
    n = CELLS
    half = 2 * GROUP
    values = 3 * GROUP

    def out_copy(z):
        return pltpu.make_async_copy(result.at[:, z], out_hbm.at[:, z], out_sem.at[z])

    lane = lax.broadcasted_iota(jnp.int32, (n, 80), 1)
    for g in range(groups):
        spread = []
        for c in range(3):
            got = jnp.concatenate([recv_y[side, g, c * values : (c + 1) * values] for side in range(2)], axis=0)
            high = got.astype(BF16).astype(jnp.float32)
            low = (got - high).astype(BF16).astype(jnp.float32)
            blank = jnp.zeros((8, n), jnp.float32)
            spread.append(jnp.concatenate([high, low, high, blank], axis=0).T.astype(BF16))
        for k in range(GROUP):
            z = g * GROUP + k
            mask = (lane % GROUP) == k
            left = [jnp.where(mask, s, jnp.zeros_like(s)) for s in spread]
            for c in range(3):
                both = dot(left[c], spread_y[...])
                gradient = both[:, :n]
                curvature = both[:, n:]
                values_z = tend[c, z] + curvature - vel[1, z] * gradient
                ends = []
                for side in range(2):
                    h, at = g // 2, c * 3 * half + (g % 2) * GROUP + k
                    s1, s2, s3 = (recv_x[side, h, at + q * half : at + q * half + 1] for q in range(3))
                    gradient = edge_x[4 + 4 * side] * s1 + edge_x[6 + 4 * side] * s3
                    curvature = edge_x[5 + 4 * side] * s2 + edge_x[7 + 4 * side] * s3
                    rows = slice(side * (n - EDGE), side * (n - EDGE) + EDGE)
                    ends.append(values_z[rows] + curvature - vel[0, z, rows] * gradient)
                result[c, z] = jnp.concatenate([ends[0], values_z[EDGE : n - EDGE], ends[1]], axis=0)
            out_copy(z).start()
    for z in range(groups * GROUP):
        out_copy(z).wait()


def in_hbm(array):
    return pltpu.with_memory_space_constraint(array, pltpu.HBM)


def body(velocity, leaf_class, drag_table):
    along_x, along_y, spread_y, sums_y, edge_x = (in_hbm(jnp.asarray(a)) for a in constants())
    velocity, leaf_class, drag_table = in_hbm(velocity), in_hbm(leaf_class), in_hbm(drag_table)
    levels, n = velocity.shape[1], CELLS
    groups = levels // GROUP
    hbm = pl.BlockSpec(memory_space=pltpu.HBM)
    vmem = pl.BlockSpec(memory_space=pltpu.VMEM)
    dma = pltpu.SemaphoreType.DMA
    sums_along_x = (2, groups // 2, 18 * GROUP, n)
    sums_along_y = (2, groups, 10 * GROUP, n)
    held = [
        jax.ShapeDtypeStruct(velocity.shape, jnp.float32),
        jax.ShapeDtypeStruct(velocity.shape, jnp.float32),
        jax.ShapeDtypeStruct(sums_along_x, jnp.float32),
        jax.ShapeDtypeStruct(sums_along_y, jnp.float32),
        jax.ShapeDtypeStruct(spread_y.shape, BF16),
        jax.ShapeDtypeStruct(edge_x.shape, jnp.float32),
    ]
    held = pl.pallas_call(
        functools.partial(first_kernel, groups),
        out_shape=held,
        in_specs=[hbm] * 8,
        out_specs=[vmem] * 6,
        scratch_shapes=[
            pltpu.VMEM((3, levels, n, 2 * n), BF16),
            pltpu.VMEM(leaf_class.shape, jnp.int32),
            pltpu.VMEM(sums_along_x, jnp.float32),
            pltpu.VMEM(sums_along_y, jnp.float32),
            pltpu.VMEM(along_x.shape, BF16),
            pltpu.VMEM(along_y.shape, BF16),
            pltpu.VMEM(sums_y.shape, BF16),
            pltpu.SMEM(drag_table.shape, jnp.float32),
            dma((3, groups)), dma((groups,)), dma((6,)), dma((2,)), dma((2,)), dma((2, groups)), dma((2, groups)),
            pltpu.SemaphoreType.REGULAR,
        ],
        compiler_params=pltpu.CompilerParams(
            collective_id=0, has_side_effects=True, vmem_limit_bytes=40 * 1024 * 1024
        ),
        cost_estimate=pl.CostEstimate(flops=4_000_000_000, bytes_accessed=5_000_000, transcendentals=300_000),
        name="exchange_and_solve",
    )(velocity, leaf_class, drag_table, along_x, along_y, spread_y, sums_y, edge_x)
    return pl.pallas_call(
        functools.partial(second_kernel, groups),
        out_shape=jax.ShapeDtypeStruct(velocity.shape, jnp.float32),
        in_specs=[vmem] * 6,
        out_specs=hbm,
        scratch_shapes=[pltpu.VMEM(velocity.shape, jnp.float32), dma((levels,))],
        compiler_params=pltpu.CompilerParams(vmem_limit_bytes=40 * 1024 * 1024),
        cost_estimate=pl.CostEstimate(flops=1_000_000_000, bytes_accessed=3_000_000, transcendentals=0),
        name="finish",
    )(*held)


def solution(mesh):
    return jax.shard_map(
        body,
        mesh=mesh,
        in_specs=(P(None, None, "gx", "gy"), P(None, "gx", "gy"), P()),
        out_specs=P(None, None, "gx", "gy"),
        check_vma=False,
    )
```

```python
import functools
import math

import jax
import jax.numpy as jnp
import ml_dtypes
import numpy as np
from jax import lax
from jax.experimental import pallas as pl
from jax.experimental.pallas import tpu as pltpu
from jax.sharding import PartitionSpec as P

SPACING = 2.0
CELLS = 128
GROUP = 4
EDGE = 24
BF16 = jnp.bfloat16


def kernel_of(coupling, stencil):
    root = (-1.0 + math.sqrt(1.0 - 4.0 * coupling * coupling)) / (2.0 * coupling)
    scale = 1.0 / math.sqrt(1.0 - 4.0 * coupling * coupling)

    def at(d):
        return sum(w * scale * root ** abs(d - m) for m, w in stencil.items())

    amplitude = at(2) / root**2
    return at, root, amplitude


def operators():
    h = SPACING
    a, b = 14.0 / 9.0 / (2.0 * h), 1.0 / 9.0 / (4.0 * h)
    first = {-1: a, 1: -a, -2: b, 2: -b}
    c, e = 12.0 / 11.0 / (h * h), 3.0 / 11.0 / (4.0 * h * h)
    second = {-1: c, 1: c, -2: e, 2: e, 0: -2.0 * c - 2.0 * e}
    return kernel_of(1.0 / 3.0, first), kernel_of(2.0 / 11.0, second)


def split(values):
    high = np.asarray(values, np.float64).astype(ml_dtypes.bfloat16)
    low = (np.asarray(values, np.float64) - high.astype(np.float64)).astype(ml_dtypes.bfloat16)
    return high, low


def constants():
    (k1, r1, a1), (k2, r2, a2) = operators()
    n = CELLS
    d1 = np.array([[k1(i - j) for j in range(n)] for i in range(n)])
    d2 = np.array([[k2(i - j) for j in range(n)] for i in range(n)])
    rows = np.concatenate([d1.reshape(n // 8, 8, n), d2.reshape(n // 8, 8, n)], axis=1).reshape(2 * n, n)
    high, low = split(rows)
    along_x = np.concatenate([high, high, low], axis=1)
    high, low = split(np.concatenate([d1.T, d2.T], axis=1))
    i = np.arange(n)
    e1, e2 = k1(1) - a1 * r1, k2(1) - a2 * r2
    zero = np.zeros(n)
    first, last = (i == 0) * 1.0, (i == n - 1) * 1.0
    before = np.stack([
        np.concatenate([r1**i, zero]),
        np.concatenate([zero, r2**i]),
        np.concatenate([e1 * first, e2 * first]),
    ])
    after = np.stack([
        np.concatenate([-(r1 ** (n - 1 - i)), zero]),
        np.concatenate([zero, r2 ** (n - 1 - i)]),
        np.concatenate([-e1 * last, e2 * last]),
    ])
    spread = np.repeat(np.concatenate([before, after]), GROUP, axis=0)
    spread_high, spread_low = split(spread)
    blank = np.zeros((8, 2 * n), spread_high.dtype)
    along_y = np.concatenate([high, high, low], axis=0)
    spread_y = np.concatenate([spread_high, spread_high, spread_low, blank], axis=0)
    forward = np.stack([a1 * r1 ** (n - i.astype(float)), a2 * r2 ** (n - i.astype(float)), last, zero])
    backward = np.stack([a1 * r1 ** (1.0 + i), a2 * r2 ** (1.0 + i), first, zero])
    high, low = split(np.concatenate([forward, backward]))
    sums_y = np.concatenate(
        [np.concatenate([high, high], axis=1), np.concatenate([low, np.zeros_like(low)], axis=1)], axis=0
    )
    lanes = np.ones((1, n))
    edge_x = np.stack([
        forward[0, n - EDGE :, None] * lanes,
        forward[1, n - EDGE :, None] * lanes,
        backward[0, :EDGE, None] * lanes,
        backward[1, :EDGE, None] * lanes,
        (r1 ** i[:EDGE])[:, None] * lanes,
        (r2 ** i[:EDGE])[:, None] * lanes,
        (e1 * first)[:EDGE, None] * lanes,
        (e2 * first)[:EDGE, None] * lanes,
        (-(r1 ** (n - 1 - i)))[n - EDGE :, None] * lanes,
        (r2 ** (n - 1 - i))[n - EDGE :, None] * lanes,
        (-e1 * last)[n - EDGE :, None] * lanes,
        (e2 * last)[n - EDGE :, None] * lanes,
    ]).astype(np.float32)
    return along_x, along_y, spread_y, sums_y, edge_x


def dot(a, b):
    return lax.dot_general(a, b, (((1,), (0,)), ((), ())), preferred_element_type=jnp.float32)


def dot_transposed(a, b):
    return lax.dot_general(a, b, (((1,), (1,)), ((), ())), preferred_element_type=jnp.float32)


def first_kernel(
    groups, vel_hbm, leaf_hbm, table_hbm, along_x_hbm, along_y_hbm, spread_y_hbm, sums_y_hbm, edge_x_hbm,
    vel, tend, recv_x, recv_y, spread_y, edge_x,
    parts, leaf, send_x, send_y, along_x, along_y, sums_y, table_ref,
    vel_sem, leaf_sem, const_sem, send_sem, recv_sem, send_y_sem, recv_y_sem, last_sem, wrap_sem,
):
    n = CELLS
    half = 2 * GROUP
    halves = groups // 2

    consts = [
        pltpu.make_async_copy(a, b, const_sem.at[i])
        for i, (a, b) in enumerate(
            [(edge_x_hbm, edge_x), (sums_y_hbm, sums_y), (along_x_hbm, along_x), (along_y_hbm, along_y),
             (table_hbm, table_ref), (spread_y_hbm, spread_y)]
        )
    ]

    def levels(g):
        return pl.ds(g * GROUP, GROUP)

    def edge_copy(h, side):
        at = (slice(None), pl.ds(h * half, half), pl.ds(side * (n - EDGE), EDGE))
        return pltpu.make_async_copy(vel_hbm.at[at], vel.at[at], vel_sem.at[side, h])

    def middle_copy(g):
        at = (slice(None), levels(g), pl.ds(EDGE, n - 2 * EDGE))
        return pltpu.make_async_copy(vel_hbm.at[at], vel.at[at], vel_sem.at[2, g])

    def leaf_copy(g):
        return pltpu.make_async_copy(leaf_hbm.at[levels(g)], leaf.at[levels(g)], leaf_sem.at[g])

    mx, my = lax.axis_index("gx"), lax.axis_index("gy")
    nx, ny = lax.axis_size("gx"), lax.axis_size("gy")
    targets = [
        {"gx": lax.rem(mx + 1, nx)},
        {"gx": lax.rem(mx + nx - 1, nx)},
        {"gy": lax.rem(my + 1, ny)},
        {"gy": lax.rem(my + ny - 1, ny)},
    ]
    first, last = my == 0, my == ny - 1
    told = jnp.logical_or(mx == nx // 2, mx == nx // 2 - 1)
    untold = jnp.logical_not(told)
    deferred = jnp.logical_and(first, jnp.logical_not(told))
    barrier = pltpu.get_barrier_semaphore()
    apart = lax.rem(my, 4) == 2
    owed = jnp.logical_and(mx == 0, apart)
    for target in (targets[1], targets[3]):
        pl.semaphore_signal(barrier, inc=1, device_id=target, device_id_type=pl.DeviceIdType.MESH)

    @pl.when(jnp.logical_not(jnp.logical_and(mx == nx - 1, apart)))
    def _():
        pl.semaphore_signal(barrier, inc=1, device_id=targets[0], device_id_type=pl.DeviceIdType.MESH)

    @pl.when(jnp.logical_or(jnp.logical_not(last), told))
    def _():
        pl.semaphore_signal(barrier, inc=1, device_id=targets[2], device_id_type=pl.DeviceIdType.MESH)

    consts[0].start()
    for h in range(halves):
        for side in range(2):
            edge_copy(h, side).start()
    consts[1].start()
    for g in range(groups):
        middle_copy(g).start()
    consts[4].start()
    consts[2].start()
    for g in range(groups):
        leaf_copy(g).start()
    consts[3].start()
    consts[5].start()

    late_x = mx == nx - 1
    late_y = jnp.logical_and(last, mx != 0)
    late = jnp.logical_or(late_x, late_y)
    punctual = jnp.logical_not(late)
    slow = jnp.logical_or(jnp.logical_and(mx == 0, jnp.logical_not(jnp.logical_or(last, apart))), jnp.logical_and(first, told))
    sending_step = jnp.where(slow, groups, groups // 2)

    def x_copy(side):
        return pltpu.make_async_remote_copy(
            src_ref=send_x.at[side], dst_ref=recv_x.at[side],
            send_sem=send_sem.at[side], recv_sem=recv_sem.at[side],
            device_id=targets[side], device_id_type=pl.DeviceIdType.MESH,
        )

    def y_copy(side, g):
        return pltpu.make_async_remote_copy(
            src_ref=send_y.at[side, g], dst_ref=recv_y.at[side, g],
            send_sem=send_y_sem.at[side, g], recv_sem=recv_y_sem.at[side, g],
            device_id=targets[2 + side], device_id_type=pl.DeviceIdType.MESH,
        )

    def meet():
        @pl.when(jnp.logical_or(deferred, owed))
        def _():
            pl.semaphore_wait(barrier, 3)

        @pl.when(jnp.logical_not(jnp.logical_or(deferred, owed)))
        def _():
            pl.semaphore_wait(barrier, 4)

        @pl.when(jnp.logical_and(last, jnp.logical_not(told)))
        def _():
            pl.semaphore_signal(last_sem, inc=1, device_id=targets[2], device_id_type=pl.DeviceIdType.MESH)

        @pl.when(jnp.logical_and(mx == nx - 1, apart))
        def _():
            pl.semaphore_signal(wrap_sem, inc=1, device_id=targets[0], device_id_type=pl.DeviceIdType.MESH)

    def send_x_sums():
        @pl.when(mx == nx // 2)
        def _():
            x_copy(1).start()

        x_copy(0).start()

        @pl.when(jnp.logical_not(jnp.logical_or(mx == nx // 2, owed)))
        def _():
            x_copy(1).start()

    def send_y_back(g):
        @pl.when(jnp.logical_not(deferred))
        def _():
            y_copy(1, g).start()

    def send_rest():
        @pl.when(punctual)
        def _():
            meet()

        @pl.when(jnp.logical_not(jnp.logical_or(late_x, mx == 0)))
        def _():
            send_x_sums()

        @pl.when(late_x)
        def _():
            x_copy(1).start()

        for g in range(groups):
            @pl.when(jnp.logical_not(late_y))
            def _():
                y_copy(0, g).start()

            send_y_back(g)

        @pl.when(mx == 0)
        def _():
            send_x_sums()

    consts[0].wait()

    @pl.loop(0, halves)
    def _(h):
        edge_copy(h, 0).wait()
        edge_copy(h, 1).wait()
        for c in range(3):
            for k in range(half):
                top, bottom = vel[c, h * half + k, :EDGE], vel[c, h * half + k, n - EDGE :]
                for q in range(2):
                    row = (c * 3 + q) * half + k
                    send_x[0, h, row : row + 1] = jnp.sum(edge_x[q] * bottom, axis=0, keepdims=True)
                    send_x[1, h, row : row + 1] = jnp.sum(edge_x[2 + q] * top, axis=0, keepdims=True)
                row = (c * 3 + 2) * half + k
                send_x[0, h, row : row + 1] = bottom[EDGE - 1 :]
                send_x[1, h, row : row + 1] = top[:1]

    @pl.when(jnp.logical_or(late_x, jnp.logical_and(late_y, untold)))
    def _():
        meet()

    @pl.when(late_x)
    def _():
        x_copy(0).start()

    consts[1].wait()

    @pl.loop(0, groups)
    def _(g):
        middle_copy(g).wait()
        for c in range(3):
            for k in range(GROUP):
                values = vel[c, g * GROUP + k]
                high = values.astype(BF16)
                parts[c, g * GROUP + k, :, :n] = high
                parts[c, g * GROUP + k, :, n:] = (values - high.astype(jnp.float32)).astype(BF16)
            for k in range(0, GROUP, 2):
                pair = parts[c, pl.ds(g * GROUP + k, 2)].reshape(2 * n, 2 * n)
                sums = dot_transposed(sums_y[...], pair)
                sums = sums[:8] + sums[8:]
                for j in range(2):
                    for q in range(3):
                        row = (c * 3 + q) * GROUP + k + j
                        send_y[0, g, row : row + 1] = sums[q : q + 1, j * n : (j + 1) * n]
                        send_y[1, g, row : row + 1] = sums[4 + q : 5 + q, j * n : (j + 1) * n]
        for side in range(2):
            send_y[side, g, 9 * GROUP :] = jnp.zeros((4, n), jnp.float32)

        @pl.when(jnp.logical_and(late_y, jnp.logical_or(late_x, untold)))
        def _():
            y_copy(0, g).start()

    @pl.when(jnp.logical_and(jnp.logical_and(late_y, told), jnp.logical_not(late_x)))
    def _():
        meet()
        for g in range(groups):
            y_copy(0, g).start()

    lane = lax.broadcasted_iota(jnp.int32, (n, n), 1)
    consts[4].wait()
    table = jnp.zeros((n, n), jnp.float32)
    for k in range(table_ref.shape[0]):
        table = jnp.where(lane == k, table_ref[k], table)
    consts[2].wait()

    @pl.loop(0, groups)
    def _(g):
        @pl.when(g == sending_step)
        def _():
            send_rest()

        leaf_copy(g).wait()
        for k in range(0, GROUP, 2):
            z = (g * GROUP + k, g * GROUP + k + 1)
            drag = []
            for j in range(2):
                speed = jnp.sqrt(vel[0, z[j]] ** 2 + vel[1, z[j]] ** 2 + vel[2, z[j]] ** 2)
                drag.append(jnp.take_along_axis(table, leaf[z[j]], axis=1) * speed)
            for c in range(3):
                high = jnp.concatenate([parts[c, z[0], :, :n], parts[c, z[1], :, :n]], axis=1)
                low = jnp.concatenate([parts[c, z[0], :, n:], parts[c, z[1], :, n:]], axis=1)
                both = dot(along_x[...], jnp.concatenate([high, low, high], axis=0))
                both = both.reshape(n // 8, 2, 8, 2 * n)
                for j in range(2):
                    gradient = both[:, 0, :, j * n : (j + 1) * n].reshape(n, n)
                    curvature = both[:, 1, :, j * n : (j + 1) * n].reshape(n, n)
                    tend[c, z[j]] = curvature - vel[0, z[j]] * gradient - drag[j] * vel[c, z[j]]

    @pl.when(sending_step == groups)
    def _():
        send_rest()

    consts[3].wait()

    @pl.loop(0, groups)
    def _(g):
        for k in range(GROUP):
            z = g * GROUP + k
            left = [jnp.concatenate([parts[c, z], parts[c, z, :, :n]], axis=1) for c in range(3)]
            both = dot(jnp.concatenate(left, axis=0), along_y[...])
            for c in range(3):
                gradient = both[c * n : (c + 1) * n, :n]
                curvature = both[c * n : (c + 1) * n, n:]
                tend[c, z] += curvature - vel[1, z] * gradient

    consts[5].wait()

    @pl.when(owed)
    def _():
        pl.semaphore_wait(wrap_sem, 1)
        x_copy(1).start()

    @pl.when(deferred)
    def _():
        pl.semaphore_wait(last_sem, 1)
        for g in range(groups):
            y_copy(1, g).start()

    for side in range(2):
        for g in range(groups):
            y_copy(side, g).wait_recv()
    for side in range(2):
        x_copy(side).wait_recv()
    for side in range(2):
        x_copy(side).wait_send()
        for g in range(groups):
            y_copy(side, g).wait_send()


def second_kernel(groups, vel, tend, recv_x, recv_y, spread_y, edge_x, out_hbm, result, out_sem):
    n = CELLS
    half = 2 * GROUP
    values = 3 * GROUP

    def out_copy(z):
        return pltpu.make_async_copy(result.at[:, z], out_hbm.at[:, z], out_sem.at[z])

    lane = lax.broadcasted_iota(jnp.int32, (n, 80), 1)
    for g in range(groups):
        spread = []
        for c in range(3):
            got = jnp.concatenate([recv_y[side, g, c * values : (c + 1) * values] for side in range(2)], axis=0)
            high = got.astype(BF16).astype(jnp.float32)
            low = (got - high).astype(BF16).astype(jnp.float32)
            blank = jnp.zeros((8, n), jnp.float32)
            spread.append(jnp.concatenate([high, low, high, blank], axis=0).T.astype(BF16))
        for k in range(GROUP):
            z = g * GROUP + k
            mask = (lane % GROUP) == k
            left = [jnp.where(mask, s, jnp.zeros_like(s)) for s in spread]
            for c in range(3):
                both = dot(left[c], spread_y[...])
                gradient = both[:, :n]
                curvature = both[:, n:]
                values_z = tend[c, z] + curvature - vel[1, z] * gradient
                ends = []
                for side in range(2):
                    h, at = g // 2, c * 3 * half + (g % 2) * GROUP + k
                    s1, s2, s3 = (recv_x[side, h, at + q * half : at + q * half + 1] for q in range(3))
                    gradient = edge_x[4 + 4 * side] * s1 + edge_x[6 + 4 * side] * s3
                    curvature = edge_x[5 + 4 * side] * s2 + edge_x[7 + 4 * side] * s3
                    rows = slice(side * (n - EDGE), side * (n - EDGE) + EDGE)
                    ends.append(values_z[rows] + curvature - vel[0, z, rows] * gradient)
                result[c, z] = jnp.concatenate([ends[0], values_z[EDGE : n - EDGE], ends[1]], axis=0)
            out_copy(z).start()
    for z in range(groups * GROUP):
        out_copy(z).wait()


def in_hbm(array):
    return pltpu.with_memory_space_constraint(array, pltpu.HBM)


def body(velocity, leaf_class, drag_table):
    along_x, along_y, spread_y, sums_y, edge_x = (in_hbm(jnp.asarray(a)) for a in constants())
    velocity, leaf_class, drag_table = in_hbm(velocity), in_hbm(leaf_class), in_hbm(drag_table)
    levels, n = velocity.shape[1], CELLS
    groups = levels // GROUP
    hbm = pl.BlockSpec(memory_space=pltpu.HBM)
    vmem = pl.BlockSpec(memory_space=pltpu.VMEM)
    dma = pltpu.SemaphoreType.DMA
    sums_along_x = (2, groups // 2, 18 * GROUP, n)
    sums_along_y = (2, groups, 10 * GROUP, n)
    held = [
        jax.ShapeDtypeStruct(velocity.shape, jnp.float32),
        jax.ShapeDtypeStruct(velocity.shape, jnp.float32),
        jax.ShapeDtypeStruct(sums_along_x, jnp.float32),
        jax.ShapeDtypeStruct(sums_along_y, jnp.float32),
        jax.ShapeDtypeStruct(spread_y.shape, BF16),
        jax.ShapeDtypeStruct(edge_x.shape, jnp.float32),
    ]
    held = pl.pallas_call(
        functools.partial(first_kernel, groups),
        out_shape=held,
        in_specs=[hbm] * 8,
        out_specs=[vmem] * 6,
        scratch_shapes=[
            pltpu.VMEM((3, levels, n, 2 * n), BF16),
            pltpu.VMEM(leaf_class.shape, jnp.int32),
            pltpu.VMEM(sums_along_x, jnp.float32),
            pltpu.VMEM(sums_along_y, jnp.float32),
            pltpu.VMEM(along_x.shape, BF16),
            pltpu.VMEM(along_y.shape, BF16),
            pltpu.VMEM(sums_y.shape, BF16),
            pltpu.SMEM(drag_table.shape, jnp.float32),
            dma((3, groups)), dma((groups,)), dma((6,)), dma((2,)), dma((2,)), dma((2, groups)), dma((2, groups)),
            pltpu.SemaphoreType.REGULAR, pltpu.SemaphoreType.REGULAR,
        ],
        compiler_params=pltpu.CompilerParams(
            collective_id=0, has_side_effects=True, vmem_limit_bytes=40 * 1024 * 1024
        ),
        cost_estimate=pl.CostEstimate(flops=4_000_000_000, bytes_accessed=5_000_000, transcendentals=300_000),
        name="exchange_and_solve",
    )(velocity, leaf_class, drag_table, along_x, along_y, spread_y, sums_y, edge_x)
    return pl.pallas_call(
        functools.partial(second_kernel, groups),
        out_shape=jax.ShapeDtypeStruct(velocity.shape, jnp.float32),
        in_specs=[vmem] * 6,
        out_specs=hbm,
        scratch_shapes=[pltpu.VMEM(velocity.shape, jnp.float32), dma((levels,))],
        compiler_params=pltpu.CompilerParams(vmem_limit_bytes=40 * 1024 * 1024),
        cost_estimate=pl.CostEstimate(flops=1_000_000_000, bytes_accessed=3_000_000, transcendentals=0),
        name="finish",
    )(*held)


def solution(mesh):
    return jax.shard_map(
        body,
        mesh=mesh,
        in_specs=(P(None, None, "gx", "gy"), P(None, "gx", "gy"), P()),
        out_specs=P(None, None, "gx", "gy"),
        check_vma=False,
    )
```

```python
import functools
import math

import jax
import jax.numpy as jnp
import ml_dtypes
import numpy as np
from jax import lax
from jax.experimental import pallas as pl
from jax.experimental.pallas import tpu as pltpu
from jax.sharding import PartitionSpec as P

SPACING = 2.0
CELLS = 128
GROUP = 4
EDGE = 24
BF16 = jnp.bfloat16


def kernel_of(coupling, stencil):
    root = (-1.0 + math.sqrt(1.0 - 4.0 * coupling * coupling)) / (2.0 * coupling)
    scale = 1.0 / math.sqrt(1.0 - 4.0 * coupling * coupling)

    def at(d):
        return sum(w * scale * root ** abs(d - m) for m, w in stencil.items())

    amplitude = at(2) / root**2
    return at, root, amplitude


def operators():
    h = SPACING
    a, b = 14.0 / 9.0 / (2.0 * h), 1.0 / 9.0 / (4.0 * h)
    first = {-1: a, 1: -a, -2: b, 2: -b}
    c, e = 12.0 / 11.0 / (h * h), 3.0 / 11.0 / (4.0 * h * h)
    second = {-1: c, 1: c, -2: e, 2: e, 0: -2.0 * c - 2.0 * e}
    return kernel_of(1.0 / 3.0, first), kernel_of(2.0 / 11.0, second)


def split(values):
    high = np.asarray(values, np.float64).astype(ml_dtypes.bfloat16)
    low = (np.asarray(values, np.float64) - high.astype(np.float64)).astype(ml_dtypes.bfloat16)
    return high, low


def constants():
    (k1, r1, a1), (k2, r2, a2) = operators()
    n = CELLS
    d1 = np.array([[k1(i - j) for j in range(n)] for i in range(n)])
    d2 = np.array([[k2(i - j) for j in range(n)] for i in range(n)])
    rows = np.concatenate([d1.reshape(n // 8, 8, n), d2.reshape(n // 8, 8, n)], axis=1).reshape(2 * n, n)
    high, low = split(rows)
    along_x = np.concatenate([high, high, low], axis=1)
    high, low = split(np.concatenate([d1.T, d2.T], axis=1))
    i = np.arange(n)
    e1, e2 = k1(1) - a1 * r1, k2(1) - a2 * r2
    zero = np.zeros(n)
    first, last = (i == 0) * 1.0, (i == n - 1) * 1.0
    before = np.stack([
        np.concatenate([r1**i, zero]),
        np.concatenate([zero, r2**i]),
        np.concatenate([e1 * first, e2 * first]),
    ])
    after = np.stack([
        np.concatenate([-(r1 ** (n - 1 - i)), zero]),
        np.concatenate([zero, r2 ** (n - 1 - i)]),
        np.concatenate([-e1 * last, e2 * last]),
    ])
    spread = np.repeat(np.concatenate([before, after]), GROUP, axis=0)
    spread_high, spread_low = split(spread)
    blank = np.zeros((8, 2 * n), spread_high.dtype)
    along_y = np.concatenate([high, high, low], axis=0)
    spread_y = np.concatenate([spread_high, spread_high, spread_low, blank], axis=0)
    forward = np.stack([a1 * r1 ** (n - i.astype(float)), a2 * r2 ** (n - i.astype(float)), last, zero])
    backward = np.stack([a1 * r1 ** (1.0 + i), a2 * r2 ** (1.0 + i), first, zero])
    high, low = split(np.concatenate([forward, backward]))
    sums_y = np.concatenate(
        [np.concatenate([high, high], axis=1), np.concatenate([low, np.zeros_like(low)], axis=1)], axis=0
    )
    lanes = np.ones((1, n))
    edge_x = np.stack([
        forward[0, n - EDGE :, None] * lanes,
        forward[1, n - EDGE :, None] * lanes,
        backward[0, :EDGE, None] * lanes,
        backward[1, :EDGE, None] * lanes,
        (r1 ** i[:EDGE])[:, None] * lanes,
        (r2 ** i[:EDGE])[:, None] * lanes,
        (e1 * first)[:EDGE, None] * lanes,
        (e2 * first)[:EDGE, None] * lanes,
        (-(r1 ** (n - 1 - i)))[n - EDGE :, None] * lanes,
        (r2 ** (n - 1 - i))[n - EDGE :, None] * lanes,
        (-e1 * last)[n - EDGE :, None] * lanes,
        (e2 * last)[n - EDGE :, None] * lanes,
    ]).astype(np.float32)
    return along_x, along_y, spread_y, sums_y, edge_x


def dot(a, b):
    return lax.dot_general(a, b, (((1,), (0,)), ((), ())), preferred_element_type=jnp.float32)


def dot_transposed(a, b):
    return lax.dot_general(a, b, (((1,), (1,)), ((), ())), preferred_element_type=jnp.float32)


def first_kernel(
    groups, vel_hbm, leaf_hbm, table_hbm, along_x_hbm, along_y_hbm, spread_y_hbm, sums_y_hbm, edge_x_hbm,
    vel, tend, recv_x, recv_y, spread_y, edge_x,
    parts, leaf, send_x, send_y, along_x, along_y, sums_y, table_ref,
    vel_sem, leaf_sem, const_sem, send_sem, recv_sem, send_y_sem, recv_y_sem, last_sem, wrap_sem,
):
    n = CELLS
    half = 2 * GROUP
    halves = groups // 2

    consts = [
        pltpu.make_async_copy(a, b, const_sem.at[i])
        for i, (a, b) in enumerate(
            [(edge_x_hbm, edge_x), (sums_y_hbm, sums_y), (along_x_hbm, along_x), (along_y_hbm, along_y),
             (table_hbm, table_ref), (spread_y_hbm, spread_y)]
        )
    ]

    def levels(g):
        return pl.ds(g * GROUP, GROUP)

    def edge_copy(h, side):
        at = (slice(None), pl.ds(h * half, half), pl.ds(side * (n - EDGE), EDGE))
        return pltpu.make_async_copy(vel_hbm.at[at], vel.at[at], vel_sem.at[side, h])

    def middle_copy(g):
        at = (slice(None), levels(g), pl.ds(EDGE, n - 2 * EDGE))
        return pltpu.make_async_copy(vel_hbm.at[at], vel.at[at], vel_sem.at[2, g])

    def leaf_copy(g):
        return pltpu.make_async_copy(leaf_hbm.at[levels(g)], leaf.at[levels(g)], leaf_sem.at[g])

    mx, my = lax.axis_index("gx"), lax.axis_index("gy")
    nx, ny = lax.axis_size("gx"), lax.axis_size("gy")
    targets = [
        {"gx": lax.rem(mx + 1, nx)},
        {"gx": lax.rem(mx + nx - 1, nx)},
        {"gy": lax.rem(my + 1, ny)},
        {"gy": lax.rem(my + ny - 1, ny)},
    ]
    first, last = my == 0, my == ny - 1
    told = jnp.logical_or(mx == nx // 2, mx == nx // 2 - 1)
    untold = jnp.logical_not(told)
    deferred = jnp.logical_and(first, jnp.logical_not(told))
    barrier = pltpu.get_barrier_semaphore()
    apart = lax.rem(my, 4) == 2
    owed = jnp.logical_and(mx == 0, apart)
    for target in (targets[1], targets[3]):
        pl.semaphore_signal(barrier, inc=1, device_id=target, device_id_type=pl.DeviceIdType.MESH)

    @pl.when(jnp.logical_not(jnp.logical_and(mx == nx - 1, apart)))
    def _():
        pl.semaphore_signal(barrier, inc=1, device_id=targets[0], device_id_type=pl.DeviceIdType.MESH)

    @pl.when(jnp.logical_or(jnp.logical_not(last), told))
    def _():
        pl.semaphore_signal(barrier, inc=1, device_id=targets[2], device_id_type=pl.DeviceIdType.MESH)

    consts[0].start()
    for h in range(halves):
        for side in range(2):
            edge_copy(h, side).start()
    consts[1].start()
    for g in range(groups):
        middle_copy(g).start()
    consts[4].start()
    consts[2].start()
    for g in range(groups):
        leaf_copy(g).start()
    consts[3].start()
    consts[5].start()

    late_x = mx == nx - 1
    late_y = jnp.logical_and(last, mx != 0)
    late = jnp.logical_or(late_x, late_y)
    punctual = jnp.logical_not(late)
    slow = jnp.logical_or(jnp.logical_and(mx == 0, jnp.logical_not(jnp.logical_or(last, apart))), jnp.logical_and(first, told))
    sending_step = jnp.where(slow, groups, groups // 2)

    def x_part(side, h):
        return pltpu.make_async_remote_copy(
            src_ref=send_x.at[side, h], dst_ref=recv_x.at[side, h],
            send_sem=send_sem.at[side, h], recv_sem=recv_sem.at[side, h],
            device_id=targets[side], device_id_type=pl.DeviceIdType.MESH,
        )

    def start_x(side):
        for h in range(halves):
            x_part(side, h).start()

    def y_copy(side, g):
        return pltpu.make_async_remote_copy(
            src_ref=send_y.at[side, g], dst_ref=recv_y.at[side, g],
            send_sem=send_y_sem.at[side, g], recv_sem=recv_y_sem.at[side, g],
            device_id=targets[2 + side], device_id_type=pl.DeviceIdType.MESH,
        )

    def meet():
        @pl.when(jnp.logical_or(deferred, owed))
        def _():
            pl.semaphore_wait(barrier, 3)

        @pl.when(jnp.logical_not(jnp.logical_or(deferred, owed)))
        def _():
            pl.semaphore_wait(barrier, 4)

        @pl.when(jnp.logical_and(last, jnp.logical_not(told)))
        def _():
            pl.semaphore_signal(last_sem, inc=1, device_id=targets[2], device_id_type=pl.DeviceIdType.MESH)

        @pl.when(jnp.logical_and(mx == nx - 1, apart))
        def _():
            pl.semaphore_signal(wrap_sem, inc=1, device_id=targets[0], device_id_type=pl.DeviceIdType.MESH)

    def send_x_sums():
        @pl.when(mx == nx // 2)
        def _():
            start_x(1)

        start_x(0)

        @pl.when(jnp.logical_not(jnp.logical_or(mx == nx // 2, owed)))
        def _():
            start_x(1)

    def send_y_back(g):
        @pl.when(jnp.logical_not(deferred))
        def _():
            y_copy(1, g).start()

    def send_rest():
        @pl.when(punctual)
        def _():
            meet()

        @pl.when(jnp.logical_not(jnp.logical_or(late_x, mx == 0)))
        def _():
            send_x_sums()

        @pl.when(late_x)
        def _():
            start_x(1)

        for g in range(groups):
            @pl.when(jnp.logical_not(late_y))
            def _():
                y_copy(0, g).start()

            send_y_back(g)

        @pl.when(mx == 0)
        def _():
            send_x_sums()

    consts[0].wait()

    @pl.loop(0, halves)
    def _(h):
        edge_copy(h, 0).wait()
        edge_copy(h, 1).wait()
        for c in range(3):
            for k in range(half):
                top, bottom = vel[c, h * half + k, :EDGE], vel[c, h * half + k, n - EDGE :]
                for q in range(2):
                    row = (c * 3 + q) * half + k
                    send_x[0, h, row : row + 1] = jnp.sum(edge_x[q] * bottom, axis=0, keepdims=True)
                    send_x[1, h, row : row + 1] = jnp.sum(edge_x[2 + q] * top, axis=0, keepdims=True)
                row = (c * 3 + 2) * half + k
                send_x[0, h, row : row + 1] = bottom[EDGE - 1 :]
                send_x[1, h, row : row + 1] = top[:1]

    @pl.when(jnp.logical_or(late_x, jnp.logical_and(late_y, untold)))
    def _():
        meet()

    @pl.when(late_x)
    def _():
        start_x(0)

    consts[1].wait()

    @pl.loop(0, groups)
    def _(g):
        middle_copy(g).wait()
        for c in range(3):
            for k in range(GROUP):
                values = vel[c, g * GROUP + k]
                high = values.astype(BF16)
                parts[c, g * GROUP + k, :, :n] = high
                parts[c, g * GROUP + k, :, n:] = (values - high.astype(jnp.float32)).astype(BF16)
            for k in range(0, GROUP, 2):
                pair = parts[c, pl.ds(g * GROUP + k, 2)].reshape(2 * n, 2 * n)
                sums = dot_transposed(sums_y[...], pair)
                sums = sums[:8] + sums[8:]
                for j in range(2):
                    for q in range(3):
                        row = (c * 3 + q) * GROUP + k + j
                        send_y[0, g, row : row + 1] = sums[q : q + 1, j * n : (j + 1) * n]
                        send_y[1, g, row : row + 1] = sums[4 + q : 5 + q, j * n : (j + 1) * n]
        for side in range(2):
            send_y[side, g, 9 * GROUP :] = jnp.zeros((4, n), jnp.float32)

        @pl.when(jnp.logical_and(late_y, jnp.logical_or(late_x, untold)))
        def _():
            y_copy(0, g).start()

    @pl.when(jnp.logical_and(jnp.logical_and(late_y, told), jnp.logical_not(late_x)))
    def _():
        meet()
        for g in range(groups):
            y_copy(0, g).start()

    lane = lax.broadcasted_iota(jnp.int32, (n, n), 1)
    consts[4].wait()
    table = jnp.zeros((n, n), jnp.float32)
    for k in range(table_ref.shape[0]):
        table = jnp.where(lane == k, table_ref[k], table)
    consts[2].wait()

    @pl.loop(0, groups)
    def _(g):
        @pl.when(g == sending_step)
        def _():
            send_rest()

        leaf_copy(g).wait()
        for k in range(0, GROUP, 2):
            z = (g * GROUP + k, g * GROUP + k + 1)
            drag = []
            for j in range(2):
                speed = jnp.sqrt(vel[0, z[j]] ** 2 + vel[1, z[j]] ** 2 + vel[2, z[j]] ** 2)
                drag.append(jnp.take_along_axis(table, leaf[z[j]], axis=1) * speed)
            for c in range(3):
                high = jnp.concatenate([parts[c, z[0], :, :n], parts[c, z[1], :, :n]], axis=1)
                low = jnp.concatenate([parts[c, z[0], :, n:], parts[c, z[1], :, n:]], axis=1)
                both = dot(along_x[...], jnp.concatenate([high, low, high], axis=0))
                both = both.reshape(n // 8, 2, 8, 2 * n)
                for j in range(2):
                    gradient = both[:, 0, :, j * n : (j + 1) * n].reshape(n, n)
                    curvature = both[:, 1, :, j * n : (j + 1) * n].reshape(n, n)
                    tend[c, z[j]] = curvature - vel[0, z[j]] * gradient - drag[j] * vel[c, z[j]]

    @pl.when(sending_step == groups)
    def _():
        send_rest()

    consts[3].wait()

    @pl.loop(0, groups)
    def _(g):
        for k in range(GROUP):
            z = g * GROUP + k
            left = [jnp.concatenate([parts[c, z], parts[c, z, :, :n]], axis=1) for c in range(3)]
            both = dot(jnp.concatenate(left, axis=0), along_y[...])
            for c in range(3):
                gradient = both[c * n : (c + 1) * n, :n]
                curvature = both[c * n : (c + 1) * n, n:]
                tend[c, z] += curvature - vel[1, z] * gradient

    consts[5].wait()

    @pl.when(owed)
    def _():
        pl.semaphore_wait(wrap_sem, 1)
        start_x(1)

    @pl.when(deferred)
    def _():
        pl.semaphore_wait(last_sem, 1)
        for g in range(groups):
            y_copy(1, g).start()

    for side in range(2):
        for g in range(groups):
            y_copy(side, g).wait_recv()
    for side in range(2):
        for h in range(halves):
            x_part(side, h).wait_recv()
    for side in range(2):
        for h in range(halves):
            x_part(side, h).wait_send()
        for g in range(groups):
            y_copy(side, g).wait_send()


def second_kernel(groups, vel, tend, recv_x, recv_y, spread_y, edge_x, out_hbm, result, out_sem):
    n = CELLS
    half = 2 * GROUP
    values = 3 * GROUP

    def out_copy(z):
        return pltpu.make_async_copy(result.at[:, z], out_hbm.at[:, z], out_sem.at[z])

    lane = lax.broadcasted_iota(jnp.int32, (n, 80), 1)
    for g in range(groups):
        spread = []
        for c in range(3):
            got = jnp.concatenate([recv_y[side, g, c * values : (c + 1) * values] for side in range(2)], axis=0)
            high = got.astype(BF16).astype(jnp.float32)
            low = (got - high).astype(BF16).astype(jnp.float32)
            blank = jnp.zeros((8, n), jnp.float32)
            spread.append(jnp.concatenate([high, low, high, blank], axis=0).T.astype(BF16))
        for k in range(GROUP):
            z = g * GROUP + k
            mask = (lane % GROUP) == k
            left = [jnp.where(mask, s, jnp.zeros_like(s)) for s in spread]
            for c in range(3):
                both = dot(left[c], spread_y[...])
                gradient = both[:, :n]
                curvature = both[:, n:]
                values_z = tend[c, z] + curvature - vel[1, z] * gradient
                ends = []
                for side in range(2):
                    h, at = g // 2, c * 3 * half + (g % 2) * GROUP + k
                    s1, s2, s3 = (recv_x[side, h, at + q * half : at + q * half + 1] for q in range(3))
                    gradient = edge_x[4 + 4 * side] * s1 + edge_x[6 + 4 * side] * s3
                    curvature = edge_x[5 + 4 * side] * s2 + edge_x[7 + 4 * side] * s3
                    rows = slice(side * (n - EDGE), side * (n - EDGE) + EDGE)
                    ends.append(values_z[rows] + curvature - vel[0, z, rows] * gradient)
                result[c, z] = jnp.concatenate([ends[0], values_z[EDGE : n - EDGE], ends[1]], axis=0)
            out_copy(z).start()
    for z in range(groups * GROUP):
        out_copy(z).wait()


def in_hbm(array):
    return pltpu.with_memory_space_constraint(array, pltpu.HBM)


def body(velocity, leaf_class, drag_table):
    along_x, along_y, spread_y, sums_y, edge_x = (in_hbm(jnp.asarray(a)) for a in constants())
    velocity, leaf_class, drag_table = in_hbm(velocity), in_hbm(leaf_class), in_hbm(drag_table)
    levels, n = velocity.shape[1], CELLS
    groups = levels // GROUP
    hbm = pl.BlockSpec(memory_space=pltpu.HBM)
    vmem = pl.BlockSpec(memory_space=pltpu.VMEM)
    dma = pltpu.SemaphoreType.DMA
    sums_along_x = (2, groups // 2, 18 * GROUP, n)
    sums_along_y = (2, groups, 10 * GROUP, n)
    held = [
        jax.ShapeDtypeStruct(velocity.shape, jnp.float32),
        jax.ShapeDtypeStruct(velocity.shape, jnp.float32),
        jax.ShapeDtypeStruct(sums_along_x, jnp.float32),
        jax.ShapeDtypeStruct(sums_along_y, jnp.float32),
        jax.ShapeDtypeStruct(spread_y.shape, BF16),
        jax.ShapeDtypeStruct(edge_x.shape, jnp.float32),
    ]
    held = pl.pallas_call(
        functools.partial(first_kernel, groups),
        out_shape=held,
        in_specs=[hbm] * 8,
        out_specs=[vmem] * 6,
        scratch_shapes=[
            pltpu.VMEM((3, levels, n, 2 * n), BF16),
            pltpu.VMEM(leaf_class.shape, jnp.int32),
            pltpu.VMEM(sums_along_x, jnp.float32),
            pltpu.VMEM(sums_along_y, jnp.float32),
            pltpu.VMEM(along_x.shape, BF16),
            pltpu.VMEM(along_y.shape, BF16),
            pltpu.VMEM(sums_y.shape, BF16),
            pltpu.SMEM(drag_table.shape, jnp.float32),
            dma((3, groups)), dma((groups,)), dma((6,)), dma((2, groups // 2)), dma((2, groups // 2)), dma((2, groups)), dma((2, groups)),
            pltpu.SemaphoreType.REGULAR, pltpu.SemaphoreType.REGULAR,
        ],
        compiler_params=pltpu.CompilerParams(
            collective_id=0, has_side_effects=True, vmem_limit_bytes=40 * 1024 * 1024
        ),
        cost_estimate=pl.CostEstimate(flops=4_000_000_000, bytes_accessed=5_000_000, transcendentals=300_000),
        name="exchange_and_solve",
    )(velocity, leaf_class, drag_table, along_x, along_y, spread_y, sums_y, edge_x)
    return pl.pallas_call(
        functools.partial(second_kernel, groups),
        out_shape=jax.ShapeDtypeStruct(velocity.shape, jnp.float32),
        in_specs=[vmem] * 6,
        out_specs=hbm,
        scratch_shapes=[pltpu.VMEM(velocity.shape, jnp.float32), dma((levels,))],
        compiler_params=pltpu.CompilerParams(vmem_limit_bytes=40 * 1024 * 1024),
        cost_estimate=pl.CostEstimate(flops=1_000_000_000, bytes_accessed=3_000_000, transcendentals=0),
        name="finish",
    )(*held)


def solution(mesh):
    return jax.shard_map(
        body,
        mesh=mesh,
        in_specs=(P(None, None, "gx", "gy"), P(None, "gx", "gy"), P()),
        out_specs=P(None, None, "gx", "gy"),
        check_vma=False,
    )
```
